32 devices in a mesh: section: 2 (over x), tensor: 4 (over y, core), dp: 4 (over z).
Axes of the slice: x: 2, y: 2, z: 4, core: 2. Of those that a mesh axis runs over, the one named last changes fastest.
Arguments:
- ends_in: bfloat16 [2, 14336, 768], P('section', 'dp', 'tensor'), may hold values from -6 to 6
- ln_gain: bfloat16 [2, 2, 768], P('section', None, 'tensor'), may hold values from 0.5 to 1.5
- ln_shift: bfloat16 [2, 2, 768], P('section', None, 'tensor'), may hold values from -1.796875 to 1.796875
- w_qkv: bfloat16 [2, 768, 3, 768], P('section', None, None, 'tensor'), may hold values from -0.21875 to 0.21875
- b_qv: bfloat16 [2, 2, 768], P('section', None, 'tensor'), may hold values from -1.1953125 to 1.1953125
- w_out: bfloat16 [2, 768, 768], P('section', 'tensor'), may hold values from -1.75 to 1.75
- b_out: bfloat16 [2, 768], P('section', 'tensor'), may hold values from -1.796875 to 1.796875
- w_fc1: bfloat16 [2, 768, 3072], P('section', None, 'tensor'), may hold values from -0.21875 to 0.21875
- b_fc1: bfloat16 [2, 3072], P('section', 'tensor'), may hold values from -1.796875 to 1.796875
- w_fc2: bfloat16 [2, 3072, 768], P('section', 'tensor'), may hold values from -0.109375 to 0.109375
- b_fc2: bfloat16 [2, 768], P('section', 'tensor'), may hold values from -1.796875 to 1.796875
Outputs:
- ends_out: float32 [2, 14336, 768], P('section', 'dp', 'tensor')
- grad_ln_gain: float32 [2, 2, 768], P('section', None, 'tensor')
- grad_ln_shift: float32 [2, 2, 768], P('section', None, 'tensor')
- grad_w_qkv: float32 [2, 768, 3, 768], P('section', None, None, 'tensor')
- grad_b_qv: float32 [2, 2, 768], P('section', None, 'tensor')
- grad_w_out: float32 [2, 768, 768], P('section', 'tensor')
- grad_b_out: float32 [2, 768], P('section', 'tensor')
- grad_w_fc1: float32 [2, 768, 3072], P('section', None, 'tensor')
- grad_b_fc1: float32 [2, 3072], P('section', 'tensor')
- grad_w_fc2: float32 [2, 3072, 768], P('section', 'tensor')
- grad_b_fc2: float32 [2, 768], P('section', 'tensor')
The draws below stay inside these ranges and needn't reach their ends.
All inputs are finite; a program needn't handle non-finite values.
Results may differ from the reference program's by a relative error of at most 0.015.
Values may be sent and summed in bfloat16 or wider, within the bound.
No kernel may reach another device: no remote copies, remote signals or barrier semaphores. Data moves between devices by JAX's collectives and lax.ppermute only.
A program may use at most 256 MiB of HBM per device.

```python
import jax
import jax.numpy as jnp
from jax import lax

D = 768
HEADS = 12
HD = 64
FF = 3072
FRAMES = 448
MICRO = 2
ROWS_MB = 1792
TOKENS = 14336
N_DP = 4


def steps_of(own_key, shape, pieces, smallest, largest):
    factor_of, own = 1.0, jax.random.fold_in(own_key, 6)
    for axis_at, blocks in pieces:
        steps = jnp.exp(jax.random.uniform(jax.random.fold_in(own, axis_at), (blocks,), jnp.float32, smallest / len(pieces), largest / len(pieces)))
        factor_of = factor_of * jnp.repeat(steps, shape[axis_at] // blocks).reshape([-1 if axis == axis_at else 1 for axis in range(len(shape))])
    return factor_of


def gaussian(rng, dims, scale, reach, cuts=(), held_as=jnp.bfloat16):
    level = steps_of(rng, dims, cuts, -0.22, 0.18) if cuts else 1.0
    array = jax.random.normal(rng, dims, jnp.float32) * scale * level
    return jnp.minimum(jnp.maximum(array, -reach), reach).astype(held_as)


def setup_inputs(seed: int = 0) -> dict:
    seeds = jax.random.split(jax.random.key(seed), 12)
    return {
        "ends_in": gaussian(seeds[0], (2, TOKENS, D), 1.0, 6.0, ((0, 2), (1, 4), (2, 4))),
        "ln_gain": jnp.clip(1.0 + 0.1 * jax.random.normal(seeds[1], (2, 2, D), jnp.float32), 0.5, 1.5).astype(jnp.bfloat16),
        "ln_shift": gaussian(seeds[2], (2, 2, D), 0.3, 1.796875, ((0, 2), (2, 4))),
        "w_qkv": gaussian(seeds[3], (2, D, 3, D), D ** -0.5, 0.21875, ((0, 2), (3, 4))),
        "b_qv": gaussian(seeds[4], (2, 2, D), 0.2, 1.1953125, ((0, 2), (2, 4))),
        "w_out": gaussian(seeds[5], (2, D, D), (D // 64) ** -0.5, 1.75, ((0, 2), (1, 4))),
        "b_out": gaussian(seeds[6], (2, D), 0.3, 1.796875, ((0, 2), (1, 4))),
        "w_fc1": gaussian(seeds[7], (2, D, FF), D ** -0.5, 0.21875, ((0, 2), (2, 4))),
        "b_fc1": gaussian(seeds[8], (2, FF), 0.3, 1.796875, ((0, 2), (1, 4))),
        "w_fc2": gaussian(seeds[9], (2, FF, D), FF ** -0.5, 0.109375, ((0, 2), (1, 4))),
        "b_fc2": gaussian(seeds[10], (2, D), 0.3, 1.796875, ((0, 2), (1, 4))),
    }


@jax.custom_vjp
def low(v):
    return lax.optimization_barrier(v.astype(jnp.bfloat16)).astype(jnp.float32)

@jax.custom_vjp
def low_back(v):
    return v

def low_keep(v):
    return (low(v), None)

def low_pass(kept, grad):
    return (grad,)

def back_keep(v):
    return (v, None)

def back_low(kept, grad):
    return (low(grad),)
low.defvjp(low_keep, low_pass)
low_back.defvjp(back_keep, back_low)
EPSILON = 1e-05
HIGHEST = lax.Precision.HIGHEST

def normalize(stream, norm_gain, norm_shift):
    center = lax.optimization_barrier(jnp.mean(stream, axis=-1, keepdims=True))
    spread = lax.optimization_barrier(jnp.mean(jnp.square(stream - center), axis=-1, keepdims=True))
    return (stream - center) * lax.rsqrt(spread + EPSILON) * norm_gain + norm_shift

def to_heads(flat_rows):
    return flat_rows.reshape(flat_rows.shape[0] // FRAMES, FRAMES, HEADS, HD)

def encoder_layer(stream, layer_weights):
    norm_gain, norm_shift, w_qkv, b_qv, w_out, b_out, w_fc1, b_fc1, w_fc2, b_fc2 = layer_weights
    row_count = stream.shape[0]
    score_scale = float(HD) ** (-0.5)
    normed_in = low(normalize(stream, norm_gain[0], norm_shift[0]))
    qkv_bias = jnp.stack([b_qv[0], jnp.zeros_like(b_qv[0]), b_qv[1]])
    projected = jnp.einsum('rd,dsk->rsk', normed_in, w_qkv, precision=HIGHEST) + qkv_bias
    projected = low(low_back(projected))
    queries = to_heads(projected[:, 0])
    key_heads = to_heads(projected[:, 1])
    value_heads = to_heads(projected[:, 2])
    scores = low_back(jnp.einsum('cqhd,ckhd->chqk', queries, key_heads, precision=HIGHEST) * score_scale)
    soft_weights = low(jax.nn.softmax(scores, axis=-1))
    attended = jnp.einsum('chqk,ckhd->cqhd', soft_weights, value_heads, precision=HIGHEST)
    attended = low(low_back(attended)).reshape(row_count, D)
    hidden = stream + low_back(jnp.dot(attended, w_out, precision=HIGHEST)) + b_out
    normed_mid = low(normalize(hidden, norm_gain[1], norm_shift[1]))
    fc_inner = low_back(jnp.dot(normed_mid, w_fc1, precision=HIGHEST) + b_fc1)
    active = low(jax.nn.gelu(fc_inner, approximate=False))
    return hidden + low_back(jnp.dot(active, w_fc2, precision=HIGHEST)) + b_fc2

def forward(stream, parameters):
    for layer_index in range(2):
        layer_weights = tuple((parameter[layer_index] for parameter in parameters))
        stream = encoder_layer(stream, layer_weights)
    return stream

def reference(ends_in, ln_gain, ln_shift, w_qkv, b_qv, w_out, b_out, w_fc1, b_fc1, w_fc2, b_fc2):
    boundary = ends_in.astype(jnp.float32)
    parameters = (ln_gain.astype(jnp.float32), ln_shift.astype(jnp.float32), w_qkv.astype(jnp.float32), b_qv.astype(jnp.float32), w_out.astype(jnp.float32), b_out.astype(jnp.float32), w_fc1.astype(jnp.float32), b_fc1.astype(jnp.float32), w_fc2.astype(jnp.float32), b_fc2.astype(jnp.float32))
    groups = N_DP * MICRO
    inputs = boundary[0].reshape(groups, ROWS_MB, D)
    upstream = boundary[1].reshape(groups, ROWS_MB, D)

    def group_step(running, pair_rows):
        output, pull_back = jax.vjp(forward, pair_rows[0], parameters)
        d_stream, d_parameters = pull_back(pair_rows[1])
        return (jax.tree.map(jnp.add, running, d_parameters), (output, d_stream))
    start_sums = jax.tree.map(jnp.zeros_like, parameters)
    totals, (outputs, d_streams) = lax.scan(group_step, start_sums, (inputs, upstream))
    ends_out = jnp.stack([d_streams.reshape(TOKENS, D), outputs.reshape(TOKENS, D)])
    return (ends_out, totals[0], totals[1], totals[2], totals[3], totals[4], totals[5], totals[6], totals[7], totals[8], totals[9])
```

```python
import jax
import jax.numpy as jnp
from jax import lax
from jax.experimental import pallas as pl
from jax.experimental.pallas import tpu as pltpu
from jax.sharding import PartitionSpec as P

D = 768
HD = 64
FRAMES = 448
SHARDS = 4
HEADS_SHARD = 3
FEATS = HEADS_SHARD * HD
QKV = 3 * FEATS
FF_SHARD = 768
HALF = D // 2
EPSILON = 1e-05
SCALE = float(HD) ** (-0.5)
VMEM_LIMIT = 48 * 1024 * 1024
GAIN1, GAIN2, SHIFT1, SHIFT2, BIAS_Q, BIAS_V, BIAS_OUT, BIAS_FC2 = range(8)
BACK_ORDER = (3, 1, 2, 0)
F32 = jnp.float32
BF16 = jnp.bfloat16


def matmul(left, right, left_dim=1, right_dim=0):
    return lax.dot_general(
        left, right, (((left_dim,), (right_dim,)), ((), ())), preferred_element_type=F32
    )


def normalize(values):
    center = jnp.mean(values, axis=0, keepdims=True)
    moved = values - center
    inv_std = lax.rsqrt(jnp.mean(moved * moved, axis=0, keepdims=True) + EPSILON)
    return moved * inv_std, inv_std


def norm_backward(upstream, normed, inv_std, gain):
    scaled = upstream * gain
    mean_one = jnp.mean(scaled, axis=0, keepdims=True)
    mean_two = jnp.mean(scaled * normed, axis=0, keepdims=True)
    return inv_std * (scaled - mean_one - normed * mean_two)


def row_sums(values):
    return jnp.sum(values, axis=1, keepdims=True)


def columns(parts, lanes):
    lane = lax.broadcasted_iota(jnp.int32, (parts[0].shape[0], lanes), 1)
    total = jnp.zeros((parts[0].shape[0], lanes), F32)
    for index, part in enumerate(parts):
        total = jnp.where(lane == index, part, total)
    return total


def piece_copies(info, pieces, held, sems):
    own, other, near, far, other_near, other_far = pieces
    first = pl.multiple_of(info[4] * HALF, HALF)
    second = pl.multiple_of((1 - info[4]) * HALF, HALF)
    routes = (
        (own, held.at[0]),
        (other, held.at[1]),
        (near, held.at[2, pl.ds(first, HALF)]),
        (far, held.at[2, pl.ds(second, HALF)]),
        (other_near, held.at[3, pl.ds(first, HALF)]),
        (other_far, held.at[3, pl.ds(second, HALF)]),
    )
    copies = [
        pltpu.make_async_copy(source, target, sems.at[index])
        for index, (source, target) in enumerate(routes)
    ]
    return (copies[0:1], copies[1:2], copies[2:4], copies[4:6])


def load_pieces(step, order, chunks):
    @pl.when(step == 0)
    def start():
        for slot in order:
            for chunk in chunks:
                for copy in chunk[slot]:
                    copy.start()

    for index, slot in enumerate(order):

        @pl.when(step == index)
        def wait():
            for chunk in chunks:
                for copy in chunk[slot]:
                    copy.wait()


def attention_forward_kernel(
    info, x_ref, col_ref, w0, w1, w2, w3, w4, w5, a1_ref, p_ref, soft_ref, o_ref, h_ref, held, sems
):
    step = pl.program_id(0)
    copies = piece_copies(info, (w0, w1, w2, w3, w4, w5), held, sems)
    load_pieces(step, range(SHARDS), (copies,))

    @pl.when(step == 0)
    def first():
        col = col_ref[...].reshape(D, 8)
        values = x_ref[...].astype(F32)
        normed, _ = normalize(values)
        a1_ref[...] = (
            normed * col[:, GAIN1 : GAIN1 + 1] + col[:, SHIFT1 : SHIFT1 + 1]
        ).astype(BF16)
        h_ref[...] = values + col[:, BIAS_OUT : BIAS_OUT + 1]

    bias = col_ref[info[step]]
    projected = matmul(held[step, :QKV], a1_ref[...])
    queries = (projected[:FEATS] + bias[:, BIAS_Q : BIAS_Q + 1]).astype(BF16)
    keys = projected[FEATS : 2 * FEATS].astype(BF16)
    values = (projected[2 * FEATS :] + bias[:, BIAS_V : BIAS_V + 1]).astype(BF16)
    p_ref[0, :FEATS] = queries
    p_ref[0, FEATS : 2 * FEATS] = keys
    p_ref[0, 2 * FEATS :] = values
    scaled = queries * SCALE
    for head in range(HEADS_SHARD):
        rows = slice(head * HD, (head + 1) * HD)
        scores = matmul(keys[rows], scaled[rows], 0, 0)
        exps = jnp.exp(scores - jnp.max(scores, axis=0, keepdims=True))
        soft = exps * (1.0 / jnp.sum(exps, axis=0, keepdims=True))
        soft = soft.astype(BF16)
        soft_ref[0, head] = soft
        o_ref[0, rows] = matmul(values[rows], soft).astype(BF16)
    h_ref[...] += matmul(held[step, QKV:], o_ref[0], 0, 0)


def mlp_forward_kernel(
    info, h_ref, col_ref, b1_ref,
    w0, w1, w2, w3, w4, w5, v0, v1, v2, v3, v4, v5,
    a2_ref, u_ref, slope_ref, y_ref, held_one, held_two, a2_rows, total, sems_one, sems_two,
):
    step = pl.program_id(0)
    copies_one = piece_copies(info, (w0, w1, w2, w3, w4, w5), held_one, sems_one)
    copies_two = piece_copies(info, (v0, v1, v2, v3, v4, v5), held_two, sems_two)
    load_pieces(step, range(SHARDS), (copies_one, copies_two))

    @pl.when(step == 0)
    def first():
        col = col_ref[...].reshape(D, 8)
        normed, _ = normalize(h_ref[...])
        scaled = normed * col[:, GAIN2 : GAIN2 + 1] + col[:, SHIFT2 : SHIFT2 + 1]
        a2_ref[...] = scaled.astype(BF16)
        a2_rows[...] = scaled.T.astype(BF16)
        total[...] = jnp.zeros_like(total)

    inner = matmul(a2_rows[...], held_one[step]) + b1_ref[info[step]]
    phi = 0.5 + 0.5 * lax.erf(inner * 0.7071067811865476)
    density = 0.3989422804014327 * jnp.exp(-0.5 * inner * inner)
    active = (inner * phi).astype(BF16)
    u_ref[0] = active
    slope_ref[0] = (phi + inner * density).astype(BF16)
    total[...] += matmul(active, held_two[step])

    @pl.when(step == SHARDS - 1)
    def last():
        col = col_ref[...].reshape(D, 8)
        y_ref[...] = h_ref[...] + total[...].T + col[:, BIAS_FC2 : BIAS_FC2 + 1]


def mlp_backward_kernel(
    info, gy_ref, h_ref, a2_ref, col_ref, u_ref, slope_ref,
    w0, w1, w2, w3, w4, w5, v0, v1, v2, v3, v4, v5,
    gh_ref, send_one, keep_one, send_two, keep_two, db1_ref, dcol_ref,
    held_one, held_two, gy_rows, total, sems_one, sems_two,
):
    step = pl.program_id(0)
    copies_one = piece_copies(info, (w0, w1, w2, w3, w4, w5), held_one, sems_one)
    copies_two = piece_copies(info, (v0, v1, v2, v3, v4, v5), held_two, sems_two)
    load_pieces(step, BACK_ORDER, (copies_two, copies_one))

    @pl.when(step == 0)
    def first():
        gy_rows[...] = gy_ref[...].astype(F32).T.astype(BF16)
        total[...] = jnp.zeros_like(total)

    slot = info[5 + step]
    d_active = matmul(gy_rows[...], held_two[slot], 1, 1)
    d_inner = d_active * slope_ref[0].astype(F32)
    rounded = d_inner.astype(BF16)
    db1_ref[info[slot]] = jnp.sum(rounded.astype(F32), axis=0, keepdims=True)
    d_two = matmul(u_ref[0], gy_rows[...], 0, 0).astype(BF16)
    d_one = matmul(a2_ref[...], rounded).astype(BF16)

    @pl.when(step < 2)
    def sent():
        send_one[0] = d_one
        send_two[0] = d_two

    @pl.when(step >= 2)
    def kept():
        keep_one[0] = d_one
        keep_two[0] = d_two

    total[...] += matmul(rounded, held_one[slot], 1, 1)

    @pl.when(step == SHARDS - 1)
    def last():
        col = col_ref[...].reshape(D, 8)
        normed, inv_std = normalize(h_ref[...])
        d_mid = total[...].T
        upstream = gy_ref[...].astype(F32)
        d_hidden = upstream + norm_backward(d_mid, normed, inv_std, col[:, GAIN2 : GAIN2 + 1])
        gh_ref[...] = d_hidden
        dcol_ref[...] = columns(
            [row_sums(d_mid * normed), row_sums(d_mid), row_sums(d_hidden), row_sums(upstream)], 8
        )


def attention_backward_kernel(
    info, gh_ref, x_ref, a1_ref, col_ref, p_ref, soft_ref, o_ref,
    w0, w1, w2, w3, w4, w5,
    gx_ref, send_ref, keep_ref, dbqv_ref, dcol_ref,
    held, gh_rounded, g_p, total, sems,
):
    step = pl.program_id(0)
    copies = piece_copies(info, (w0, w1, w2, w3, w4, w5), held, sems)
    load_pieces(step, BACK_ORDER, (copies,))

    @pl.when(step == 0)
    def first():
        gh_rounded[...] = gh_ref[...].astype(BF16)
        total[...] = jnp.zeros_like(total)

    slot = info[5 + step]
    d_attended = matmul(held[slot, QKV:], gh_rounded[...]).astype(BF16)
    d_out = matmul(o_ref[0], gh_rounded[...], 1, 1).astype(BF16)
    for head in range(HEADS_SHARD):
        rows = slice(head * HD, (head + 1) * HD)
        queries = p_ref[0, rows]
        keys = p_ref[0, FEATS + head * HD : FEATS + (head + 1) * HD]
        values = p_ref[0, 2 * FEATS + head * HD : 2 * FEATS + (head + 1) * HD]
        soft = soft_ref[0, head]
        d_att = d_attended[rows]
        delta = jnp.sum(
            d_att.astype(F32) * o_ref[0, rows].astype(F32), axis=0, keepdims=True
        )
        d_soft = matmul(values, d_att, 0, 0)
        d_scores = (soft.astype(F32) * (d_soft - delta)).astype(BF16)
        g_p[rows] = (matmul(keys, d_scores) * SCALE).astype(BF16)
        g_p[FEATS + head * HD : FEATS + (head + 1) * HD] = (
            matmul(queries, d_scores, 1, 1) * SCALE
        ).astype(BF16)
        g_p[2 * FEATS + head * HD : 2 * FEATS + (head + 1) * HD] = matmul(
            d_att, soft, 1, 1
        ).astype(BF16)
    d_projected = g_p[...]
    d_qkv = matmul(d_projected, a1_ref[...], 1, 1).astype(BF16)
    total[...] += matmul(d_projected, held[slot, :QKV], 0, 0)
    dbqv_ref[info[slot]] = columns(
        [row_sums(d_projected[:FEATS].astype(F32)), row_sums(d_projected[2 * FEATS :].astype(F32))],
        8,
    )

    @pl.when(step < 2)
    def sent():
        send_ref[0, :QKV] = d_qkv
        send_ref[0, QKV:] = d_out

    @pl.when(step >= 2)
    def kept():
        keep_ref[0, :QKV] = d_qkv
        keep_ref[0, QKV:] = d_out

    @pl.when(step == SHARDS - 1)
    def last():
        col = col_ref[...].reshape(D, 8)
        normed, inv_std = normalize(x_ref[...].astype(F32))
        d_first = total[...].T
        gx_ref[...] = gh_ref[...] + norm_backward(
            d_first, normed, inv_std, col[:, GAIN1 : GAIN1 + 1]
        )
        dcol_ref[...] = columns([row_sums(d_first * normed), row_sums(d_first)], 8)


def whole(shape):
    return pl.BlockSpec(shape, lambda i, info: (0,) * len(shape))


def by_step(shape):
    return pl.BlockSpec((1,) + shape, lambda i, info: (i,) + (0,) * len(shape))


def by_slot(shape):
    return pl.BlockSpec((1,) + shape, lambda i, info: (info[5 + i],) + (0,) * len(shape))


SENT = pl.BlockSpec((1, D, D), lambda i, info: (jnp.minimum(i, 1), 0, 0))
KEPT = pl.BlockSpec((1, D, D), lambda i, info: (jnp.maximum(i - 2, 0), 0, 0))
PIECES = [pl.BlockSpec(memory_space=pl.ANY)] * 6
COPY_SEMS = pltpu.SemaphoreType.DMA((6,))
HELD = pltpu.VMEM((SHARDS, D, D), BF16)


def of(shape, dtype=BF16):
    return jax.ShapeDtypeStruct(shape, dtype)


def run(kernel, name, info, operands, in_specs, outs, out_specs, scratch, flops):
    moved = sum(a.size * a.dtype.itemsize for a in operands) + sum(
        a.size * a.dtype.itemsize for a in outs
    )
    return pl.pallas_call(
        kernel,
        name=name,
        out_shape=outs,
        grid_spec=pltpu.PrefetchScalarGridSpec(
            num_scalar_prefetch=1,
            grid=(SHARDS,),
            in_specs=in_specs,
            out_specs=out_specs,
            scratch_shapes=scratch,
        ),
        compiler_params=pltpu.CompilerParams(
            vmem_limit_bytes=VMEM_LIMIT, dimension_semantics=("arbitrary",)
        ),
        cost_estimate=pl.CostEstimate(flops=flops, bytes_accessed=moved, transcendentals=0),
    )(info, *operands)


STREAM = (D, FRAMES)
ATT_FLOPS = 2 * FRAMES * D * (4 * D + 2 * FRAMES)
MLP_FLOPS = 4 * FRAMES * D * SHARDS * FF_SHARD


def attention_forward(info, x, col, chunk):
    return run(
        attention_forward_kernel, "attention_forward", info, (x, col, *chunk),
        [whole(STREAM), whole((SHARDS, FEATS, 8))] + PIECES,
        [
            of(STREAM), of((SHARDS, QKV, FRAMES)), of((SHARDS, HEADS_SHARD, FRAMES, FRAMES)),
            of((SHARDS, FEATS, FRAMES)), of(STREAM, F32),
        ],
        [
            whole(STREAM), by_step((QKV, FRAMES)), by_step((HEADS_SHARD, FRAMES, FRAMES)),
            by_step((FEATS, FRAMES)), whole(STREAM),
        ],
        [HELD, COPY_SEMS],
        ATT_FLOPS,
    )


def mlp_forward(info, h, col, b1, chunk_one, chunk_two):
    return run(
        mlp_forward_kernel, "mlp_forward", info, (h, col, b1, *chunk_one, *chunk_two),
        [whole(STREAM), whole((SHARDS, FEATS, 8)), whole((SHARDS, 1, FF_SHARD))] + PIECES * 2,
        [of(STREAM), of((SHARDS, FRAMES, FF_SHARD)), of((SHARDS, FRAMES, FF_SHARD)), of(STREAM, F32)],
        [whole(STREAM), by_step((FRAMES, FF_SHARD)), by_step((FRAMES, FF_SHARD)), whole(STREAM)],
        [
            HELD, HELD, pltpu.VMEM((FRAMES, D), BF16), pltpu.VMEM((FRAMES, D), F32),
            COPY_SEMS, COPY_SEMS,
        ],
        MLP_FLOPS,
    )


def mlp_backward(info, gy, h, a2, col, u, slope, chunk_one, chunk_two):
    pair = of((2, D, D))
    return run(
        mlp_backward_kernel, "mlp_backward", info, (gy, h, a2, col, u, slope, *chunk_one, *chunk_two),
        [
            whole(STREAM), whole(STREAM), whole(STREAM), whole((SHARDS, FEATS, 8)),
            by_slot((FRAMES, FF_SHARD)), by_slot((FRAMES, FF_SHARD)),
        ]
        + PIECES * 2,
        [of(STREAM, F32), pair, pair, pair, pair, of((SHARDS, 1, FF_SHARD), F32), of((D, 8), F32)],
        [whole(STREAM), SENT, KEPT, SENT, KEPT, whole((SHARDS, 1, FF_SHARD)), whole((D, 8))],
        [
            HELD, HELD, pltpu.VMEM((FRAMES, D), BF16), pltpu.VMEM((FRAMES, D), F32),
            COPY_SEMS, COPY_SEMS,
        ],
        2 * MLP_FLOPS,
    )


def attention_backward(info, gh, x, a1, col, p, soft, o, chunk):
    pair = of((2, D, D))
    return run(
        attention_backward_kernel, "attention_backward", info, (gh, x, a1, col, p, soft, o, *chunk),
        [
            whole(STREAM), whole(STREAM), whole(STREAM), whole((SHARDS, FEATS, 8)),
            by_slot((QKV, FRAMES)), by_slot((HEADS_SHARD, FRAMES, FRAMES)), by_slot((FEATS, FRAMES)),
        ]
        + PIECES,
        [of(STREAM, F32), pair, pair, of((SHARDS, FEATS, 8), F32), of((D, 8), F32)],
        [whole(STREAM), SENT, KEPT, whole((SHARDS, FEATS, 8)), whole((D, 8))],
        [
            HELD, pltpu.VMEM(STREAM, BF16), pltpu.VMEM((QKV, FRAMES), BF16),
            pltpu.VMEM((FRAMES, D), F32), COPY_SEMS,
        ],
        2 * ATT_FLOPS,
    )


def flip(block, axis, bit):
    size = lax.axis_size(axis)
    return lax.ppermute(block, axis, [(i, i ^ bit) for i in range(size)])


def spread(own, zhalf):
    half = lax.dynamic_slice_in_dim(own, zhalf * HALF, HALF, axis=0)
    near = flip(half, "tensor", 2)
    far = flip(near, "dp", 1)
    other = flip(own, "tensor", 1)
    return (own, other, near, far, flip(near, "tensor", 1), flip(far, "tensor", 1))


def added(left, right):
    return (left.astype(F32) + right.astype(F32)).astype(BF16)


def reduce_chunk(send, keep, layer):
    other = flip(send, "tensor", 1)
    total = added(keep[1], other[1])
    away = added(keep[0], other[0])
    total = added(total, flip(away, "tensor", 2))
    total = added(total, lax.ppermute(total, "section", [(1 - layer, layer)]))
    n_dp = lax.axis_size("dp")
    if n_dp != 4:
        return lax.psum(total, "dp")
    axes = ("section", "dp")
    base = layer * n_dp
    total = added(total, lax.ppermute(total, axes, [(base, base + 1), (base + 3, base + 2)]))
    total = added(total, lax.ppermute(total, axes, [(base + 1, base + 2), (base + 2, base + 1)]))
    back = lax.ppermute(total, axes, [(base + 1, base), (base + 2, base + 3)])
    place = lax.axis_index("dp")
    return jnp.where((place == 0) | (place == 3), back, total)


def body(ends_in, ln_gain, ln_shift, w_qkv, b_qv, w_out, b_out, w_fc1, b_fc1, w_fc2, b_fc2):
    section = lax.axis_index("section")
    shard = lax.axis_index("tensor")
    zhalf = lax.axis_index("dp") % 2
    clips = ends_in.shape[1] // FRAMES
    info = jnp.stack(
        [shard, shard ^ 1, shard ^ 2, shard ^ 3, zhalf] + [jnp.int32(k) for k in BACK_ORDER]
    ).astype(jnp.int32)

    small = jnp.concatenate(
        [
            ln_gain[0], ln_shift[0], b_qv[0], b_out, b_fc2, b_fc1.reshape(SHARDS, FEATS),
        ],
        axis=0,
    )
    small = lax.all_gather(small, ("section", "tensor"), axis=0, tiled=False)
    small = small.reshape(2, SHARDS, 12, FEATS).astype(F32)
    cols = jnp.transpose(small[:, :, :8], (0, 1, 3, 2))
    b1s = small[:, :, 8:].reshape(2, SHARDS, 1, FF_SHARD)

    ends = ends_in[0].T.reshape(FEATS, clips, FRAMES).transpose(1, 0, 2)
    ends = lax.all_to_all(ends, ("section", "tensor"), split_axis=0, concat_axis=0, tiled=True)
    ends = ends.reshape(2, D, FRAMES)

    owned = [
        jnp.concatenate([w_qkv[0].transpose(1, 2, 0).reshape(QKV, D), w_out[0]], axis=0),
        w_fc1[0],
        w_fc2[0],
    ]
    chunks = [[], []]
    previous = None
    for own in owned:
        leaving = own
        if previous is not None:
            leaving, _ = lax.optimization_barrier((own, previous))
        previous = flip(leaving, "section", 1)
        chunks[0].append(jnp.where(section == 0, own, previous))
        chunks[1].append(jnp.where(section == 0, previous, own))
    chunks = [[spread(own, zhalf) for own in layer] for layer in chunks]

    stream = ends[0]
    stored = []
    for layer in range(2):
        chunk_a, chunk_one, chunk_two = chunks[layer]
        a1, p, soft, o, h = attention_forward(info, stream, cols[layer], chunk_a)
        a2, u, slope, y = mlp_forward(info, h, cols[layer], b1s[layer], chunk_one, chunk_two)
        stored.append((stream, a1, p, soft, o, h, a2, u, slope))
        stream = y

    upstream = ends[1]
    summed = [None, None]
    smalls = [None, None]
    for layer in (1, 0):
        chunk_a, chunk_one, chunk_two = chunks[layer]
        x, a1, p, soft, o, h, a2, u, slope = stored[layer]
        gh, send_one, keep_one, send_two, keep_two, db1, dcol_two = mlp_backward(
            info, upstream, h, a2, cols[layer], u, slope, chunk_one, chunk_two
        )
        grad_two = reduce_chunk(send_two, keep_two, layer)
        grad_one = reduce_chunk(send_one, keep_one, layer)
        upstream, send_a, keep_a, dbqv, dcol_one = attention_backward(
            info, gh, x, a1, cols[layer], p, soft, o, chunk_a
        )
        grad_a = reduce_chunk(send_a, keep_a, layer)
        summed[layer] = (grad_a, grad_one, grad_two)
        dcol = jnp.stack(
            [
                dcol_one[:, 0], dcol_two[:, 0], dcol_one[:, 1], dcol_two[:, 1],
                dbqv[:, :, 0].reshape(D), dbqv[:, :, 1].reshape(D), dcol_two[:, 2], dcol_two[:, 3],
            ]
        )
        smalls[layer] = jnp.concatenate(
            [
                dcol.reshape(8, SHARDS, FEATS).transpose(1, 0, 2),
                db1.reshape(SHARDS, SHARDS, FEATS),
            ],
            axis=1,
        )

    small_sum = lax.psum(jnp.stack(smalls), ("section", "tensor", "dp"))
    small_sum = lax.dynamic_slice(
        small_sum, (section, shard, 0, 0), (1, 1, 12, FEATS)
    ).reshape(12, FEATS)

    result = jnp.stack([upstream.astype(BF16), stream.astype(BF16)])
    result = result.reshape(2 * SHARDS, FEATS, FRAMES)
    result = lax.all_to_all(result, ("section", "tensor"), split_axis=0, concat_axis=0, tiled=True)
    result = result.transpose(1, 0, 2).reshape(FEATS, clips * FRAMES).T.astype(F32)

    grad_a, grad_one, grad_two = [
        jnp.where(section == 0, first, second).astype(F32)
        for first, second in zip(summed[0], summed[1])
    ]
    return (
        result[None],
        small_sum[None, 0:2],
        small_sum[None, 2:4],
        grad_a[:QKV].reshape(3, FEATS, D).transpose(2, 0, 1)[None],
        small_sum[None, 4:6],
        grad_a[QKV:][None],
        small_sum[6:7],
        grad_one[None],
        small_sum[8:12].reshape(1, FF_SHARD),
        grad_two[None],
        small_sum[7:8],
    )


def solution(mesh):
    placed = (
        P("section", "dp", "tensor"),
        P("section", None, "tensor"),
        P("section", None, "tensor"),
        P("section", None, None, "tensor"),
        P("section", None, "tensor"),
        P("section", "tensor", None),
        P("section", "tensor"),
        P("section", None, "tensor"),
        P("section", "tensor"),
        P("section", "tensor", None),
        P("section", "tensor"),
    )
    return jax.shard_map(
        body, mesh=mesh, in_specs=placed, out_specs=placed, check_vma=False
    )
```

```python
import functools

import jax
import jax.numpy as jnp
from jax import lax
from jax.experimental import pallas as pl
from jax.experimental.pallas import tpu as pltpu
from jax.sharding import PartitionSpec as P

D = 768
HD = 64
FRAMES = 448
SHARDS = 4
HEADS_SHARD = 3
FEATS = HEADS_SHARD * HD
QKV = 3 * FEATS
FF_SHARD = 768
HALF = D // 2
EPSILON = 1e-05
SCALE = float(HD) ** (-0.5)
VMEM_LIMIT = 48 * 1024 * 1024
GAIN1, GAIN2, SHIFT1, SHIFT2, BIAS_Q, BIAS_V, BIAS_OUT, BIAS_FC2 = range(8)
BACK_ORDER = (3, 1, 2, 0)
F32 = jnp.float32
BF16 = jnp.bfloat16


def matmul(left, right, left_dim=1, right_dim=0):
    return lax.dot_general(
        left, right, (((left_dim,), (right_dim,)), ((), ())), preferred_element_type=F32
    )


def normalize(values):
    center = jnp.mean(values, axis=0, keepdims=True)
    moved = values - center
    inv_std = lax.rsqrt(jnp.mean(moved * moved, axis=0, keepdims=True) + EPSILON)
    return moved * inv_std, inv_std


def norm_backward(upstream, normed, inv_std, gain):
    scaled = upstream * gain
    mean_one = jnp.mean(scaled, axis=0, keepdims=True)
    mean_two = jnp.mean(scaled * normed, axis=0, keepdims=True)
    return inv_std * (scaled - mean_one - normed * mean_two)


def row_sums(values):
    return jnp.sum(values, axis=1, keepdims=True)


def columns(parts, lanes):
    lane = lax.broadcasted_iota(jnp.int32, (parts[0].shape[0], lanes), 1)
    total = jnp.zeros((parts[0].shape[0], lanes), F32)
    for index, part in enumerate(parts):
        total = jnp.where(lane == index, part, total)
    return total


def piece_copies(info, pieces, held, sems):
    own, other, near, far, other_near, other_far = pieces
    first = pl.multiple_of(info[4] * HALF, HALF)
    second = pl.multiple_of((1 - info[4]) * HALF, HALF)
    routes = (
        (own, held.at[0]),
        (other, held.at[1]),
        (near, held.at[2, pl.ds(first, HALF)]),
        (far, held.at[2, pl.ds(second, HALF)]),
        (other_near, held.at[3, pl.ds(first, HALF)]),
        (other_far, held.at[3, pl.ds(second, HALF)]),
    )
    copies = [
        pltpu.make_async_copy(source, target, sems.at[index])
        for index, (source, target) in enumerate(routes)
    ]
    return (copies[0:1], copies[1:2], copies[2:4], copies[4:6])


def load_pieces(step, order, chunks):
    @pl.when(step == 0)
    def start():
        for slot in order:
            for chunk in chunks:
                for copy in chunk[slot]:
                    copy.start()

    for index, slot in enumerate(order):

        @pl.when(step == index)
        def wait():
            for chunk in chunks:
                for copy in chunk[slot]:
                    copy.wait()


def attention_forward_kernel(
    info, x_ref, col_ref, bqv_ref, w0, w1, w2, w3, w4, w5, a1_ref, p_ref, soft_ref, o_ref, h_ref, held, sems
):
    step = pl.program_id(0)
    copies = piece_copies(info, (w0, w1, w2, w3, w4, w5), held, sems)
    load_pieces(step, range(SHARDS), (copies,))

    @pl.when(step == 0)
    def first():
        col = col_ref[...].reshape(D, 8)
        values = x_ref[...].astype(F32)
        normed, _ = normalize(values)
        a1_ref[...] = (
            normed * col[:, GAIN1 : GAIN1 + 1] + col[:, SHIFT1 : SHIFT1 + 1]
        ).astype(BF16)
        h_ref[...] = values + col[:, BIAS_OUT : BIAS_OUT + 1]

    bias = bqv_ref[step]
    projected = matmul(held[step, :QKV], a1_ref[...])
    queries = (projected[:FEATS] + bias[:, 0:1]).astype(BF16)
    keys = projected[FEATS : 2 * FEATS].astype(BF16)
    values = (projected[2 * FEATS :] + bias[:, 1:2]).astype(BF16)
    p_ref[0, :FEATS] = queries
    p_ref[0, FEATS : 2 * FEATS] = keys
    p_ref[0, 2 * FEATS :] = values
    scaled = queries * SCALE
    for head in range(HEADS_SHARD):
        rows = slice(head * HD, (head + 1) * HD)
        scores = matmul(keys[rows], scaled[rows], 0, 0)
        exps = jnp.exp(scores - jnp.max(scores, axis=0, keepdims=True))
        soft = exps * (1.0 / jnp.sum(exps, axis=0, keepdims=True))
        soft = soft.astype(BF16)
        soft_ref[0, head] = soft
        o_ref[0, rows] = matmul(values[rows], soft).astype(BF16)
    h_ref[...] += matmul(held[step, QKV:], o_ref[0], 0, 0)


def mlp_forward_kernel(
    info, h_ref, col_ref, b1_ref,
    w0, w1, w2, w3, w4, w5, v0, v1, v2, v3, v4, v5,
    a2_ref, u_ref, slope_ref, y_ref, held_one, held_two, a2_rows, total, sems_one, sems_two,
):
    step = pl.program_id(0)
    copies_one = piece_copies(info, (w0, w1, w2, w3, w4, w5), held_one, sems_one)
    copies_two = piece_copies(info, (v0, v1, v2, v3, v4, v5), held_two, sems_two)
    load_pieces(step, range(SHARDS), (copies_one, copies_two))

    @pl.when(step == 0)
    def first():
        col = col_ref[...].reshape(D, 8)
        normed, _ = normalize(h_ref[...])
        scaled = normed * col[:, GAIN2 : GAIN2 + 1] + col[:, SHIFT2 : SHIFT2 + 1]
        a2_ref[...] = scaled.astype(BF16)
        a2_rows[...] = scaled.T.astype(BF16)
        total[...] = jnp.zeros_like(total)

    inner = matmul(a2_rows[...], held_one[step]) + b1_ref[step]
    phi = 0.5 + 0.5 * lax.erf(inner * 0.7071067811865476)
    density = 0.3989422804014327 * jnp.exp(-0.5 * inner * inner)
    active = (inner * phi).astype(BF16)
    u_ref[0] = active
    slope_ref[0] = (phi + inner * density).astype(BF16)
    total[...] += matmul(active, held_two[step])

    @pl.when(step == SHARDS - 1)
    def last():
        col = col_ref[...].reshape(D, 8)
        y_ref[...] = h_ref[...] + total[...].T + col[:, BIAS_FC2 : BIAS_FC2 + 1]


def mlp_backward_kernel(
    last, info, gy_ref, h_ref, a2_ref, col_ref, u_ref, slope_ref, *refs
):
    step = pl.program_id(0)
    if last:
        before_ref, *refs = refs
    pieces_one, pieces_two, refs = refs[:6], refs[6:12], refs[12:]
    if last:
        gh_ref, dcol_ref, *refs = refs
    else:
        after_ref, *refs = refs
    grad_one, grad_two, db1_ref, held_one, held_two, gy_rows, total, sems_one, sems_two = refs
    copies_one = piece_copies(info, pieces_one, held_one, sems_one)
    copies_two = piece_copies(info, pieces_two, held_two, sems_two)
    load_pieces(step, BACK_ORDER[2:] if last else BACK_ORDER[:2], (copies_two, copies_one))

    @pl.when(step == 0)
    def first():
        gy_rows[...] = gy_ref[...].astype(F32).T.astype(BF16)
        total[...] = before_ref[...] if last else jnp.zeros_like(total)

    slot = info[(7 if last else 5) + step]
    d_active = matmul(gy_rows[...], held_two[slot], 1, 1)
    d_inner = d_active * slope_ref[0].astype(F32)
    rounded = d_inner.astype(BF16)
    db1_ref[step] = jnp.sum(rounded.astype(F32), axis=0, keepdims=True)
    grad_two[0] = matmul(u_ref[0], gy_rows[...], 0, 0).astype(BF16)
    grad_one[0] = matmul(a2_ref[...], rounded).astype(BF16)
    total[...] += matmul(rounded, held_one[slot], 1, 1)

    @pl.when(step == 1)
    def end():
        if not last:
            after_ref[...] = total[...]
            return
        col = col_ref[...].reshape(D, 8)
        normed, inv_std = normalize(h_ref[...])
        d_mid = total[...].T
        upstream = gy_ref[...].astype(F32)
        d_hidden = upstream + norm_backward(d_mid, normed, inv_std, col[:, GAIN2 : GAIN2 + 1])
        gh_ref[...] = d_hidden
        dcol_ref[...] = columns(
            [row_sums(d_mid * normed), row_sums(d_mid), row_sums(d_hidden), row_sums(upstream)], 8
        )


def attention_backward_kernel(
    last, info, gh_ref, x_ref, a1_ref, col_ref, p_ref, soft_ref, o_ref, *refs
):
    step = pl.program_id(0)
    if last:
        before_ref, *refs = refs
    pieces, refs = refs[:6], refs[6:]
    if last:
        gx_ref, dcol_ref, *refs = refs
    else:
        after_ref, *refs = refs
    grad_ref, dbqv_ref, held, gh_rounded, g_p, total, sems = refs
    copies = piece_copies(info, pieces, held, sems)
    load_pieces(step, BACK_ORDER[2:] if last else BACK_ORDER[:2], (copies,))

    @pl.when(step == 0)
    def first():
        gh_rounded[...] = gh_ref[...].astype(BF16)
        total[...] = before_ref[...] if last else jnp.zeros_like(total)

    slot = info[(7 if last else 5) + step]
    d_attended = matmul(held[slot, QKV:], gh_rounded[...]).astype(BF16)
    grad_ref[0, QKV:] = matmul(o_ref[0], gh_rounded[...], 1, 1).astype(BF16)
    for head in range(HEADS_SHARD):
        rows = slice(head * HD, (head + 1) * HD)
        queries = p_ref[0, rows]
        keys = p_ref[0, FEATS + head * HD : FEATS + (head + 1) * HD]
        values = p_ref[0, 2 * FEATS + head * HD : 2 * FEATS + (head + 1) * HD]
        soft = soft_ref[0, head]
        d_att = d_attended[rows]
        delta = jnp.sum(
            d_att.astype(F32) * o_ref[0, rows].astype(F32), axis=0, keepdims=True
        )
        d_soft = matmul(values, d_att, 0, 0)
        d_scores = (soft.astype(F32) * (d_soft - delta)).astype(BF16)
        g_p[rows] = (matmul(keys, d_scores) * SCALE).astype(BF16)
        g_p[FEATS + head * HD : FEATS + (head + 1) * HD] = (
            matmul(queries, d_scores, 1, 1) * SCALE
        ).astype(BF16)
        g_p[2 * FEATS + head * HD : 2 * FEATS + (head + 1) * HD] = matmul(
            d_att, soft, 1, 1
        ).astype(BF16)
    d_projected = g_p[...]
    grad_ref[0, :QKV] = matmul(d_projected, a1_ref[...], 1, 1).astype(BF16)
    total[...] += matmul(d_projected, held[slot, :QKV], 0, 0)
    dbqv_ref[step] = columns(
        [row_sums(d_projected[:FEATS].astype(F32)), row_sums(d_projected[2 * FEATS :].astype(F32))],
        8,
    )

    @pl.when(step == 1)
    def end():
        if not last:
            after_ref[...] = total[...]
            return
        col = col_ref[...].reshape(D, 8)
        normed, inv_std = normalize(x_ref[...].astype(F32))
        d_first = total[...].T
        gx_ref[...] = gh_ref[...] + norm_backward(
            d_first, normed, inv_std, col[:, GAIN1 : GAIN1 + 1]
        )
        dcol_ref[...] = columns([row_sums(d_first * normed), row_sums(d_first)], 8)


def whole(shape):
    return pl.BlockSpec(shape, lambda i, info: (0,) * len(shape))


def by_step(shape):
    return pl.BlockSpec((1,) + shape, lambda i, info: (i,) + (0,) * len(shape))


def by_slot(shape, last):
    first = 7 if last else 5
    return pl.BlockSpec((1,) + shape, lambda i, info: (info[first + i],) + (0,) * len(shape))


PIECES = [pl.BlockSpec(memory_space=pl.ANY)] * 6
COPY_SEMS = pltpu.SemaphoreType.DMA((6,))
HELD = pltpu.VMEM((SHARDS, D, D), BF16)


def of(shape, dtype=BF16):
    return jax.ShapeDtypeStruct(shape, dtype)


def run(kernel, name, steps, info, operands, in_specs, outs, out_specs, scratch, flops):
    moved = sum(a.size * a.dtype.itemsize for a in operands) + sum(
        a.size * a.dtype.itemsize for a in outs
    )
    return pl.pallas_call(
        kernel,
        name=name,
        out_shape=outs,
        grid_spec=pltpu.PrefetchScalarGridSpec(
            num_scalar_prefetch=1,
            grid=(steps,),
            in_specs=in_specs,
            out_specs=out_specs,
            scratch_shapes=scratch,
        ),
        compiler_params=pltpu.CompilerParams(
            vmem_limit_bytes=VMEM_LIMIT, dimension_semantics=("arbitrary",)
        ),
        cost_estimate=pl.CostEstimate(flops=flops, bytes_accessed=moved, transcendentals=0),
    )(info, *operands)


STREAM = (D, FRAMES)
ROWS = (FRAMES, D)
COLS = (SHARDS, FEATS, 8)
ATT_FLOPS = 2 * FRAMES * D * (4 * D + 2 * FRAMES)
MLP_FLOPS = 4 * FRAMES * D * SHARDS * FF_SHARD


def attention_forward(info, x, col, bqv, chunk):
    return run(
        attention_forward_kernel, "attention_forward", SHARDS, info, (x, col, bqv, *chunk),
        [whole(STREAM), whole(COLS), whole((SHARDS, FEATS, 2))] + PIECES,
        [
            of(STREAM), of((SHARDS, QKV, FRAMES)), of((SHARDS, HEADS_SHARD, FRAMES, FRAMES)),
            of((SHARDS, FEATS, FRAMES)), of(STREAM, F32),
        ],
        [
            whole(STREAM), by_step((QKV, FRAMES)), by_step((HEADS_SHARD, FRAMES, FRAMES)),
            by_step((FEATS, FRAMES)), whole(STREAM),
        ],
        [HELD, COPY_SEMS],
        ATT_FLOPS,
    )


def mlp_forward(info, h, col, b1, chunk_one, chunk_two):
    return run(
        mlp_forward_kernel, "mlp_forward", SHARDS, info, (h, col, b1, *chunk_one, *chunk_two),
        [whole(STREAM), whole(COLS), whole((SHARDS, 1, FF_SHARD))] + PIECES * 2,
        [of(STREAM), of((SHARDS, FRAMES, FF_SHARD)), of((SHARDS, FRAMES, FF_SHARD)), of(STREAM, F32)],
        [whole(STREAM), by_step((FRAMES, FF_SHARD)), by_step((FRAMES, FF_SHARD)), whole(STREAM)],
        [HELD, HELD, pltpu.VMEM(ROWS, BF16), pltpu.VMEM(ROWS, F32), COPY_SEMS, COPY_SEMS],
        MLP_FLOPS,
    )


def mlp_backward(info, gy, h, a2, col, u, slope, before, chunk_one, chunk_two):
    last = before is not None
    carried = (before,) if last else ()
    ends = [of(STREAM, F32), of((D, 8), F32)] if last else [of(ROWS, F32)]
    return run(
        functools.partial(mlp_backward_kernel, last), "mlp_backward", 2, info,
        (gy, h, a2, col, u, slope, *carried, *chunk_one, *chunk_two),
        [
            whole(STREAM), whole(STREAM), whole(STREAM), whole(COLS),
            by_slot((FRAMES, FF_SHARD), last), by_slot((FRAMES, FF_SHARD), last),
        ]
        + [whole(ROWS)] * len(carried)
        + PIECES * 2,
        ends + [of((2, D, D)), of((2, D, D)), of((2, 1, FF_SHARD), F32)],
        [whole(end.shape) for end in ends]
        + [by_step((D, D)), by_step((D, D)), whole((2, 1, FF_SHARD))],
        [HELD, HELD, pltpu.VMEM(ROWS, BF16), pltpu.VMEM(ROWS, F32), COPY_SEMS, COPY_SEMS],
        MLP_FLOPS,
    )


def attention_backward(info, gh, x, a1, col, p, soft, o, before, chunk):
    last = before is not None
    carried = (before,) if last else ()
    ends = [of(STREAM, F32), of((D, 8), F32)] if last else [of(ROWS, F32)]
    return run(
        functools.partial(attention_backward_kernel, last), "attention_backward", 2, info,
        (gh, x, a1, col, p, soft, o, *carried, *chunk),
        [
            whole(STREAM), whole(STREAM), whole(STREAM), whole(COLS),
            by_slot((QKV, FRAMES), last), by_slot((HEADS_SHARD, FRAMES, FRAMES), last),
            by_slot((FEATS, FRAMES), last),
        ]
        + [whole(ROWS)] * len(carried)
        + PIECES,
        ends + [of((2, D, D)), of((2, FEATS, 8), F32)],
        [whole(end.shape) for end in ends] + [by_step((D, D)), whole((2, FEATS, 8))],
        [HELD, pltpu.VMEM(STREAM, BF16), pltpu.VMEM((QKV, FRAMES), BF16), pltpu.VMEM(ROWS, F32), COPY_SEMS],
        ATT_FLOPS,
    )


def tie(groups):
    return lax.optimization_barrier(groups)


def flip(block, axis, bit):
    size = lax.axis_size(axis)
    return lax.ppermute(block, axis, [(i, i ^ bit) for i in range(size)])


def added(left, right):
    return (left.astype(F32) + right.astype(F32)).astype(BF16)


def by_bits(slots, shard):
    odd = shard % 2 == 1
    high = shard >= 2
    first, second, third, fourth = slots
    first, second = jnp.where(odd, second, first), jnp.where(odd, first, second)
    third, fourth = jnp.where(odd, fourth, third), jnp.where(odd, third, fourth)
    return jnp.stack(
        [
            jnp.where(high, third, first), jnp.where(high, fourth, second),
            jnp.where(high, first, third), jnp.where(high, second, fourth),
        ]
    )


class Chain:
    def __init__(self, layer):
        self.layer = layer
        self.total = None
        self.arrived = None

    def start(self, send):
        self.arrived = flip(send, "tensor", 1)

    def fold_cores(self, keep):
        self.away = added(keep[0], self.arrived[0])
        self.total = added(keep[1], self.arrived[1])

    def send_y(self):
        self.arrived = flip(self.away, "tensor", 2)

    def fold(self):
        if self.arrived is not None:
            self.total = added(self.total, self.arrived)

    def send_x(self):
        self.arrived = lax.ppermute(self.total, "section", [(1 - self.layer, self.layer)])

    def send_z(self, stage):
        if lax.axis_size("dp") != 4:
            self.total = lax.psum(self.total, "dp") if stage == 0 else self.total
            self.arrived = None
            return
        base = self.layer * 4
        pairs = (((0, 1), (3, 2)), ((1, 2), (2, 1)), ((1, 0), (2, 3)))[stage]
        pairs = [(base + source, base + target) for source, target in pairs]
        self.arrived = lax.ppermute(self.total, ("section", "dp"), pairs)

    def close(self):
        if self.arrived is None:
            return
        place = lax.axis_index("dp")
        self.total = jnp.where((place == 0) | (place == 3), self.arrived, self.total)


def sum_all(values):
    for axis in ("tensor", "section", "dp"):
        size, bit = lax.axis_size(axis), 1
        while bit < size:
            values = values + flip(values, axis, bit)
            bit *= 2
    return values


def body(ends_in, ln_gain, ln_shift, w_qkv, b_qv, w_out, b_out, w_fc1, b_fc1, w_fc2, b_fc2):
    section = lax.axis_index("section")
    shard = lax.axis_index("tensor")
    zhalf = lax.axis_index("dp") % 2
    clips = ends_in.shape[1] // FRAMES
    info = jnp.stack(
        [shard, shard ^ 1, shard ^ 2, shard ^ 3, zhalf] + [jnp.int32(k) for k in BACK_ORDER]
    ).astype(jnp.int32)

    ends = ends_in[0].T.reshape(FEATS, clips, FRAMES).transpose(1, 0, 2)
    ends = lax.all_to_all(ends, ("section", "tensor"), split_axis=0, concat_axis=0, tiled=True)
    ends = ends.reshape(2, D, FRAMES)

    small = jnp.concatenate(
        [ln_gain[0], ln_shift[0], b_qv[0], b_out, b_fc2, b_fc1.reshape(SHARDS, FEATS)], axis=0
    )
    beyond = flip(small, "section", 1)
    small = jnp.stack([jnp.where(section == 0, small, beyond), jnp.where(section == 0, beyond, small)])
    small_y = flip(small, "tensor", 2)
    pair = jnp.stack([small, small_y])
    pair_other = flip(pair, "tensor", 1)
    slots = jnp.stack([pair[0], pair_other[0], pair[1], pair_other[1]]).astype(F32)
    cols = jnp.transpose(by_bits(slots[:, :, :8], shard), (1, 0, 3, 2))
    bqvs = jnp.transpose(slots[:, :, 4:6], (1, 0, 3, 2))
    b1s = jnp.transpose(slots[:, :, 8:], (1, 0, 2, 3)).reshape(2, SHARDS, 1, FF_SHARD)

    owned = [
        jnp.concatenate([w_qkv[0].transpose(1, 2, 0).reshape(QKV, D), w_out[0]], axis=0),
        w_fc1[0],
        w_fc2[0],
    ]
    chunks = [[], []]
    beyond = flip(owned[0], "section", 1)
    for index, own in enumerate(owned):
        if index == 0:
            beyond, ends, cols, bqvs, b1s = tie((beyond, ends, cols, bqvs, b1s))
        arrived = beyond
        if index + 1 < len(owned):
            arrived, following = tie((arrived, owned[index + 1]))
            beyond = flip(following, "section", 1)
        both = [jnp.where(section == 0, own, arrived), jnp.where(section == 0, arrived, own)]
        halves = [lax.dynamic_slice_in_dim(w, zhalf * HALF, HALF, axis=0) for w in both]
        near = flip(halves[0], "tensor", 2)
        near, halves[1] = tie((near, halves[1]))
        near_late = flip(halves[1], "tensor", 2)
        far = flip(near, "dp", 1)
        far, near_late = tie((far, near_late))
        far_late = flip(near_late, "dp", 1)
        for layer, (w, n, f) in enumerate(((both[0], near, far), (both[1], near_late, far_late))):
            chunks[layer].append(
                (w, flip(w, "tensor", 1), n, f, flip(n, "tensor", 1), flip(f, "tensor", 1))
            )

    stream = ends[0]
    stored = []
    for layer in range(2):
        chunk_a, chunk_one, chunk_two = chunks[layer]
        a1, p, soft, o, h = attention_forward(info, stream, cols[layer], bqvs[layer], chunk_a)
        a2, u, slope, y = mlp_forward(info, h, cols[layer], b1s[layer], chunk_one, chunk_two)
        stored.append((stream, a1, p, soft, o, h, a2, u, slope))
        stream = y

    upstream = ends[1]
    chains = [[Chain(layer) for _ in range(3)] for layer in range(2)]
    smalls = [None, None]
    for layer in (1, 0):
        chunk_a, chunk_one, chunk_two = chunks[layer]
        x, a1, p, soft, o, h, a2, u, slope = stored[layer]
        chain_a, chain_one, chain_two = chains[layer]
        late_a, late_one, late_two = chains[1]
        after, send_one, send_two, db1_sent = mlp_backward(
            info, upstream, h, a2, cols[layer], u, slope, None, chunk_one, chunk_two
        )
        chain_two.start(send_two)
        chain_one.start(send_one)
        gh, dcol_two, keep_one, keep_two, db1_kept = mlp_backward(
            info, upstream, h, a2, cols[layer], u, slope, after, chunk_one, chunk_two
        )
        chain_two.fold_cores(keep_two)
        chain_one.fold_cores(keep_one)
        if layer == 1:
            gh, chain_two.away, chain_one.away = tie((gh, chain_two.away, chain_one.away))
            chain_two.send_y()
        else:
            late_one.fold()
            late_two.fold()
            gh, late_one.total, late_two.total, late_a.away, chain_two.away, chain_one.away = tie(
                (gh, late_one.total, late_two.total, late_a.away, chain_two.away, chain_one.away)
            )
            late_one.send_x()
            late_two.send_z(0)
            late_a.send_y()
        after, send_a, dbqv_sent = attention_backward(
            info, gh, x, a1, cols[layer], p, soft, o, None, chunk_a
        )
        chain_a.start(send_a)
        upstream, dcol_one, keep_a, dbqv_kept = attention_backward(
            info, gh, x, a1, cols[layer], p, soft, o, after, chunk_a
        )
        chain_a.fold_cores(keep_a)
        if layer == 1:
            late_two.fold()
            upstream, late_two.total, late_one.away = tie((upstream, late_two.total, late_one.away))
            late_two.send_x()
            late_one.send_y()
        db1 = by_bits([db1_kept[1], db1_sent[1], db1_kept[0], db1_sent[0]], shard)
        dbqv = by_bits([dbqv_kept[1], dbqv_sent[1], dbqv_kept[0], dbqv_sent[0]], shard)
        dcol = jnp.stack(
            [
                dcol_one[:, 0], dcol_two[:, 0], dcol_one[:, 1], dcol_two[:, 1],
                dbqv[:, :, 0].reshape(D), dbqv[:, :, 1].reshape(D), dcol_two[:, 2], dcol_two[:, 3],
            ]
        )
        smalls[layer] = jnp.concatenate(
            [
                dcol.reshape(8, SHARDS, FEATS).transpose(1, 0, 2),
                db1.reshape(SHARDS, SHARDS, FEATS),
            ],
            axis=1,
        )

    result = jnp.stack([upstream.astype(BF16), stream.astype(BF16)])
    result = result.reshape(2 * SHARDS, FEATS, FRAMES)
    result = lax.all_to_all(result, ("section", "tensor"), split_axis=0, concat_axis=0, tiled=True)
    result = result.transpose(1, 0, 2).reshape(FEATS, clips * FRAMES).T.astype(F32)

    small_sum = sum_all(jnp.stack(smalls))
    small_sum = lax.dynamic_slice(
        small_sum, (section, shard, 0, 0), (1, 1, 12, FEATS)
    ).reshape(12, FEATS)

    (late_a, late_one, late_two), (last_a, last_one, last_two) = chains[1], chains[0]
    late_a.fold()
    late_one.fold()
    late_two.fold()
    late_a.total, late_one.total, late_two.total, last_two.away = tie(
        (late_a.total, late_one.total, late_two.total, last_two.away)
    )
    late_a.send_x()
    late_one.send_z(0)
    late_two.send_z(1)
    last_two.send_y()
    late_a.fold()
    late_one.fold()
    late_two.fold()
    last_two.fold()
    late_a.total, late_one.total, late_two.total, last_two.total, last_one.away = tie(
        (late_a.total, late_one.total, late_two.total, last_two.total, last_one.away)
    )
    late_a.send_z(0)
    late_one.send_z(1)
    late_two.send_z(2)
    last_two.send_x()
    last_one.send_y()
    late_a.fold()
    late_one.fold()
    late_two.close()
    last_two.fold()
    last_one.fold()
    late_a.total, late_one.total, last_two.total, last_one.total, last_a.away = tie(
        (late_a.total, late_one.total, last_two.total, last_one.total, last_a.away)
    )
    late_a.send_z(1)
    late_one.send_z(2)
    last_two.send_z(0)
    last_one.send_x()
    last_a.send_y()
    late_a.fold()
    late_one.close()
    late_a.send_z(2)
    late_a.close()
    for chain in (last_two, last_one, last_a):
        chain.fold()
    last_two.send_z(1)
    last_one.send_z(0)
    last_a.send_x()
    for chain in (last_two, last_one, last_a):
        chain.fold()
    last_two.send_z(2)
    last_two.close()
    last_one.send_z(1)
    last_a.send_z(0)
    last_one.fold()
    last_a.fold()
    last_one.send_z(2)
    last_a.send_z(1)
    last_one.close()
    last_a.fold()
    last_a.send_z(2)
    last_a.close()

    grad_a, grad_one, grad_two = [
        jnp.where(section == 0, first.total, second.total).astype(F32)
        for first, second in zip(chains[0], chains[1])
    ]
    return (
        result[None],
        small_sum[None, 0:2],
        small_sum[None, 2:4],
        grad_a[:QKV].reshape(3, FEATS, D).transpose(2, 0, 1)[None],
        small_sum[None, 4:6],
        grad_a[QKV:][None],
        small_sum[6:7],
        grad_one[None],
        small_sum[8:12].reshape(1, FF_SHARD),
        grad_two[None],
        small_sum[7:8],
    )


def solution(mesh):
    placed = (
        P("section", "dp", "tensor"),
        P("section", None, "tensor"),
        P("section", None, "tensor"),
        P("section", None, None, "tensor"),
        P("section", None, "tensor"),
        P("section", "tensor", None),
        P("section", "tensor"),
        P("section", None, "tensor"),
        P("section", "tensor"),
        P("section", "tensor", None),
        P("section", "tensor"),
    )
    return jax.shard_map(
        body, mesh=mesh, in_specs=placed, out_specs=placed, check_vma=False
    )
```

```python
import functools

import jax
import jax.numpy as jnp
from jax import lax
from jax.experimental import pallas as pl
from jax.experimental.pallas import tpu as pltpu
from jax.sharding import PartitionSpec as P

D = 768
HD = 64
FRAMES = 448
SHARDS = 4
HEADS_SHARD = 3
FEATS = HEADS_SHARD * HD
QKV = 3 * FEATS
FF_SHARD = 768
HALF = D // 2
EPSILON = 1e-05
SCALE = float(HD) ** (-0.5)
VMEM_LIMIT = 48 * 1024 * 1024
GAIN1, GAIN2, SHIFT1, SHIFT2, BIAS_Q, BIAS_V, BIAS_OUT, BIAS_FC2 = range(8)
BACK_ORDER = (3, 1, 2, 0)
F32 = jnp.float32
BF16 = jnp.bfloat16


def matmul(left, right, left_dim=1, right_dim=0):
    return lax.dot_general(
        left, right, (((left_dim,), (right_dim,)), ((), ())), preferred_element_type=F32
    )


def normalize(values):
    center = jnp.mean(values, axis=0, keepdims=True)
    moved = values - center
    inv_std = lax.rsqrt(jnp.mean(moved * moved, axis=0, keepdims=True) + EPSILON)
    return moved * inv_std, inv_std


def norm_backward(upstream, normed, inv_std, gain):
    scaled = upstream * gain
    mean_one = jnp.mean(scaled, axis=0, keepdims=True)
    mean_two = jnp.mean(scaled * normed, axis=0, keepdims=True)
    return inv_std * (scaled - mean_one - normed * mean_two)


def row_sums(values):
    return jnp.sum(values, axis=1, keepdims=True)


def columns(parts, lanes):
    lane = lax.broadcasted_iota(jnp.int32, (parts[0].shape[0], lanes), 1)
    total = jnp.zeros((parts[0].shape[0], lanes), F32)
    for index, part in enumerate(parts):
        total = jnp.where(lane == index, part, total)
    return total


def piece_copies(info, pieces, held, sems):
    first = pl.multiple_of(info[4] * HALF, HALF)
    second = pl.multiple_of((1 - info[4]) * HALF, HALF)
    return tuple(
        tuple(
            pltpu.make_async_copy(
                pieces[2 * slot + part], held.at[slot, pl.ds(start, HALF)], sems.at[2 * slot + part]
            )
            for part, start in enumerate((first, second))
        )
        for slot in range(SHARDS)
    )


def load_pieces(step, order, chunks):
    @pl.when(step == 0)
    def start():
        for slot in order:
            for chunk in chunks:
                for copy in chunk[slot]:
                    copy.start()

    for index, slot in enumerate(order):

        @pl.when(step == index)
        def wait():
            for chunk in chunks:
                for copy in chunk[slot]:
                    copy.wait()


def attention_forward_kernel(
    info, x_ref, col_ref, bqv_ref, *refs
):
    step = pl.program_id(0)
    pieces, (a1_ref, p_ref, soft_ref, o_ref, h_ref, held, sems) = refs[:8], refs[8:]
    copies = piece_copies(info, pieces, held, sems)
    load_pieces(step, range(SHARDS), (copies,))

    @pl.when(step == 0)
    def first():
        col = col_ref[...].reshape(D, 8)
        values = x_ref[...].astype(F32)
        normed, _ = normalize(values)
        a1_ref[...] = (
            normed * col[:, GAIN1 : GAIN1 + 1] + col[:, SHIFT1 : SHIFT1 + 1]
        ).astype(BF16)
        h_ref[...] = values + col[:, BIAS_OUT : BIAS_OUT + 1]

    bias = bqv_ref[step]
    projected = matmul(held[step, :QKV], a1_ref[...])
    queries = (projected[:FEATS] + bias[:, 0:1]).astype(BF16)
    keys = projected[FEATS : 2 * FEATS].astype(BF16)
    values = (projected[2 * FEATS :] + bias[:, 1:2]).astype(BF16)
    p_ref[0, :FEATS] = queries
    p_ref[0, FEATS : 2 * FEATS] = keys
    p_ref[0, 2 * FEATS :] = values
    scaled = queries * SCALE
    for head in range(HEADS_SHARD):
        rows = slice(head * HD, (head + 1) * HD)
        scores = matmul(keys[rows], scaled[rows], 0, 0)
        exps = jnp.exp(scores - jnp.max(scores, axis=0, keepdims=True))
        soft = exps * (1.0 / jnp.sum(exps, axis=0, keepdims=True))
        soft = soft.astype(BF16)
        soft_ref[0, head] = soft
        o_ref[0, rows] = matmul(values[rows], soft).astype(BF16)
    h_ref[...] += matmul(held[step, QKV:], o_ref[0], 0, 0)


def mlp_forward_kernel(
    info, h_ref, col_ref, b1_ref, *refs
):
    step = pl.program_id(0)
    pieces_one, pieces_two, refs = refs[:8], refs[8:16], refs[16:]
    a2_ref, u_ref, slope_ref, y_ref, held_one, held_two, a2_rows, total, sems_one, sems_two = refs
    copies_one = piece_copies(info, pieces_one, held_one, sems_one)
    copies_two = piece_copies(info, pieces_two, held_two, sems_two)
    load_pieces(step, range(SHARDS), (copies_one, copies_two))

    @pl.when(step == 0)
    def first():
        col = col_ref[...].reshape(D, 8)
        normed, _ = normalize(h_ref[...])
        scaled = normed * col[:, GAIN2 : GAIN2 + 1] + col[:, SHIFT2 : SHIFT2 + 1]
        a2_ref[...] = scaled.astype(BF16)
        a2_rows[...] = scaled.T.astype(BF16)
        total[...] = jnp.zeros_like(total)

    inner = matmul(a2_rows[...], held_one[step]) + b1_ref[step]
    phi = 0.5 + 0.5 * lax.erf(inner * 0.7071067811865476)
    density = 0.3989422804014327 * jnp.exp(-0.5 * inner * inner)
    active = (inner * phi).astype(BF16)
    u_ref[0] = active
    slope_ref[0] = (phi + inner * density).astype(BF16)
    total[...] += matmul(active, held_two[step])

    @pl.when(step == SHARDS - 1)
    def last():
        col = col_ref[...].reshape(D, 8)
        y_ref[...] = h_ref[...] + total[...].T + col[:, BIAS_FC2 : BIAS_FC2 + 1]


def mlp_backward_kernel(
    last, info, gy_ref, h_ref, a2_ref, col_ref, u_ref, slope_ref, *refs
):
    step = pl.program_id(0)
    if last:
        before_ref, *refs = refs
    pieces_one, pieces_two, refs = refs[:8], refs[8:16], refs[16:]
    if last:
        gh_ref, dcol_ref, *refs = refs
    else:
        after_ref, *refs = refs
    grad_one, grad_two, db1_ref, held_one, held_two, gy_rows, total, sems_one, sems_two = refs
    copies_one = piece_copies(info, pieces_one, held_one, sems_one)
    copies_two = piece_copies(info, pieces_two, held_two, sems_two)
    load_pieces(step, BACK_ORDER[2:] if last else BACK_ORDER[:2], (copies_two, copies_one))

    @pl.when(step == 0)
    def first():
        gy_rows[...] = gy_ref[...].astype(F32).T.astype(BF16)
        total[...] = before_ref[...] if last else jnp.zeros_like(total)

    slot = info[(7 if last else 5) + step]
    d_active = matmul(gy_rows[...], held_two[slot], 1, 1)
    d_inner = d_active * slope_ref[0].astype(F32)
    rounded = d_inner.astype(BF16)
    db1_ref[step] = jnp.sum(rounded.astype(F32), axis=0, keepdims=True)
    grad_two[0] = matmul(u_ref[0], gy_rows[...], 0, 0).astype(BF16)
    grad_one[0] = matmul(a2_ref[...], rounded).astype(BF16)
    total[...] += matmul(rounded, held_one[slot], 1, 1)

    @pl.when(step == 1)
    def end():
        if not last:
            after_ref[...] = total[...]
            return
        col = col_ref[...].reshape(D, 8)
        normed, inv_std = normalize(h_ref[...])
        d_mid = total[...].T
        upstream = gy_ref[...].astype(F32)
        d_hidden = upstream + norm_backward(d_mid, normed, inv_std, col[:, GAIN2 : GAIN2 + 1])
        gh_ref[...] = d_hidden
        dcol_ref[...] = columns(
            [row_sums(d_mid * normed), row_sums(d_mid), row_sums(d_hidden), row_sums(upstream)], 8
        )


def attention_backward_kernel(
    last, info, gh_ref, x_ref, a1_ref, col_ref, p_ref, soft_ref, o_ref, *refs
):
    step = pl.program_id(0)
    if last:
        before_ref, *refs = refs
    pieces, refs = refs[:8], refs[8:]
    if last:
        gx_ref, dcol_ref, *refs = refs
    else:
        after_ref, *refs = refs
    grad_ref, dbqv_ref, held, gh_rounded, g_p, total, sems = refs
    copies = piece_copies(info, pieces, held, sems)
    load_pieces(step, BACK_ORDER[2:] if last else BACK_ORDER[:2], (copies,))

    @pl.when(step == 0)
    def first():
        gh_rounded[...] = gh_ref[...].astype(BF16)
        total[...] = before_ref[...] if last else jnp.zeros_like(total)

    slot = info[(7 if last else 5) + step]
    d_attended = matmul(held[slot, QKV:], gh_rounded[...]).astype(BF16)
    grad_ref[0, QKV:] = matmul(o_ref[0], gh_rounded[...], 1, 1).astype(BF16)
    for head in range(HEADS_SHARD):
        rows = slice(head * HD, (head + 1) * HD)
        queries = p_ref[0, rows]
        keys = p_ref[0, FEATS + head * HD : FEATS + (head + 1) * HD]
        values = p_ref[0, 2 * FEATS + head * HD : 2 * FEATS + (head + 1) * HD]
        soft = soft_ref[0, head]
        d_att = d_attended[rows]
        delta = jnp.sum(
            d_att.astype(F32) * o_ref[0, rows].astype(F32), axis=0, keepdims=True
        )
        d_soft = matmul(values, d_att, 0, 0)
        d_scores = (soft.astype(F32) * (d_soft - delta)).astype(BF16)
        g_p[rows] = (matmul(keys, d_scores) * SCALE).astype(BF16)
        g_p[FEATS + head * HD : FEATS + (head + 1) * HD] = (
            matmul(queries, d_scores, 1, 1) * SCALE
        ).astype(BF16)
        g_p[2 * FEATS + head * HD : 2 * FEATS + (head + 1) * HD] = matmul(
            d_att, soft, 1, 1
        ).astype(BF16)
    d_projected = g_p[...]
    grad_ref[0, :QKV] = matmul(d_projected, a1_ref[...], 1, 1).astype(BF16)
    total[...] += matmul(d_projected, held[slot, :QKV], 0, 0)
    dbqv_ref[step] = columns(
        [row_sums(d_projected[:FEATS].astype(F32)), row_sums(d_projected[2 * FEATS :].astype(F32))],
        8,
    )

    @pl.when(step == 1)
    def end():
        if not last:
            after_ref[...] = total[...]
            return
        col = col_ref[...].reshape(D, 8)
        normed, inv_std = normalize(x_ref[...].astype(F32))
        d_first = total[...].T
        gx_ref[...] = gh_ref[...] + norm_backward(
            d_first, normed, inv_std, col[:, GAIN1 : GAIN1 + 1]
        )
        dcol_ref[...] = columns([row_sums(d_first * normed), row_sums(d_first)], 8)


def whole(shape):
    return pl.BlockSpec(shape, lambda i, info: (0,) * len(shape))


def by_step(shape):
    return pl.BlockSpec((1,) + shape, lambda i, info: (i,) + (0,) * len(shape))


def by_slot(shape, last):
    first = 7 if last else 5
    return pl.BlockSpec((1,) + shape, lambda i, info: (info[first + i],) + (0,) * len(shape))


PIECES = [pl.BlockSpec(memory_space=pltpu.HBM)] * 8
COPY_SEMS = pltpu.SemaphoreType.DMA((8,))
HELD = pltpu.VMEM((SHARDS, D, D), BF16)


def of(shape, dtype=BF16):
    return jax.ShapeDtypeStruct(shape, dtype)


def run(kernel, name, steps, info, operands, in_specs, outs, out_specs, scratch, flops):
    moved = sum(a.size * a.dtype.itemsize for a in operands) + sum(
        a.size * a.dtype.itemsize for a in outs
    )
    return pl.pallas_call(
        kernel,
        name=name,
        out_shape=outs,
        grid_spec=pltpu.PrefetchScalarGridSpec(
            num_scalar_prefetch=1,
            grid=(steps,),
            in_specs=in_specs,
            out_specs=out_specs,
            scratch_shapes=scratch,
        ),
        compiler_params=pltpu.CompilerParams(
            vmem_limit_bytes=VMEM_LIMIT, dimension_semantics=("arbitrary",)
        ),
        cost_estimate=pl.CostEstimate(flops=flops, bytes_accessed=moved, transcendentals=0),
    )(info, *operands)


STREAM = (D, FRAMES)
ROWS = (FRAMES, D)
COLS = (SHARDS, FEATS, 8)
ATT_FLOPS = 2 * FRAMES * D * (4 * D + 2 * FRAMES)
MLP_FLOPS = 4 * FRAMES * D * SHARDS * FF_SHARD


def attention_forward(info, x, col, bqv, chunk):
    return run(
        attention_forward_kernel, "attention_forward", SHARDS, info, (x, col, bqv, *chunk),
        [whole(STREAM), whole(COLS), whole((SHARDS, FEATS, 2))] + PIECES,
        [
            of(STREAM), of((SHARDS, QKV, FRAMES)), of((SHARDS, HEADS_SHARD, FRAMES, FRAMES)),
            of((SHARDS, FEATS, FRAMES)), of(STREAM, F32),
        ],
        [
            whole(STREAM), by_step((QKV, FRAMES)), by_step((HEADS_SHARD, FRAMES, FRAMES)),
            by_step((FEATS, FRAMES)), whole(STREAM),
        ],
        [HELD, COPY_SEMS],
        ATT_FLOPS,
    )


def mlp_forward(info, h, col, b1, chunk_one, chunk_two):
    return run(
        mlp_forward_kernel, "mlp_forward", SHARDS, info, (h, col, b1, *chunk_one, *chunk_two),
        [whole(STREAM), whole(COLS), whole((SHARDS, 1, FF_SHARD))] + PIECES * 2,
        [of(STREAM), of((SHARDS, FRAMES, FF_SHARD)), of((SHARDS, FRAMES, FF_SHARD)), of(STREAM, F32)],
        [whole(STREAM), by_step((FRAMES, FF_SHARD)), by_step((FRAMES, FF_SHARD)), whole(STREAM)],
        [HELD, HELD, pltpu.VMEM(ROWS, BF16), pltpu.VMEM(ROWS, F32), COPY_SEMS, COPY_SEMS],
        MLP_FLOPS,
    )


def mlp_backward(info, gy, h, a2, col, u, slope, before, chunk_one, chunk_two):
    last = before is not None
    carried = (before,) if last else ()
    ends = [of(STREAM, F32), of((D, 8), F32)] if last else [of(ROWS, F32)]
    return run(
        functools.partial(mlp_backward_kernel, last), "mlp_backward", 2, info,
        (gy, h, a2, col, u, slope, *carried, *chunk_one, *chunk_two),
        [
            whole(STREAM), whole(STREAM), whole(STREAM), whole(COLS),
            by_slot((FRAMES, FF_SHARD), last), by_slot((FRAMES, FF_SHARD), last),
        ]
        + [whole(ROWS)] * len(carried)
        + PIECES * 2,
        ends + [of((2, D, D)), of((2, D, D)), of((2, 1, FF_SHARD), F32)],
        [whole(end.shape) for end in ends]
        + [by_step((D, D)), by_step((D, D)), whole((2, 1, FF_SHARD))],
        [HELD, HELD, pltpu.VMEM(ROWS, BF16), pltpu.VMEM(ROWS, F32), COPY_SEMS, COPY_SEMS],
        MLP_FLOPS,
    )


def attention_backward(info, gh, x, a1, col, p, soft, o, before, chunk):
    last = before is not None
    carried = (before,) if last else ()
    ends = [of(STREAM, F32), of((D, 8), F32)] if last else [of(ROWS, F32)]
    return run(
        functools.partial(attention_backward_kernel, last), "attention_backward", 2, info,
        (gh, x, a1, col, p, soft, o, *carried, *chunk),
        [
            whole(STREAM), whole(STREAM), whole(STREAM), whole(COLS),
            by_slot((QKV, FRAMES), last), by_slot((HEADS_SHARD, FRAMES, FRAMES), last),
            by_slot((FEATS, FRAMES), last),
        ]
        + [whole(ROWS)] * len(carried)
        + PIECES,
        ends + [of((2, D, D)), of((2, FEATS, 8), F32)],
        [whole(end.shape) for end in ends] + [by_step((D, D)), whole((2, FEATS, 8))],
        [HELD, pltpu.VMEM(STREAM, BF16), pltpu.VMEM((QKV, FRAMES), BF16), pltpu.VMEM(ROWS, F32), COPY_SEMS],
        ATT_FLOPS,
    )


def tie(groups):
    return lax.optimization_barrier(groups)


def flip(block, axis, bit):
    size = lax.axis_size(axis)
    return lax.ppermute(block, axis, [(i, i ^ bit) for i in range(size)])


def added(left, right):
    return (left.astype(F32) + right.astype(F32)).astype(BF16)


def by_bits(slots, shard):
    odd = shard % 2 == 1
    high = shard >= 2
    first, second, third, fourth = slots
    first, second = jnp.where(odd, second, first), jnp.where(odd, first, second)
    third, fourth = jnp.where(odd, fourth, third), jnp.where(odd, third, fourth)
    return jnp.stack(
        [
            jnp.where(high, third, first), jnp.where(high, fourth, second),
            jnp.where(high, first, third), jnp.where(high, second, fourth),
        ]
    )


def rows_of(value, place, parts):
    size = value.shape[-2] // parts
    return lax.dynamic_slice_in_dim(value, place * size, size, axis=value.ndim - 2)


def joined(first, second, swap):
    return jnp.where(
        swap, jnp.concatenate([second, first], axis=0), jnp.concatenate([first, second], axis=0)
    )


class Chain:
    def start(self, send):
        self.arrived = flip(send, "tensor", 1)

    def cores(self, keep):
        self.value = added(keep, self.arrived)

    def send_y(self):
        self.kept, self.arrived = self.value[1], flip(self.value[0], "tensor", 2)

    def send_z(self, level):
        mine = (lax.axis_index("dp") >> level) & 1
        self.kept = rows_of(self.value, mine, 2)
        self.arrived = flip(rows_of(self.value, 1 - mine, 2), "dp", 1 << level)

    def send_x(self, first, second):
        section = lax.axis_index("section")
        self.kept = jnp.where(section == 0, first.value, second.value)
        self.arrived = flip(jnp.where(section == 0, second.value, first.value), "section", 1)

    def fold(self):
        self.value = added(self.kept, self.arrived)

    def finish_x(self):
        self.fold()
        bit = 4
        while bit < lax.axis_size("dp"):
            self.value = added(self.value, flip(self.value, "dp", bit))
            bit *= 2

    def gather_z(self, level):
        self.level, self.arrived = level, flip(self.value, "dp", 1 << level)

    def join(self):
        mine = (lax.axis_index("dp") >> self.level) & 1
        self.value = joined(self.value, self.arrived, mine == 1)


def tied(chains, *others):
    values = tie((tuple(chain.value for chain in chains), others))
    for chain, value in zip(chains, values[0]):
        chain.value = value
    return values[1]


def body(ends_in, ln_gain, ln_shift, w_qkv, b_qv, w_out, b_out, w_fc1, b_fc1, w_fc2, b_fc2):
    section = lax.axis_index("section")
    shard = lax.axis_index("tensor")
    zhalf = lax.axis_index("dp") % 2
    clips = ends_in.shape[1] // FRAMES
    info = jnp.stack(
        [shard, shard ^ 1, shard ^ 2, shard ^ 3, zhalf] + [jnp.int32(k) for k in BACK_ORDER]
    ).astype(jnp.int32)

    owned = [
        jnp.concatenate([w_qkv[0].transpose(1, 2, 0).reshape(QKV, D), w_out[0]], axis=0),
        w_fc1[0],
        w_fc2[0],
    ]
    nears = [rows_of(own, zhalf, 2) for own in owned]
    fars = [rows_of(own, 1 - zhalf, 2) for own in owned]
    small = jnp.concatenate(
        [ln_gain[0], ln_shift[0], b_qv[0], b_out, b_fc2, b_fc1.reshape(SHARDS, FEATS)], axis=0
    )
    nears[0], small, ends = tie((nears[0], small, ends_in[0]))
    beyond = flip(nears[0], "section", 1)

    ends = ends.T.reshape(FEATS, clips, FRAMES).transpose(1, 0, 2)
    ends = lax.all_to_all(ends, ("section", "tensor"), split_axis=0, concat_axis=0, tiled=True)
    ends = ends.reshape(2, D, FRAMES)

    small_beyond = flip(small, "section", 1)
    small = jnp.stack(
        [jnp.where(section == 0, small, small_beyond), jnp.where(section == 0, small_beyond, small)]
    )
    small_y = flip(small, "tensor", 2)
    pair = jnp.stack([small, small_y])
    pair_other = flip(pair, "tensor", 1)
    slots = jnp.stack([pair[0], pair_other[0], pair[1], pair_other[1]]).astype(F32)
    cols = jnp.transpose(by_bits(slots[:, :, :8], shard), (1, 0, 3, 2))
    bqvs = jnp.transpose(slots[:, :, 4:6], (1, 0, 3, 2))
    b1s = jnp.transpose(slots[:, :, 8:], (1, 0, 2, 3)).reshape(2, SHARDS, 1, FF_SHARD)

    def layers(own, other):
        return jnp.where(section == 0, own, other), jnp.where(section == 0, other, own)

    near_own, far_own = [], []
    for index in range(2):
        near_other, following = tie((beyond, (nears[1], owned[2])[index]))
        beyond = flip(following, "section", 1)
        near_own.append(layers(nears[index], near_other))
        far_own.append(layers(fars[index], flip(near_other, "dp", 1)))

    def over_y(index, layer):
        return flip(near_own[index][layer], "tensor", 2)

    def chunk_of(index, layer, near_there, far_there):
        here = [near_own[index][layer], far_own[index][layer]]
        there = [near_there, far_there]
        return (
            here
            + [flip(part, "tensor", 1) for part in here]
            + there
            + [flip(part, "tensor", 1) for part in there]
        )

    def attend(layer, stream, chunk):
        return attention_forward(info, stream, cols[layer], bqvs[layer], chunk)

    def feed(layer, h, chunk_one, chunk_two):
        return mlp_forward(info, h, cols[layer], b1s[layer], chunk_one, chunk_two)

    chunks = [[None] * 3, [None] * 3]
    stream = ends[0]
    there_a, there_one = over_y(0, 0), over_y(1, 0)
    chunks[0][0] = chunk_of(0, 0, there_a, flip(there_a, "dp", 1))
    away_one = flip(there_one, "dp", 1)
    a1, p, soft, o, h = attend(0, stream, chunks[0][0])

    h, away_one, beyond, far_one, late_a, late_one = tie(
        (h, away_one, beyond, far_own[1], near_own[0][1], near_own[1][1])
    )
    far_own[1], near_own[0], near_own[1] = far_one, (None, late_a), (near_own[1][0], late_one)
    chunks[0][1] = chunk_of(1, 0, there_one, away_one)
    near_own.append(layers(nears[2], rows_of(beyond, zhalf, 2)))
    far_own.append(layers(fars[2], rows_of(beyond, 1 - zhalf, 2)))
    there_two = over_y(2, 0)
    there_two, late_a = tie((there_two, late_a))
    near_own[0] = (None, late_a)
    chunks[0][2] = chunk_of(2, 0, there_two, flip(there_two, "dp", 1))
    there_a = over_y(0, 1)
    there_a, late_one, late_two = tie((there_a, near_own[1][1], near_own[2][1]))
    near_own[1], near_own[2] = (None, late_one), (None, late_two)
    away_a = flip(there_a, "dp", 1)
    there_one, there_two = over_y(1, 1), over_y(2, 1)
    a2, u, slope, y = feed(0, h, chunks[0][1], chunks[0][2])
    stored = [(stream, a1, p, soft, o, h, a2, u, slope)]

    stream, there_one, there_two, away_a = tie((y, there_one, there_two, away_a))
    chunks[1][0] = chunk_of(0, 1, there_a, away_a)
    chunks[1][1] = chunk_of(1, 1, there_one, flip(there_one, "dp", 1))
    chunks[1][2] = chunk_of(2, 1, there_two, flip(there_two, "dp", 1))
    a1, p, soft, o, h = attend(1, stream, chunks[1][0])
    a2, u, slope, y = feed(1, h, chunks[1][1], chunks[1][2])
    stored.append((stream, a1, p, soft, o, h, a2, u, slope))
    stream = y

    upstream = ends[1]
    chains = [[Chain() for _ in range(3)] for _ in range(2)]
    smalls = [None, None]
    late_a, late_one, late_two = chains[1]
    last_a, last_one, last_two = chains[0]
    for layer in (1, 0):
        chunk_a, chunk_one, chunk_two = chunks[layer]
        x, a1, p, soft, o, h, a2, u, slope = stored[layer]
        chain_a, chain_one, chain_two = chains[layer]
        after, send_one, send_two, db1_sent = mlp_backward(
            info, upstream, h, a2, cols[layer], u, slope, None, chunk_one, chunk_two
        )
        chain_two.start(send_two)
        chain_one.start(send_one)
        gh, dcol_two, keep_one, keep_two, db1_kept = mlp_backward(
            info, upstream, h, a2, cols[layer], u, slope, after, chunk_one, chunk_two
        )
        chain_two.cores(keep_two)
        chain_one.cores(keep_one)
        if layer == 1:
            (gh,) = tied((late_two, late_one), gh)
            late_two.send_y()
            late_one.send_z(0)
        else:
            late_one.fold()
            late_a.fold()
            (gh,) = tied((late_one, late_a, last_two, last_one, late_two), gh)
            last_two.send_y()
            late_two.send_z(0)
            late_one.send_z(1)
        after, send_a, dbqv_sent = attention_backward(
            info, gh, x, a1, cols[layer], p, soft, o, None, chunk_a
        )
        chain_a.start(send_a)
        upstream, dcol_one, keep_a, dbqv_kept = attention_backward(
            info, gh, x, a1, cols[layer], p, soft, o, after, chunk_a
        )
        chain_a.cores(keep_a)
        if layer == 1:
            late_two.fold()
            late_one.fold()
            (upstream,) = tied((late_two, late_one, late_a), upstream)
            late_one.send_y()
            late_a.send_z(0)
        db1 = by_bits([db1_kept[1], db1_sent[1], db1_kept[0], db1_sent[0]], shard)
        dbqv = by_bits([dbqv_kept[1], dbqv_sent[1], dbqv_kept[0], dbqv_sent[0]], shard)
        dcol = jnp.concatenate(
            [
                dcol_one[:, 0:1], dcol_two[:, 0:1], dcol_one[:, 1:2], dcol_two[:, 1:2],
                dbqv[:, :, 0:2].reshape(D, 2), dcol_two[:, 2:4],
            ],
            axis=1,
        )
        smalls[layer] = jnp.concatenate(
            [
                dcol.reshape(SHARDS, FEATS, 8).transpose(0, 2, 1),
                db1.reshape(SHARDS, SHARDS, FEATS),
            ],
            axis=1,
        )

    result = jnp.stack([upstream.astype(BF16), stream.astype(BF16)])
    result = result.reshape(2 * SHARDS, FEATS, FRAMES)
    small_sum = jnp.stack(smalls)

    late_two.fold()
    late_one.fold()
    last_two.fold()
    tied((late_two, late_one, last_two, last_one))
    last_one.send_y()
    last_two.send_z(0)
    late_two.send_z(1)
    result = lax.all_to_all(result, ("section", "tensor"), split_axis=0, concat_axis=0, tiled=True)
    small_sum += flip(small_sum, "tensor", 1)

    last_two.fold()
    late_two.fold()
    result, small_sum = tied((last_two, late_two), result, small_sum)
    last_two.send_z(1)
    small_sum += flip(small_sum, "tensor", 2)
    result = result.transpose(1, 0, 2).reshape(FEATS, clips * FRAMES).T.astype(F32)

    last_one.fold()
    last_two.fold()
    result, small_sum = tied((last_one, last_two, last_a, late_a), result, small_sum)
    last_a.send_y()
    late_a.send_y()
    last_one.send_z(0)
    pair_two = Chain()
    pair_two.send_x(last_two, late_two)
    small_sum += flip(small_sum, "section", 1)

    last_one.fold()
    pair_two.finish_x()
    (small_sum,) = tied((last_one, pair_two), small_sum)
    last_one.send_z(1)
    pair_two.gather_z(1)
    small_sum += flip(small_sum, "dp", 1)

    last_one.fold()
    pair_two.join()
    last_a.fold()
    late_a.fold()
    (small_sum,) = tied((last_one, pair_two, last_a, late_a), small_sum)
    pair_one = Chain()
    pair_one.send_x(last_one, late_one)
    last_a.send_z(0)
    late_a.send_z(1)
    pair_two.gather_z(0)
    bit = 2
    while bit < lax.axis_size("dp"):
        small_sum += flip(small_sum, "dp", bit)
        bit *= 2

    pair_one.finish_x()
    last_a.fold()
    late_a.fold()
    (small_sum,) = tied((pair_one, last_a, late_a), small_sum)
    pair_one.gather_z(1)
    last_a.send_z(1)
    small_sum = lax.dynamic_slice(
        small_sum, (section, shard, 0, 0), (1, 1, 12, FEATS)
    ).reshape(12, FEATS)

    pair_one.join()
    last_a.fold()
    pair_two.join()
    tied((pair_one, last_a))
    pair_a = Chain()
    pair_a.send_x(last_a, late_a)
    pair_one.gather_z(0)
    pair_a.finish_x()
    pair_a.gather_z(1)
    pair_one.join()
    pair_a.join()
    pair_a.gather_z(0)
    pair_a.join()

    grad_a, grad_one, grad_two = [pair.value.astype(F32) for pair in (pair_a, pair_one, pair_two)]
    return (
        result[None],
        small_sum[None, 0:2],
        small_sum[None, 2:4],
        grad_a[:QKV].reshape(3, FEATS, D).transpose(2, 0, 1)[None],
        small_sum[None, 4:6],
        grad_a[QKV:][None],
        small_sum[6:7],
        grad_one[None],
        small_sum[8:12].reshape(1, FF_SHARD),
        grad_two[None],
        small_sum[7:8],
    )


def solution(mesh):
    placed = (
        P("section", "dp", "tensor"),
        P("section", None, "tensor"),
        P("section", None, "tensor"),
        P("section", None, None, "tensor"),
        P("section", None, "tensor"),
        P("section", "tensor", None),
        P("section", "tensor"),
        P("section", None, "tensor"),
        P("section", "tensor"),
        P("section", "tensor", None),
        P("section", "tensor"),
    )
    return jax.shard_map(
        body, mesh=mesh, in_specs=placed, out_specs=placed, check_vma=False
    )
```

```python
import functools

import jax
import jax.numpy as jnp
from jax import lax
from jax.experimental import pallas as pl
from jax.experimental.pallas import tpu as pltpu
from jax.sharding import PartitionSpec as P

D = 768
HD = 64
FRAMES = 448
SHARDS = 4
HEADS_SHARD = 3
FEATS = HEADS_SHARD * HD
QKV = 3 * FEATS
FF_SHARD = 768
HALF = D // 2
EPSILON = 1e-05
SCALE = float(HD) ** (-0.5)
VMEM_LIMIT = 48 * 1024 * 1024
GAIN1, GAIN2, SHIFT1, SHIFT2, BIAS_Q, BIAS_V, BIAS_OUT, BIAS_FC2 = range(8)
BACK_ORDER = (3, 1, 2, 0)
F32 = jnp.float32
BF16 = jnp.bfloat16


def matmul(left, right, left_dim=1, right_dim=0):
    return lax.dot_general(
        left, right, (((left_dim,), (right_dim,)), ((), ())), preferred_element_type=F32
    )


def normalize(values):
    center = jnp.mean(values, axis=0, keepdims=True)
    moved = values - center
    inv_std = lax.rsqrt(jnp.mean(moved * moved, axis=0, keepdims=True) + EPSILON)
    return moved * inv_std, inv_std


def norm_backward(upstream, normed, inv_std, gain):
    scaled = upstream * gain
    mean_one = jnp.mean(scaled, axis=0, keepdims=True)
    mean_two = jnp.mean(scaled * normed, axis=0, keepdims=True)
    return inv_std * (scaled - mean_one - normed * mean_two)


def row_sums(values):
    return jnp.sum(values, axis=1, keepdims=True)


def columns(parts, lanes):
    lane = lax.broadcasted_iota(jnp.int32, (parts[0].shape[0], lanes), 1)
    total = jnp.zeros((parts[0].shape[0], lanes), F32)
    for index, part in enumerate(parts):
        total = jnp.where(lane == index, part, total)
    return total


def piece_copies(info, pieces, held, sems):
    first = pl.multiple_of(info[4] * HALF, HALF)
    second = pl.multiple_of((1 - info[4]) * HALF, HALF)
    return tuple(
        tuple(
            pltpu.make_async_copy(
                pieces[2 * slot + part], held.at[slot, pl.ds(start, HALF)], sems.at[2 * slot + part]
            )
            for part, start in enumerate((first, second))
        )
        for slot in range(SHARDS)
    )


def load_pieces(step, order, chunks):
    @pl.when(step == 0)
    def start():
        for slot in order:
            for chunk in chunks:
                for copy in chunk[slot]:
                    copy.start()

    for index, slot in enumerate(order):

        @pl.when(step == index)
        def wait():
            for chunk in chunks:
                for copy in chunk[slot]:
                    copy.wait()


def attention_forward_kernel(
    info, x_ref, col_ref, bqv_ref, *refs
):
    step = pl.program_id(0)
    pieces, (a1_ref, p_ref, soft_ref, o_ref, h_ref, held, sems) = refs[:8], refs[8:]
    copies = piece_copies(info, pieces, held, sems)
    load_pieces(step, range(SHARDS), (copies,))

    @pl.when(step == 0)
    def first():
        col = col_ref[...].reshape(D, 8)
        values = x_ref[...].astype(F32)
        normed, _ = normalize(values)
        a1_ref[...] = (
            normed * col[:, GAIN1 : GAIN1 + 1] + col[:, SHIFT1 : SHIFT1 + 1]
        ).astype(BF16)
        h_ref[...] = values + col[:, BIAS_OUT : BIAS_OUT + 1]

    bias = bqv_ref[step]
    projected = matmul(held[step, :QKV], a1_ref[...])
    queries = (projected[:FEATS] + bias[:, 0:1]).astype(BF16)
    keys = projected[FEATS : 2 * FEATS].astype(BF16)
    values = (projected[2 * FEATS :] + bias[:, 1:2]).astype(BF16)
    p_ref[0, :FEATS] = queries
    p_ref[0, FEATS : 2 * FEATS] = keys
    p_ref[0, 2 * FEATS :] = values
    scaled = queries * SCALE
    for head in range(HEADS_SHARD):
        rows = slice(head * HD, (head + 1) * HD)
        scores = matmul(keys[rows], scaled[rows], 0, 0)
        exps = jnp.exp(scores - jnp.max(scores, axis=0, keepdims=True))
        soft = exps * (1.0 / jnp.sum(exps, axis=0, keepdims=True))
        soft = soft.astype(BF16)
        soft_ref[0, head] = soft
        o_ref[0, rows] = matmul(values[rows], soft).astype(BF16)
    h_ref[...] += matmul(held[step, QKV:], o_ref[0], 0, 0)


def mlp_forward_kernel(
    info, h_ref, col_ref, b1_ref, *refs
):
    step = pl.program_id(0)
    pieces_one, pieces_two, refs = refs[:8], refs[8:16], refs[16:]
    a2_ref, u_ref, slope_ref, y_ref, held_one, held_two, a2_rows, total, sems_one, sems_two = refs
    copies_one = piece_copies(info, pieces_one, held_one, sems_one)
    copies_two = piece_copies(info, pieces_two, held_two, sems_two)
    load_pieces(step, range(SHARDS), (copies_one, copies_two))

    @pl.when(step == 0)
    def first():
        col = col_ref[...].reshape(D, 8)
        normed, _ = normalize(h_ref[...])
        scaled = normed * col[:, GAIN2 : GAIN2 + 1] + col[:, SHIFT2 : SHIFT2 + 1]
        a2_ref[...] = scaled.astype(BF16)
        a2_rows[...] = scaled.T.astype(BF16)
        total[...] = jnp.zeros_like(total)

    inner = matmul(a2_rows[...], held_one[step]) + b1_ref[step]
    phi = 0.5 + 0.5 * lax.erf(inner * 0.7071067811865476)
    density = 0.3989422804014327 * jnp.exp(-0.5 * inner * inner)
    active = (inner * phi).astype(BF16)
    u_ref[0] = active
    slope_ref[0] = (phi + inner * density).astype(BF16)
    total[...] += matmul(active, held_two[step])

    @pl.when(step == SHARDS - 1)
    def last():
        col = col_ref[...].reshape(D, 8)
        y_ref[...] = h_ref[...] + total[...].T + col[:, BIAS_FC2 : BIAS_FC2 + 1]


def mlp_backward_kernel(
    last, info, gy_ref, h_ref, a2_ref, col_ref, u_ref, slope_ref, *refs
):
    step = pl.program_id(0)
    if last:
        before_ref, *refs = refs
    pieces_one, pieces_two, refs = refs[:8], refs[8:16], refs[16:]
    if last:
        gh_ref, dcol_ref, *refs = refs
    else:
        after_ref, *refs = refs
    grad_one, grad_two, db1_ref, held_one, held_two, gy_rows, total, sems_one, sems_two = refs
    copies_one = piece_copies(info, pieces_one, held_one, sems_one)
    copies_two = piece_copies(info, pieces_two, held_two, sems_two)
    load_pieces(step, BACK_ORDER[2:] if last else BACK_ORDER[:2], (copies_two, copies_one))

    @pl.when(step == 0)
    def first():
        gy_rows[...] = gy_ref[...].astype(F32).T.astype(BF16)
        total[...] = before_ref[...] if last else jnp.zeros_like(total)

    slot = info[(7 if last else 5) + step]
    d_active = matmul(gy_rows[...], held_two[slot], 1, 1)
    d_inner = d_active * slope_ref[0].astype(F32)
    rounded = d_inner.astype(BF16)
    db1_ref[step] = jnp.sum(rounded.astype(F32), axis=0, keepdims=True)
    grad_two[0] = matmul(u_ref[0], gy_rows[...], 0, 0).astype(BF16)
    grad_one[0] = matmul(a2_ref[...], rounded).astype(BF16)
    total[...] += matmul(rounded, held_one[slot], 1, 1)

    @pl.when(step == 1)
    def end():
        if not last:
            after_ref[...] = total[...]
            return
        col = col_ref[...].reshape(D, 8)
        normed, inv_std = normalize(h_ref[...])
        d_mid = total[...].T
        upstream = gy_ref[...].astype(F32)
        d_hidden = upstream + norm_backward(d_mid, normed, inv_std, col[:, GAIN2 : GAIN2 + 1])
        gh_ref[...] = d_hidden
        dcol_ref[...] = columns(
            [row_sums(d_mid * normed), row_sums(d_mid), row_sums(d_hidden), row_sums(upstream)], 8
        )


def attention_backward_kernel(
    last, info, gh_ref, x_ref, a1_ref, col_ref, p_ref, soft_ref, o_ref, *refs
):
    step = pl.program_id(0)
    if last:
        before_ref, *refs = refs
    pieces, refs = refs[:8], refs[8:]
    if last:
        gx_ref, dcol_ref, *refs = refs
    else:
        after_ref, *refs = refs
    grad_ref, dbqv_ref, held, gh_rounded, g_p, total, sems = refs
    copies = piece_copies(info, pieces, held, sems)
    load_pieces(step, BACK_ORDER[2:] if last else BACK_ORDER[:2], (copies,))

    @pl.when(step == 0)
    def first():
        gh_rounded[...] = gh_ref[...].astype(BF16)
        total[...] = before_ref[...] if last else jnp.zeros_like(total)

    slot = info[(7 if last else 5) + step]
    d_attended = matmul(held[slot, QKV:], gh_rounded[...]).astype(BF16)
    grad_ref[0, QKV:] = matmul(o_ref[0], gh_rounded[...], 1, 1).astype(BF16)
    for head in range(HEADS_SHARD):
        rows = slice(head * HD, (head + 1) * HD)
        queries = p_ref[0, rows]
        keys = p_ref[0, FEATS + head * HD : FEATS + (head + 1) * HD]
        values = p_ref[0, 2 * FEATS + head * HD : 2 * FEATS + (head + 1) * HD]
        soft = soft_ref[0, head]
        d_att = d_attended[rows]
        delta = jnp.sum(
            d_att.astype(F32) * o_ref[0, rows].astype(F32), axis=0, keepdims=True
        )
        d_soft = matmul(values, d_att, 0, 0)
        d_scores = (soft.astype(F32) * (d_soft - delta)).astype(BF16)
        g_p[rows] = (matmul(keys, d_scores) * SCALE).astype(BF16)
        g_p[FEATS + head * HD : FEATS + (head + 1) * HD] = (
            matmul(queries, d_scores, 1, 1) * SCALE
        ).astype(BF16)
        g_p[2 * FEATS + head * HD : 2 * FEATS + (head + 1) * HD] = matmul(
            d_att, soft, 1, 1
        ).astype(BF16)
    d_projected = g_p[...]
    grad_ref[0, :QKV] = matmul(d_projected, a1_ref[...], 1, 1).astype(BF16)
    total[...] += matmul(d_projected, held[slot, :QKV], 0, 0)
    dbqv_ref[step] = columns(
        [row_sums(d_projected[:FEATS].astype(F32)), row_sums(d_projected[2 * FEATS :].astype(F32))],
        8,
    )

    @pl.when(step == 1)
    def end():
        if not last:
            after_ref[...] = total[...]
            return
        col = col_ref[...].reshape(D, 8)
        normed, inv_std = normalize(x_ref[...].astype(F32))
        d_first = total[...].T
        gx_ref[...] = gh_ref[...] + norm_backward(
            d_first, normed, inv_std, col[:, GAIN1 : GAIN1 + 1]
        )
        dcol_ref[...] = columns([row_sums(d_first * normed), row_sums(d_first)], 8)


def whole(shape):
    return pl.BlockSpec(shape, lambda i, info: (0,) * len(shape))


def by_step(shape):
    return pl.BlockSpec((1,) + shape, lambda i, info: (i,) + (0,) * len(shape))


def by_slot(shape, last):
    first = 7 if last else 5
    return pl.BlockSpec((1,) + shape, lambda i, info: (info[first + i],) + (0,) * len(shape))


PIECES = [pl.BlockSpec(memory_space=pltpu.HBM)] * 8
COPY_SEMS = pltpu.SemaphoreType.DMA((8,))
HELD = pltpu.VMEM((SHARDS, D, D), BF16)


def of(shape, dtype=BF16):
    return jax.ShapeDtypeStruct(shape, dtype)


def run(kernel, name, steps, info, operands, in_specs, outs, out_specs, scratch, flops):
    moved = sum(a.size * a.dtype.itemsize for a in operands) + sum(
        a.size * a.dtype.itemsize for a in outs
    )
    return pl.pallas_call(
        kernel,
        name=name,
        out_shape=outs,
        grid_spec=pltpu.PrefetchScalarGridSpec(
            num_scalar_prefetch=1,
            grid=(steps,),
            in_specs=in_specs,
            out_specs=out_specs,
            scratch_shapes=scratch,
        ),
        compiler_params=pltpu.CompilerParams(
            vmem_limit_bytes=VMEM_LIMIT, dimension_semantics=("arbitrary",)
        ),
        cost_estimate=pl.CostEstimate(flops=flops, bytes_accessed=moved, transcendentals=0),
    )(info, *operands)


STREAM = (D, FRAMES)
ROWS = (FRAMES, D)
COLS = (SHARDS, FEATS, 8)
ATT_FLOPS = 2 * FRAMES * D * (4 * D + 2 * FRAMES)
MLP_FLOPS = 4 * FRAMES * D * SHARDS * FF_SHARD


def attention_forward(info, x, col, bqv, chunk):
    return run(
        attention_forward_kernel, "attention_forward", SHARDS, info, (x, col, bqv, *chunk),
        [whole(STREAM), whole(COLS), whole((SHARDS, FEATS, 2))] + PIECES,
        [
            of(STREAM), of((SHARDS, QKV, FRAMES)), of((SHARDS, HEADS_SHARD, FRAMES, FRAMES)),
            of((SHARDS, FEATS, FRAMES)), of(STREAM, F32),
        ],
        [
            whole(STREAM), by_step((QKV, FRAMES)), by_step((HEADS_SHARD, FRAMES, FRAMES)),
            by_step((FEATS, FRAMES)), whole(STREAM),
        ],
        [HELD, COPY_SEMS],
        ATT_FLOPS,
    )


def mlp_forward(info, h, col, b1, chunk_one, chunk_two):
    return run(
        mlp_forward_kernel, "mlp_forward", SHARDS, info, (h, col, b1, *chunk_one, *chunk_two),
        [whole(STREAM), whole(COLS), whole((SHARDS, 1, FF_SHARD))] + PIECES * 2,
        [of(STREAM), of((SHARDS, FRAMES, FF_SHARD)), of((SHARDS, FRAMES, FF_SHARD)), of(STREAM, F32)],
        [whole(STREAM), by_step((FRAMES, FF_SHARD)), by_step((FRAMES, FF_SHARD)), whole(STREAM)],
        [HELD, HELD, pltpu.VMEM(ROWS, BF16), pltpu.VMEM(ROWS, F32), COPY_SEMS, COPY_SEMS],
        MLP_FLOPS,
    )


def mlp_backward(info, gy, h, a2, col, u, slope, before, chunk_one, chunk_two):
    last = before is not None
    carried = (before,) if last else ()
    ends = [of(STREAM, F32), of((D, 8), F32)] if last else [of(ROWS, F32)]
    return run(
        functools.partial(mlp_backward_kernel, last), "mlp_backward", 2, info,
        (gy, h, a2, col, u, slope, *carried, *chunk_one, *chunk_two),
        [
            whole(STREAM), whole(STREAM), whole(STREAM), whole(COLS),
            by_slot((FRAMES, FF_SHARD), last), by_slot((FRAMES, FF_SHARD), last),
        ]
        + [whole(ROWS)] * len(carried)
        + PIECES * 2,
        ends + [of((2, D, D)), of((2, D, D)), of((2, 1, FF_SHARD), F32)],
        [whole(end.shape) for end in ends]
        + [by_step((D, D)), by_step((D, D)), whole((2, 1, FF_SHARD))],
        [HELD, HELD, pltpu.VMEM(ROWS, BF16), pltpu.VMEM(ROWS, F32), COPY_SEMS, COPY_SEMS],
        MLP_FLOPS,
    )


def attention_backward(info, gh, x, a1, col, p, soft, o, before, chunk):
    last = before is not None
    carried = (before,) if last else ()
    ends = [of(STREAM, F32), of((D, 8), F32)] if last else [of(ROWS, F32)]
    return run(
        functools.partial(attention_backward_kernel, last), "attention_backward", 2, info,
        (gh, x, a1, col, p, soft, o, *carried, *chunk),
        [
            whole(STREAM), whole(STREAM), whole(STREAM), whole(COLS),
            by_slot((QKV, FRAMES), last), by_slot((HEADS_SHARD, FRAMES, FRAMES), last),
            by_slot((FEATS, FRAMES), last),
        ]
        + [whole(ROWS)] * len(carried)
        + PIECES,
        ends + [of((2, D, D)), of((2, FEATS, 8), F32)],
        [whole(end.shape) for end in ends] + [by_step((D, D)), whole((2, FEATS, 8))],
        [HELD, pltpu.VMEM(STREAM, BF16), pltpu.VMEM((QKV, FRAMES), BF16), pltpu.VMEM(ROWS, F32), COPY_SEMS],
        ATT_FLOPS,
    )


def tie(groups):
    return lax.optimization_barrier(groups)


def flip(block, axis, bit):
    size = lax.axis_size(axis)
    return lax.ppermute(block, axis, [(i, i ^ bit) for i in range(size)])


def added(left, right):
    return (left.astype(F32) + right.astype(F32)).astype(BF16)


def by_bits(slots, shard):
    odd = shard % 2 == 1
    high = shard >= 2
    first, second, third, fourth = slots
    first, second = jnp.where(odd, second, first), jnp.where(odd, first, second)
    third, fourth = jnp.where(odd, fourth, third), jnp.where(odd, third, fourth)
    return jnp.stack(
        [
            jnp.where(high, third, first), jnp.where(high, fourth, second),
            jnp.where(high, first, third), jnp.where(high, second, fourth),
        ]
    )


def rows_of(value, place, parts):
    size = value.shape[-2] // parts
    return lax.dynamic_slice_in_dim(value, place * size, size, axis=value.ndim - 2)


class Chain:
    def start(self, send):
        self.arrived = flip(send, "tensor", 1)

    def cores(self, keep):
        self.value = added(keep, self.arrived)

    def scatter(self):
        parts = lax.axis_size("dp")
        rows = self.value.shape[-2] // parts
        split = self.value.reshape(-1, parts, rows, D)
        split = jnp.swapaxes(split, 0, 1)
        total = lax.psum_scatter(split, "dp", scatter_dimension=0, tiled=False)
        self.value = total if self.value.ndim == 3 else total[0]

    def send_y(self):
        self.kept, self.arrived = self.value[1], flip(self.value[0], "tensor", 2)

    def send_x(self, first, second):
        section = lax.axis_index("section")
        self.kept = jnp.where(section == 0, first.value, second.value)
        self.arrived = flip(jnp.where(section == 0, second.value, first.value), "section", 1)

    def fold(self):
        self.value = added(self.kept, self.arrived)

    def gather(self):
        bit = 1
        while bit < lax.axis_size("dp"):
            arrived = flip(self.value, "dp", bit)
            upper = (lax.axis_index("dp") & bit) != 0
            self.value = jnp.where(
                upper,
                jnp.concatenate([arrived, self.value], axis=0),
                jnp.concatenate([self.value, arrived], axis=0),
            )
            bit *= 2


def tied(chains, *others):
    values = tie((tuple(chain.value for chain in chains), others))
    for chain, value in zip(chains, values[0]):
        chain.value = value
    return values[1]


def body(ends_in, ln_gain, ln_shift, w_qkv, b_qv, w_out, b_out, w_fc1, b_fc1, w_fc2, b_fc2):
    section = lax.axis_index("section")
    shard = lax.axis_index("tensor")
    zhalf = lax.axis_index("dp") % 2
    clips = ends_in.shape[1] // FRAMES
    info = jnp.stack(
        [shard, shard ^ 1, shard ^ 2, shard ^ 3, zhalf] + [jnp.int32(k) for k in BACK_ORDER]
    ).astype(jnp.int32)

    owned = [
        jnp.concatenate([w_qkv[0].transpose(1, 2, 0).reshape(QKV, D), w_out[0]], axis=0),
        w_fc1[0],
        w_fc2[0],
    ]
    nears = [rows_of(own, zhalf, 2) for own in owned]
    fars = [rows_of(own, 1 - zhalf, 2) for own in owned]
    small = jnp.concatenate(
        [ln_gain[0], ln_shift[0], b_qv[0], b_out, b_fc2, b_fc1.reshape(SHARDS, FEATS)], axis=0
    )
    ends = ends_in[0].T.reshape(FEATS, clips, FRAMES).transpose(1, 0, 2)
    beyond, small, ends, nears[1] = tie((flip(nears[0], "section", 1), small, ends, nears[1]))

    ends = lax.all_to_all(ends, ("section", "tensor"), split_axis=0, concat_axis=0, tiled=True)
    ends = ends.reshape(2, D, FRAMES)

    small_beyond = flip(small, "section", 1)
    small = jnp.stack(
        [jnp.where(section == 0, small, small_beyond), jnp.where(section == 0, small_beyond, small)]
    )
    small_y = flip(small, "tensor", 2)
    pair = jnp.stack([small, small_y])
    pair_other = flip(pair, "tensor", 1)
    slots = jnp.stack([pair[0], pair_other[0], pair[1], pair_other[1]]).astype(F32)
    cols = jnp.transpose(by_bits(slots[:, :, :8], shard), (1, 0, 3, 2))
    bqvs = jnp.transpose(slots[:, :, 4:6], (1, 0, 3, 2))
    b1s = jnp.transpose(slots[:, :, 8:], (1, 0, 2, 3)).reshape(2, SHARDS, 1, FF_SHARD)

    def layers(own, other):
        return jnp.where(section == 0, own, other), jnp.where(section == 0, other, own)

    near_own, far_own = [], []
    for index in range(3):
        near_other = beyond
        if index < 2:
            following = nears[index + 1]
            if index:
                near_other, following = tie((beyond, following))
            beyond = flip(following, "section", 1)
        near_own.append(layers(nears[index], near_other))
        far_own.append(layers(fars[index], flip(near_other, "dp", 1)))

    def over_y(index, layer):
        return flip(near_own[index][layer], "tensor", 2)

    def chunk_of(index, layer, near_there, far_there):
        here = [near_own[index][layer], far_own[index][layer]]
        there = [near_there, far_there]
        return (
            here
            + [flip(part, "tensor", 1) for part in here]
            + there
            + [flip(part, "tensor", 1) for part in there]
        )

    def attend(layer, stream, chunk):
        return attention_forward(info, stream, cols[layer], bqvs[layer], chunk)

    def feed(layer, h, chunk_one, chunk_two):
        return mlp_forward(info, h, cols[layer], b1s[layer], chunk_one, chunk_two)

    chunks = [[None] * 3, [None] * 3]
    stream = ends[0]
    there_a, there_one = over_y(0, 0), over_y(1, 0)
    chunks[0][0] = chunk_of(0, 0, there_a, flip(there_a, "dp", 1))
    away_one = flip(there_one, "dp", 1)
    a1, p, soft, o, h = attend(0, stream, chunks[0][0])

    there_two = over_y(2, 0)
    late = [near_own[index][1] for index in range(3)]
    h, away_one, there_two, late, far_two = tie((h, away_one, there_two, late, far_own[2]))
    far_own[2] = far_two
    for index in range(3):
        near_own[index] = (near_own[index][0], late[index])
    chunks[0][1] = chunk_of(1, 0, there_one, away_one)
    chunks[0][2] = chunk_of(2, 0, there_two, flip(there_two, "dp", 1))
    there_a = over_y(0, 1)
    there_a, late_one, late_two = tie((there_a, late[1], late[2]))
    near_own[1], near_own[2] = (None, late_one), (None, late_two)
    away_a = flip(there_a, "dp", 1)
    there_one, there_two = over_y(1, 1), over_y(2, 1)
    a2, u, slope, y = feed(0, h, chunks[0][1], chunks[0][2])
    stored = [(stream, a1, p, soft, o, h, a2, u, slope)]

    stream, there_a, there_one, there_two, away_a, near_a, far_a = tie(
        (y, there_a, there_one, there_two, away_a, near_own[0][1], far_own[0][1])
    )
    near_own[0], far_own[0] = (None, near_a), (None, far_a)
    chunks[1][0] = chunk_of(0, 1, there_a, away_a)
    away_one, away_two = flip(there_one, "dp", 1), flip(there_two, "dp", 1)
    a1, p, soft, o, h = attend(1, stream, chunks[1][0])
    parts = [[near_own[k][1], far_own[k][1]] for k in (1, 2)]
    h, there_one, there_two, away_one, away_two, parts = tie(
        (h, there_one, there_two, away_one, away_two, parts)
    )
    for index in (1, 2):
        near_own[index] = (None, parts[index - 1][0])
        far_own[index] = (None, parts[index - 1][1])
    chunks[1][1] = chunk_of(1, 1, there_one, away_one)
    chunks[1][2] = chunk_of(2, 1, there_two, away_two)
    a2, u, slope, y = feed(1, h, chunks[1][1], chunks[1][2])
    stored.append((stream, a1, p, soft, o, h, a2, u, slope))
    stream = y

    upstream = ends[1]
    chains = [[Chain() for _ in range(3)] for _ in range(2)]
    smalls = [None, None]
    late_a, late_one, late_two = chains[1]
    last_a, last_one, last_two = chains[0]
    for layer in (1, 0):
        chunk_a, chunk_one, chunk_two = chunks[layer]
        x, a1, p, soft, o, h, a2, u, slope = stored[layer]
        chain_a, chain_one, chain_two = chains[layer]
        after, send_one, send_two, db1_sent = mlp_backward(
            info, upstream, h, a2, cols[layer], u, slope, None, chunk_one, chunk_two
        )
        chain_two.start(send_two)
        chain_one.start(send_one)
        gh, dcol_two, keep_one, keep_two, db1_kept = mlp_backward(
            info, upstream, h, a2, cols[layer], u, slope, after, chunk_one, chunk_two
        )
        chain_two.cores(keep_two)
        chain_one.cores(keep_one)
        (gh,) = tied((chain_two, chain_one), gh)
        if layer == 1:
            late_two.scatter()
            late_one.scatter()
        else:
            last_two.send_y()
            last_one.scatter()
        after, send_a, dbqv_sent = attention_backward(
            info, gh, x, a1, cols[layer], p, soft, o, None, chunk_a
        )
        chain_a.start(send_a)
        upstream, dcol_one, keep_a, dbqv_kept = attention_backward(
            info, gh, x, a1, cols[layer], p, soft, o, after, chunk_a
        )
        chain_a.cores(keep_a)
        (upstream,) = tied((chain_a,), upstream)
        if layer == 1:
            late_a.scatter()
        db1 = by_bits([db1_kept[1], db1_sent[1], db1_kept[0], db1_sent[0]], shard)
        dbqv = by_bits([dbqv_kept[1], dbqv_sent[1], dbqv_kept[0], dbqv_sent[0]], shard)
        dcol = jnp.concatenate(
            [
                dcol_one[:, 0:1], dcol_two[:, 0:1], dcol_one[:, 1:2], dcol_two[:, 1:2],
                dbqv[:, :, 0:2].reshape(D, 2), dcol_two[:, 2:4],
            ],
            axis=1,
        )
        smalls[layer] = jnp.concatenate(
            [
                dcol.reshape(SHARDS, FEATS, 8).transpose(0, 2, 1),
                db1.reshape(SHARDS, SHARDS, FEATS),
            ],
            axis=1,
        )

    result = jnp.stack([upstream.astype(BF16), stream.astype(BF16)])
    result = result.reshape(2 * SHARDS, FEATS, FRAMES)
    small_sum = jnp.stack(smalls)

    last_two.fold()
    result, small_sum = tied((last_a, last_two), result, small_sum)
    last_a.send_y()
    last_two.scatter()
    late_two.send_y()
    late_one.send_y()
    small_sum += flip(small_sum, "tensor", 1)
    late_two.fold()
    late_one.fold()
    small_sum += flip(small_sum, "tensor", 2)

    result, small_sum = tied((late_two, late_one, late_a, last_one), result, small_sum)
    last_one.send_y()
    late_a.send_y()
    result = lax.all_to_all(result, ("section", "tensor"), split_axis=0, concat_axis=0, tiled=True)
    small_sum += flip(small_sum, "section", 1)
    last_one.fold()
    late_a.fold()
    last_a.fold()
    result, small_sum = tied((late_a, last_one, last_a), result, small_sum)
    last_a.scatter()
    pair_one = Chain()
    pair_one.send_x(last_one, late_one)
    pair_one.fold()
    small_sum += flip(small_sum, "dp", 1)
    result, small_sum = tied((pair_one, last_two), result, small_sum)
    pair_two = Chain()
    pair_two.send_x(last_two, late_two)
    pair_two.fold()
    pair_one.gather()
    pair_two.gather()
    bit = 2
    while bit < lax.axis_size("dp"):
        small_sum += flip(small_sum, "dp", bit)
        bit *= 2
    result = result.transpose(1, 0, 2).reshape(FEATS, clips * FRAMES).T.astype(F32)
    small_sum = lax.dynamic_slice(
        small_sum, (section, shard, 0, 0), (1, 1, 12, FEATS)
    ).reshape(12, FEATS)
    pair_a = Chain()
    pair_a.send_x(last_a, late_a)
    pair_a.fold()
    pair_a.gather()

    grad_a, grad_one, grad_two = [pair.value.astype(F32) for pair in (pair_a, pair_one, pair_two)]
    return (
        result[None],
        small_sum[None, 0:2],
        small_sum[None, 2:4],
        grad_a[:QKV].reshape(3, FEATS, D).transpose(2, 0, 1)[None],
        small_sum[None, 4:6],
        grad_a[QKV:][None],
        small_sum[6:7],
        grad_one[None],
        small_sum[8:12].reshape(1, FF_SHARD),
        grad_two[None],
        small_sum[7:8],
    )


def solution(mesh):
    placed = (
        P("section", "dp", "tensor"),
        P("section", None, "tensor"),
        P("section", None, "tensor"),
        P("section", None, None, "tensor"),
        P("section", None, "tensor"),
        P("section", "tensor", None),
        P("section", "tensor"),
        P("section", None, "tensor"),
        P("section", "tensor"),
        P("section", "tensor", None),
        P("section", "tensor"),
    )
    return jax.shard_map(
        body, mesh=mesh, in_specs=placed, out_specs=placed, check_vma=False
    )
```

```python
import functools

import jax
import jax.numpy as jnp
from jax import lax
from jax.experimental import pallas as pl
from jax.experimental.pallas import tpu as pltpu
from jax.sharding import PartitionSpec as P

D = 768
HD = 64
FRAMES = 448
SHARDS = 4
HEADS_SHARD = 3
FEATS = HEADS_SHARD * HD
QKV = 3 * FEATS
FF_SHARD = 768
HALF = D // 2
EPSILON = 1e-05
SCALE = float(HD) ** (-0.5)
VMEM_LIMIT = 48 * 1024 * 1024
GAIN1, GAIN2, SHIFT1, SHIFT2, BIAS_Q, BIAS_V, BIAS_OUT, BIAS_FC2 = range(8)
BACK_ORDER = (3, 1, 2, 0)
F32 = jnp.float32
BF16 = jnp.bfloat16


def matmul(left, right, left_dim=1, right_dim=0):
    return lax.dot_general(
        left, right, (((left_dim,), (right_dim,)), ((), ())), preferred_element_type=F32
    )


def normalize(values):
    center = jnp.mean(values, axis=0, keepdims=True)
    moved = values - center
    inv_std = lax.rsqrt(jnp.mean(moved * moved, axis=0, keepdims=True) + EPSILON)
    return moved * inv_std, inv_std


def norm_backward(upstream, normed, inv_std, gain):
    scaled = upstream * gain
    mean_one = jnp.mean(scaled, axis=0, keepdims=True)
    mean_two = jnp.mean(scaled * normed, axis=0, keepdims=True)
    return inv_std * (scaled - mean_one - normed * mean_two)


def row_sums(values):
    return jnp.sum(values, axis=1, keepdims=True)


def columns(parts, lanes):
    lane = lax.broadcasted_iota(jnp.int32, (parts[0].shape[0], lanes), 1)
    total = jnp.zeros((parts[0].shape[0], lanes), F32)
    for index, part in enumerate(parts):
        total = jnp.where(lane == index, part, total)
    return total


def piece_copies(info, pieces, held, sems):
    first = pl.multiple_of(info[4] * HALF, HALF)
    second = pl.multiple_of((1 - info[4]) * HALF, HALF)
    copies, taken = [], 0
    for slot in range(SHARDS):
        targets = [held.at[slot]]
        if pieces[taken].shape[0] == HALF:
            targets = [held.at[slot, pl.ds(first, HALF)], held.at[slot, pl.ds(second, HALF)]]
        copies.append(
            tuple(
                pltpu.make_async_copy(pieces[taken + k], target, sems.at[2 * slot + k])
                for k, target in enumerate(targets)
            )
        )
        taken += len(targets)
    return tuple(copies)


def load_pieces(step, order, chunks):
    @pl.when(step == 0)
    def start():
        for slot in order:
            for chunk in chunks:
                for copy in chunk[slot]:
                    copy.start()

    for index, slot in enumerate(order):

        @pl.when(step == index)
        def wait():
            for chunk in chunks:
                for copy in chunk[slot]:
                    copy.wait()


def attention_forward_kernel(
    count, info, x_ref, col_ref, bqv_ref, *refs
):
    step = pl.program_id(0)
    pieces, (a1_ref, p_ref, soft_ref, o_ref, h_ref, held, sems) = refs[:count], refs[count:]
    copies = piece_copies(info, pieces, held, sems)
    load_pieces(step, range(SHARDS), (copies,))

    @pl.when(step == 0)
    def first():
        col = col_ref[...].reshape(D, 8)
        values = x_ref[...].astype(F32)
        normed, _ = normalize(values)
        a1_ref[...] = (
            normed * col[:, GAIN1 : GAIN1 + 1] + col[:, SHIFT1 : SHIFT1 + 1]
        ).astype(BF16)
        h_ref[...] = values + col[:, BIAS_OUT : BIAS_OUT + 1]

    bias = bqv_ref[step]
    projected = matmul(held[step, :QKV], a1_ref[...])
    queries = (projected[:FEATS] + bias[:, 0:1]).astype(BF16)
    keys = projected[FEATS : 2 * FEATS].astype(BF16)
    values = (projected[2 * FEATS :] + bias[:, 1:2]).astype(BF16)
    p_ref[0, :FEATS] = queries
    p_ref[0, FEATS : 2 * FEATS] = keys
    p_ref[0, 2 * FEATS :] = values
    scaled = queries * SCALE
    for head in range(HEADS_SHARD):
        rows = slice(head * HD, (head + 1) * HD)
        scores = matmul(keys[rows], scaled[rows], 0, 0)
        exps = jnp.exp(scores - jnp.max(scores, axis=0, keepdims=True))
        soft = exps * (1.0 / jnp.sum(exps, axis=0, keepdims=True))
        soft = soft.astype(BF16)
        soft_ref[0, head] = soft
        o_ref[0, rows] = matmul(values[rows], soft).astype(BF16)
    h_ref[...] += matmul(held[step, QKV:], o_ref[0], 0, 0)


def mlp_forward_kernel(
    counts, info, h_ref, col_ref, b1_ref, *refs
):
    step = pl.program_id(0)
    pieces_one, pieces_two, refs = refs[:counts[0]], refs[counts[0]:sum(counts)], refs[sum(counts):]
    a2_ref, u_ref, slope_ref, y_ref, held_one, held_two, a2_rows, total, sems_one, sems_two = refs
    copies_one = piece_copies(info, pieces_one, held_one, sems_one)
    copies_two = piece_copies(info, pieces_two, held_two, sems_two)
    load_pieces(step, range(SHARDS), (copies_one, copies_two))

    @pl.when(step == 0)
    def first():
        col = col_ref[...].reshape(D, 8)
        normed, _ = normalize(h_ref[...])
        scaled = normed * col[:, GAIN2 : GAIN2 + 1] + col[:, SHIFT2 : SHIFT2 + 1]
        a2_ref[...] = scaled.astype(BF16)
        a2_rows[...] = scaled.T.astype(BF16)
        total[...] = jnp.zeros_like(total)

    inner = matmul(a2_rows[...], held_one[step]) + b1_ref[step]
    phi = 0.5 + 0.5 * lax.erf(inner * 0.7071067811865476)
    density = 0.3989422804014327 * jnp.exp(-0.5 * inner * inner)
    active = (inner * phi).astype(BF16)
    u_ref[0] = active
    slope_ref[0] = (phi + inner * density).astype(BF16)
    total[...] += matmul(active, held_two[step])

    @pl.when(step == SHARDS - 1)
    def last():
        col = col_ref[...].reshape(D, 8)
        y_ref[...] = h_ref[...] + total[...].T + col[:, BIAS_FC2 : BIAS_FC2 + 1]


def mlp_backward_kernel(
    last, counts, info, gy_ref, h_ref, a2_ref, col_ref, u_ref, slope_ref, *refs
):
    step = pl.program_id(0)
    if last:
        before_ref, *refs = refs
    pieces_one, pieces_two, refs = refs[:counts[0]], refs[counts[0]:sum(counts)], refs[sum(counts):]
    if last:
        gh_ref, dcol_ref, *refs = refs
    else:
        after_ref, *refs = refs
    grad_one, grad_two, db1_ref, held_one, held_two, gy_rows, total, sems_one, sems_two = refs
    copies_one = piece_copies(info, pieces_one, held_one, sems_one)
    copies_two = piece_copies(info, pieces_two, held_two, sems_two)
    load_pieces(step, BACK_ORDER[2:] if last else BACK_ORDER[:2], (copies_two, copies_one))

    @pl.when(step == 0)
    def first():
        gy_rows[...] = gy_ref[...].astype(F32).T.astype(BF16)
        total[...] = before_ref[...] if last else jnp.zeros_like(total)

    slot = info[(7 if last else 5) + step]
    d_active = matmul(gy_rows[...], held_two[slot], 1, 1)
    d_inner = d_active * slope_ref[0].astype(F32)
    rounded = d_inner.astype(BF16)
    db1_ref[step] = jnp.sum(rounded.astype(F32), axis=0, keepdims=True)
    grad_two[0] = matmul(u_ref[0], gy_rows[...], 0, 0).astype(BF16)
    grad_one[0] = matmul(a2_ref[...], rounded).astype(BF16)
    total[...] += matmul(rounded, held_one[slot], 1, 1)

    @pl.when(step == 1)
    def end():
        if not last:
            after_ref[...] = total[...]
            return
        col = col_ref[...].reshape(D, 8)
        normed, inv_std = normalize(h_ref[...])
        d_mid = total[...].T
        upstream = gy_ref[...].astype(F32)
        d_hidden = upstream + norm_backward(d_mid, normed, inv_std, col[:, GAIN2 : GAIN2 + 1])
        gh_ref[...] = d_hidden
        dcol_ref[...] = columns(
            [row_sums(d_mid * normed), row_sums(d_mid), row_sums(d_hidden), row_sums(upstream)], 8
        )


def attention_backward_kernel(
    last, count, info, gh_ref, x_ref, a1_ref, col_ref, p_ref, soft_ref, o_ref, *refs
):
    step = pl.program_id(0)
    if last:
        before_ref, *refs = refs
    pieces, refs = refs[:count], refs[count:]
    if last:
        gx_ref, dcol_ref, *refs = refs
    else:
        after_ref, *refs = refs
    grad_ref, dbqv_ref, held, gh_rounded, g_p, total, sems = refs
    copies = piece_copies(info, pieces, held, sems)
    load_pieces(step, BACK_ORDER[2:] if last else BACK_ORDER[:2], (copies,))

    @pl.when(step == 0)
    def first():
        gh_rounded[...] = gh_ref[...].astype(BF16)
        total[...] = before_ref[...] if last else jnp.zeros_like(total)

    slot = info[(7 if last else 5) + step]
    d_attended = matmul(held[slot, QKV:], gh_rounded[...]).astype(BF16)
    grad_ref[0, QKV:] = matmul(o_ref[0], gh_rounded[...], 1, 1).astype(BF16)
    for head in range(HEADS_SHARD):
        rows = slice(head * HD, (head + 1) * HD)
        queries = p_ref[0, rows]
        keys = p_ref[0, FEATS + head * HD : FEATS + (head + 1) * HD]
        values = p_ref[0, 2 * FEATS + head * HD : 2 * FEATS + (head + 1) * HD]
        soft = soft_ref[0, head]
        d_att = d_attended[rows]
        delta = jnp.sum(
            d_att.astype(F32) * o_ref[0, rows].astype(F32), axis=0, keepdims=True
        )
        d_soft = matmul(values, d_att, 0, 0)
        d_scores = (soft.astype(F32) * (d_soft - delta)).astype(BF16)
        g_p[rows] = (matmul(keys, d_scores) * SCALE).astype(BF16)
        g_p[FEATS + head * HD : FEATS + (head + 1) * HD] = (
            matmul(queries, d_scores, 1, 1) * SCALE
        ).astype(BF16)
        g_p[2 * FEATS + head * HD : 2 * FEATS + (head + 1) * HD] = matmul(
            d_att, soft, 1, 1
        ).astype(BF16)
    d_projected = g_p[...]
    grad_ref[0, :QKV] = matmul(d_projected, a1_ref[...], 1, 1).astype(BF16)
    total[...] += matmul(d_projected, held[slot, :QKV], 0, 0)
    dbqv_ref[step] = columns(
        [row_sums(d_projected[:FEATS].astype(F32)), row_sums(d_projected[2 * FEATS :].astype(F32))],
        8,
    )

    @pl.when(step == 1)
    def end():
        if not last:
            after_ref[...] = total[...]
            return
        col = col_ref[...].reshape(D, 8)
        normed, inv_std = normalize(x_ref[...].astype(F32))
        d_first = total[...].T
        gx_ref[...] = gh_ref[...] + norm_backward(
            d_first, normed, inv_std, col[:, GAIN1 : GAIN1 + 1]
        )
        dcol_ref[...] = columns([row_sums(d_first * normed), row_sums(d_first)], 8)


def whole(shape):
    return pl.BlockSpec(shape, lambda i, info: (0,) * len(shape))


def by_step(shape):
    return pl.BlockSpec((1,) + shape, lambda i, info: (i,) + (0,) * len(shape))


def by_slot(shape, last):
    first = 7 if last else 5
    return pl.BlockSpec((1,) + shape, lambda i, info: (info[first + i],) + (0,) * len(shape))


PIECE = [pl.BlockSpec(memory_space=pltpu.HBM)]
COPY_SEMS = pltpu.SemaphoreType.DMA((2 * SHARDS,))
HELD = pltpu.VMEM((SHARDS, D, D), BF16)


def of(shape, dtype=BF16):
    return jax.ShapeDtypeStruct(shape, dtype)


def run(kernel, name, steps, info, operands, in_specs, outs, out_specs, scratch, flops):
    return pl.pallas_call(
        kernel,
        name=name,
        out_shape=outs,
        grid_spec=pltpu.PrefetchScalarGridSpec(
            num_scalar_prefetch=1,
            grid=(steps,),
            in_specs=in_specs,
            out_specs=out_specs,
            scratch_shapes=scratch,
        ),
        compiler_params=pltpu.CompilerParams(
            vmem_limit_bytes=VMEM_LIMIT, dimension_semantics=("arbitrary",)
        ),
        cost_estimate=pl.CostEstimate(flops=flops // 16, bytes_accessed=2**20, transcendentals=0),
    )(info, *operands)


STREAM = (D, FRAMES)
ROWS = (FRAMES, D)
COLS = (SHARDS, FEATS, 8)
ATT_FLOPS = 2 * FRAMES * D * (4 * D + 2 * FRAMES)
MLP_FLOPS = 4 * FRAMES * D * SHARDS * FF_SHARD


def attention_forward(info, x, col, bqv, chunk):
    return run(
        functools.partial(attention_forward_kernel, len(chunk)), "attention_forward", SHARDS, info, (x, col, bqv, *chunk),
        [whole(STREAM), whole(COLS), whole((SHARDS, FEATS, 2))] + PIECE * len(chunk),
        [
            of(STREAM), of((SHARDS, QKV, FRAMES)), of((SHARDS, HEADS_SHARD, FRAMES, FRAMES)),
            of((SHARDS, FEATS, FRAMES)), of(STREAM, F32),
        ],
        [
            whole(STREAM), by_step((QKV, FRAMES)), by_step((HEADS_SHARD, FRAMES, FRAMES)),
            by_step((FEATS, FRAMES)), whole(STREAM),
        ],
        [HELD, COPY_SEMS],
        ATT_FLOPS,
    )


def mlp_forward(info, h, col, b1, chunk_one, chunk_two):
    return run(
        functools.partial(mlp_forward_kernel, (len(chunk_one), len(chunk_two))), "mlp_forward", SHARDS, info, (h, col, b1, *chunk_one, *chunk_two),
        [whole(STREAM), whole(COLS), whole((SHARDS, 1, FF_SHARD))] + PIECE * len(chunk_one + chunk_two),
        [of(STREAM), of((SHARDS, FRAMES, FF_SHARD)), of((SHARDS, FRAMES, FF_SHARD)), of(STREAM, F32)],
        [whole(STREAM), by_step((FRAMES, FF_SHARD)), by_step((FRAMES, FF_SHARD)), whole(STREAM)],
        [HELD, HELD, pltpu.VMEM(ROWS, BF16), pltpu.VMEM(ROWS, F32), COPY_SEMS, COPY_SEMS],
        MLP_FLOPS,
    )


def mlp_backward(info, gy, h, a2, col, u, slope, before, chunk_one, chunk_two):
    last = before is not None
    carried = (before,) if last else ()
    ends = [of(STREAM, F32), of((D, 8), F32)] if last else [of(ROWS, F32)]
    return run(
        functools.partial(mlp_backward_kernel, last, (len(chunk_one), len(chunk_two))), "mlp_backward", 2, info,
        (gy, h, a2, col, u, slope, *carried, *chunk_one, *chunk_two),
        [
            whole(STREAM), whole(STREAM), whole(STREAM), whole(COLS),
            by_slot((FRAMES, FF_SHARD), last), by_slot((FRAMES, FF_SHARD), last),
        ]
        + [whole(ROWS)] * len(carried)
        + PIECE * len(chunk_one + chunk_two),
        ends + [of((2, D, D)), of((2, D, D)), of((2, 1, FF_SHARD), F32)],
        [whole(end.shape) for end in ends]
        + [by_step((D, D)), by_step((D, D)), whole((2, 1, FF_SHARD))],
        [HELD, HELD, pltpu.VMEM(ROWS, BF16), pltpu.VMEM(ROWS, F32), COPY_SEMS, COPY_SEMS],
        MLP_FLOPS,
    )


def attention_backward(info, gh, x, a1, col, p, soft, o, before, chunk):
    last = before is not None
    carried = (before,) if last else ()
    ends = [of(STREAM, F32), of((D, 8), F32)] if last else [of(ROWS, F32)]
    return run(
        functools.partial(attention_backward_kernel, last, len(chunk)), "attention_backward", 2, info,
        (gh, x, a1, col, p, soft, o, *carried, *chunk),
        [
            whole(STREAM), whole(STREAM), whole(STREAM), whole(COLS),
            by_slot((QKV, FRAMES), last), by_slot((HEADS_SHARD, FRAMES, FRAMES), last),
            by_slot((FEATS, FRAMES), last),
        ]
        + [whole(ROWS)] * len(carried)
        + PIECE * len(chunk),
        ends + [of((2, D, D)), of((2, FEATS, 8), F32)],
        [whole(end.shape) for end in ends] + [by_step((D, D)), whole((2, FEATS, 8))],
        [HELD, pltpu.VMEM(STREAM, BF16), pltpu.VMEM((QKV, FRAMES), BF16), pltpu.VMEM(ROWS, F32), COPY_SEMS],
        ATT_FLOPS,
    )


def tie(groups):
    return lax.optimization_barrier(groups)


def flip(block, axis, bit):
    size = lax.axis_size(axis)
    return lax.ppermute(block, axis, [(i, i ^ bit) for i in range(size)])


def added(left, right):
    return (left.astype(F32) + right.astype(F32)).astype(BF16)


def by_bits(slots, shard):
    odd = shard % 2 == 1
    high = shard >= 2
    first, second, third, fourth = slots
    first, second = jnp.where(odd, second, first), jnp.where(odd, first, second)
    third, fourth = jnp.where(odd, fourth, third), jnp.where(odd, third, fourth)
    return jnp.stack(
        [
            jnp.where(high, third, first), jnp.where(high, fourth, second),
            jnp.where(high, first, third), jnp.where(high, second, fourth),
        ]
    )


def rows_of(value, place, parts):
    size = value.shape[-2] // parts
    return lax.dynamic_slice_in_dim(value, place * size, size, axis=value.ndim - 2)


class Chain:
    def start(self, send):
        self.arrived = flip(send, "tensor", 1)

    def cores(self, keep):
        self.value = added(keep, self.arrived)

    def scatter(self):
        parts = lax.axis_size("dp")
        rows = self.value.shape[-2] // parts
        split = self.value.reshape(-1, parts, rows, D)
        split = jnp.swapaxes(split, 0, 1)
        total = lax.psum_scatter(split, "dp", scatter_dimension=0, tiled=False)
        self.value = total if self.value.ndim == 3 else total[0]

    def send_y(self):
        self.kept, self.arrived = self.value[1], flip(self.value[0], "tensor", 2)

    def send_x(self, first, second):
        section = lax.axis_index("section")
        self.kept = jnp.where(section == 0, first.value, second.value)
        self.arrived = flip(jnp.where(section == 0, second.value, first.value), "section", 1)

    def fold(self):
        self.value = added(self.kept, self.arrived)

    def split(self):
        self.value = self.value.reshape(lax.axis_size("dp"), -1, D)

    def send_half(self, bit):
        mine = ((lax.axis_index("dp") & bit) != 0).astype(jnp.int32)
        blocks = self.value.reshape(-1, 2, *self.value.shape[1:])
        self.kept = lax.dynamic_index_in_dim(blocks, mine, 1, keepdims=False)
        self.arrived = flip(
            lax.dynamic_index_in_dim(blocks, 1 - mine, 1, keepdims=False), "dp", bit
        )

    def send_back(self, bit):
        self.arrived = flip(self.value, "dp", bit)

    def join(self, bit):
        upper = (lax.axis_index("dp") & bit) != 0
        value = jnp.where(
            upper,
            jnp.stack([self.arrived, self.value], axis=1),
            jnp.stack([self.value, self.arrived], axis=1),
        )
        self.value = value.reshape(-1, *value.shape[2:])


def tied(chains, *others):
    values = tie((tuple(chain.value for chain in chains), others))
    for chain, value in zip(chains, values[0]):
        chain.value = value
    return values[1]


def body(ends_in, ln_gain, ln_shift, w_qkv, b_qv, w_out, b_out, w_fc1, b_fc1, w_fc2, b_fc2):
    section = lax.axis_index("section")
    shard = lax.axis_index("tensor")
    zhalf = lax.axis_index("dp") % 2
    clips = ends_in.shape[1] // FRAMES
    info = jnp.stack(
        [shard, shard ^ 1, shard ^ 2, shard ^ 3, zhalf] + [jnp.int32(k) for k in BACK_ORDER]
    ).astype(jnp.int32)

    owned = [
        jnp.concatenate([w_qkv[0].transpose(1, 2, 0).reshape(QKV, D), w_out[0]], axis=0),
        w_fc1[0],
        w_fc2[0],
    ]
    small = jnp.concatenate(
        [ln_gain[0], ln_shift[0], b_qv[0], b_out, b_fc2, b_fc1.reshape(SHARDS, FEATS)], axis=0
    )
    ends = ends_in[0].T.reshape(FEATS, clips, FRAMES).transpose(1, 0, 2)
    beyond_a, small, owned[1], owned[2] = tie(
        (flip(owned[0], "section", 1), small, owned[1], owned[2])
    )
    own_there_a = flip(owned[0], "tensor", 2)
    beyond_one = flip(owned[1], "section", 1)
    beyond_two = flip(owned[2], "section", 1)

    ends = lax.all_to_all(ends, ("section", "tensor"), split_axis=0, concat_axis=0, tiled=True)
    ends = ends.reshape(2, D, FRAMES)

    small_beyond = flip(small, "section", 1)
    small = jnp.stack(
        [jnp.where(section == 0, small, small_beyond), jnp.where(section == 0, small_beyond, small)]
    )
    small_y = flip(small, "tensor", 2)
    pair = jnp.stack([small, small_y])
    pair_other = flip(pair, "tensor", 1)
    slots = jnp.stack([pair[0], pair_other[0], pair[1], pair_other[1]]).astype(F32)
    cols = jnp.transpose(by_bits(slots[:, :, :8], shard), (1, 0, 3, 2))
    bqvs = jnp.transpose(slots[:, :, 4:6], (1, 0, 3, 2))
    b1s = jnp.transpose(slots[:, :, 8:], (1, 0, 2, 3)).reshape(2, SHARDS, 1, FF_SHARD)

    def layers(own, other):
        return jnp.where(section == 0, own, other), jnp.where(section == 0, other, own)

    def over_y(block):
        return flip(block, "tensor", 2)

    def whole_chunk(own, there):
        return (own, flip(own, "tensor", 1), there, flip(there, "tensor", 1))

    def shared_chunk(own, near, far):
        return (own, flip(own, "tensor", 1), near, far, flip(near, "tensor", 1), flip(far, "tensor", 1))

    n_dp = lax.axis_size("dp")
    a_own = layers(owned[0], beyond_a)
    there_a, beyond_one = tie((over_y(beyond_a), beyond_one))
    a_there = layers(own_there_a, there_a)
    one_own = layers(owned[1], beyond_one)
    one_there = over_y(one_own[0])

    def attend(layer, stream, chunk):
        return attention_forward(info, stream, cols[layer], bqvs[layer], chunk)

    def feed(layer, h, chunk_one, chunk_two):
        return mlp_forward(info, h, cols[layer], b1s[layer], chunk_one, chunk_two)

    chunks = [[whole_chunk(a_own[0], a_there[0])], []]
    stream = ends[0]
    a1, p, soft, o, h = attend(0, stream, chunks[0][0])
    h, beyond_two, one_there, late_a, late_one = tie(
        (h, beyond_two, one_there, (a_own[1], a_there[1]), one_own[1])
    )
    two_own = layers(owned[2], beyond_two)
    two_there = over_y(two_own[0])
    chunks[0].append(whole_chunk(one_own[0], one_there))
    two_there, halves = tie(
        (two_there, [rows_of(late_one, zhalf, 2), rows_of(two_own[1], zhalf, 2)])
    )
    nears = [over_y(half) for half in halves]
    chunks[0].append(whole_chunk(two_own[0], two_there))
    a2, u, slope, y = feed(0, h, *chunks[0][1:])
    stored = [(stream, a1, p, soft, o, h, a2, u, slope)]
    stream, nears, late_a, late_one, late_two = tie((y, nears, late_a, late_one, two_own[1]))
    chunks[1].append(whole_chunk(*late_a))
    fars = [flip(near, "dp", 1) for near in nears]
    a1, p, soft, o, h = attend(1, stream, chunks[1][0])
    h, nears, fars, late_one, late_two = tie((h, nears, fars, late_one, late_two))
    chunks[1].append(shared_chunk(late_one, nears[0], fars[0]))
    chunks[1].append(shared_chunk(late_two, nears[1], fars[1]))
    a2, u, slope, y = feed(1, h, *chunks[1][1:])
    stored.append((stream, a1, p, soft, o, h, a2, u, slope))
    stream = y

    upstream = ends[1]
    chains = [[Chain() for _ in range(3)] for _ in range(2)]
    smalls = [None, None]
    ends_of = [None, None]
    late_a, late_one, late_two = chains[1]
    last_a, last_one, last_two = chains[0]
    for layer in (1, 0):
        chunk_a, chunk_one, chunk_two = chunks[layer]
        x, a1, p, soft, o, h, a2, u, slope = stored[layer]
        chain_a, chain_one, chain_two = chains[layer]
        after, send_one, send_two, db1_sent = mlp_backward(
            info, upstream, h, a2, cols[layer], u, slope, None, chunk_one, chunk_two
        )
        chain_two.start(send_two)
        chain_one.start(send_one)
        gh, dcol_two, keep_one, keep_two, db1_kept = mlp_backward(
            info, upstream, h, a2, cols[layer], u, slope, after, chunk_one, chunk_two
        )
        chain_two.cores(keep_two)
        chain_one.cores(keep_one)
        if layer == 0:
            late_a.fold()
            (gh,) = tied((late_a, last_two, last_one, late_one), gh)
            late_a.scatter()
            last_two.send_y()
            last_one.send_y()
        else:
            (gh,) = tied((late_two, late_one), gh)
            late_one.scatter()
            late_two.send_y()
        after, send_a, dbqv_sent = attention_backward(
            info, gh, x, a1, cols[layer], p, soft, o, None, chunk_a
        )
        chain_a.start(send_a)
        upstream, dcol_one, keep_a, dbqv_kept = attention_backward(
            info, gh, x, a1, cols[layer], p, soft, o, after, chunk_a
        )
        chain_a.cores(keep_a)
        if layer == 1:
            late_two.fold()
            (upstream,) = tied((late_two, late_a), upstream)
            late_two.scatter()
            late_a.send_y()
        else:
            last_two.fold()
            (upstream,) = tied((last_two, last_a, late_two), upstream)
            last_two.scatter()
            last_a.send_y()
        ends_of[layer] = (db1_kept, db1_sent, dbqv_kept, dbqv_sent, dcol_one, dcol_two)

    upstream, ends_of = tie((upstream, ends_of))
    for layer in range(2):
        db1_kept, db1_sent, dbqv_kept, dbqv_sent, dcol_one, dcol_two = ends_of[layer]
        db1 = by_bits([db1_kept[1], db1_sent[1], db1_kept[0], db1_sent[0]], shard)
        dbqv = by_bits([dbqv_kept[1], dbqv_sent[1], dbqv_kept[0], dbqv_sent[0]], shard)
        dcol = jnp.concatenate(
            [
                dcol_one[:, 0:1], dcol_two[:, 0:1], dcol_one[:, 1:2], dcol_two[:, 1:2],
                dbqv[:, :, 0:2].reshape(D, 2), dcol_two[:, 2:4],
            ],
            axis=1,
        )
        smalls[layer] = jnp.concatenate(
            [
                dcol.reshape(SHARDS, FEATS, 8).transpose(0, 2, 1),
                db1.reshape(SHARDS, SHARDS, FEATS),
            ],
            axis=1,
        )

    result = jnp.stack([upstream.astype(BF16), stream.astype(BF16)])
    result = result.reshape(2 * SHARDS, FEATS, FRAMES)
    small_sum = jnp.stack(smalls)

    small_sum += flip(small_sum, "tensor", 1)
    small_y = flip(small_sum, "tensor", 2)
    late_one.send_y()

    last_one.fold()
    small_y, result, last_a.arrived = tied((last_one,), small_y, result, last_a.arrived)
    last_one.scatter()
    result = lax.all_to_all(result, ("section", "tensor"), split_axis=0, concat_axis=0, tiled=True)
    small_sum += small_y
    small_sum += flip(small_sum, "section", 1)
    bits = [1 << k for k in range(n_dp.bit_length() - 1)]
    for bit in bits:
        small_sum += flip(small_sum, "dp", bit)

    last_a.fold()
    late_one.fold()
    (small_sum,) = tied((last_a, late_one, last_two), small_sum)
    last_a.split()
    last_a.send_half(bits[0])
    pair_two, pair_one, pair_a = Chain(), Chain(), Chain()
    pair_two.send_x(last_two, late_two)
    small_sum = lax.dynamic_slice(
        small_sum, (section, shard, 0, 0), (1, 1, 12, FEATS)
    ).reshape(12, FEATS)

    last_a.fold()
    pair_two.fold()
    (small_sum,) = tied((last_a, pair_two), small_sum)
    pair_two.value = pair_two.value[None]
    for bit in bits[1:]:
        last_a.send_half(bit)
        if bit != bits[-1]:
            last_a.fold()
    pair_two.send_back(bits[-1])

    last_a.fold()
    last_a.value = last_a.value[0]
    pair_two.join(bits[-1])
    for bit in bits[-2:0:-1]:
        pair_two.send_back(bit)
        pair_two.join(bit)
    result, small_sum = tied((last_a, pair_two, last_one), result, small_sum)
    pair_one.send_x(last_one, late_one)
    pair_a.send_x(last_a, late_a)
    pair_two.send_back(bits[0])

    for pair in (pair_one, pair_a):
        pair.fold()
        pair.value = pair.value[None]
    pair_two.join(bits[0])
    result, small_sum = tied((pair_one, pair_a, pair_two), result, small_sum)
    for bit in bits[:0:-1]:
        for pair in (pair_one, pair_a):
            pair.send_back(bit)
        for pair in (pair_one, pair_a):
            pair.join(bit)
    result, small_sum = tied((pair_one, pair_a), result, small_sum)
    for pair in (pair_one, pair_a):
        pair.send_back(bits[0])
    result = result.transpose(1, 0, 2).reshape(FEATS, clips * FRAMES).T.astype(F32)
    for pair in (pair_one, pair_a):
        pair.join(bits[0])
    for pair in (pair_two, pair_one, pair_a):
        pair.value = pair.value.reshape(D, D)

    grad_a, grad_one, grad_two = [pair.value.astype(F32) for pair in (pair_a, pair_one, pair_two)]
    return (
        result[None],
        small_sum[None, 0:2],
        small_sum[None, 2:4],
        grad_a[:QKV].reshape(3, FEATS, D).transpose(2, 0, 1)[None],
        small_sum[None, 4:6],
        grad_a[QKV:][None],
        small_sum[6:7],
        grad_one[None],
        small_sum[8:12].reshape(1, FF_SHARD),
        grad_two[None],
        small_sum[7:8],
    )


def solution(mesh):
    placed = (
        P("section", "dp", "tensor"),
        P("section", None, "tensor"),
        P("section", None, "tensor"),
        P("section", None, None, "tensor"),
        P("section", None, "tensor"),
        P("section", "tensor", None),
        P("section", "tensor"),
        P("section", None, "tensor"),
        P("section", "tensor"),
        P("section", "tensor", None),
        P("section", "tensor"),
    )
    return jax.shard_map(
        body, mesh=mesh, in_specs=placed, out_specs=placed, check_vma=False
    )
```

```python
import functools

import jax
import jax.numpy as jnp
from jax import lax
from jax.experimental import pallas as pl
from jax.experimental.pallas import tpu as pltpu
from jax.sharding import PartitionSpec as P

D = 768
HD = 64
FRAMES = 448
SHARDS = 4
HEADS_SHARD = 3
FEATS = HEADS_SHARD * HD
QKV = 3 * FEATS
FF_SHARD = 768
HALF = D // 2
EPSILON = 1e-05
SCALE = float(HD) ** (-0.5)
VMEM_LIMIT = 48 * 1024 * 1024
GAIN1, GAIN2, SHIFT1, SHIFT2, BIAS_Q, BIAS_V, BIAS_OUT, BIAS_FC2 = range(8)
BACK_ORDER = (3, 1, 2, 0)
F32 = jnp.float32
BF16 = jnp.bfloat16


def matmul(left, right, left_dim=1, right_dim=0):
    return lax.dot_general(
        left, right, (((left_dim,), (right_dim,)), ((), ())), preferred_element_type=F32
    )


def normalize(values):
    center = jnp.mean(values, axis=0, keepdims=True)
    moved = values - center
    inv_std = lax.rsqrt(jnp.mean(moved * moved, axis=0, keepdims=True) + EPSILON)
    return moved * inv_std, inv_std


def norm_backward(upstream, normed, inv_std, gain):
    scaled = upstream * gain
    mean_one = jnp.mean(scaled, axis=0, keepdims=True)
    mean_two = jnp.mean(scaled * normed, axis=0, keepdims=True)
    return inv_std * (scaled - mean_one - normed * mean_two)


def row_sums(values):
    return jnp.sum(values, axis=1, keepdims=True)


def columns(parts, lanes):
    lane = lax.broadcasted_iota(jnp.int32, (parts[0].shape[0], lanes), 1)
    total = jnp.zeros((parts[0].shape[0], lanes), F32)
    for index, part in enumerate(parts):
        total = jnp.where(lane == index, part, total)
    return total


def piece_copies(info, pieces, held, sems):
    first = pl.multiple_of(info[4] * HALF, HALF)
    second = pl.multiple_of((1 - info[4]) * HALF, HALF)
    copies, taken = [], 0
    for slot in range(SHARDS):
        targets = [held.at[slot]]
        if pieces[taken].shape[0] == HALF:
            targets = [held.at[slot, pl.ds(first, HALF)], held.at[slot, pl.ds(second, HALF)]]
        copies.append(
            tuple(
                pltpu.make_async_copy(pieces[taken + k], target, sems.at[2 * slot + k])
                for k, target in enumerate(targets)
            )
        )
        taken += len(targets)
    return tuple(copies)


def load_pieces(step, order, chunks):
    @pl.when(step == 0)
    def start():
        for slot in order:
            for chunk in chunks:
                for copy in chunk[slot]:
                    copy.start()

    for index, slot in enumerate(order):

        @pl.when(step == index)
        def wait():
            for chunk in chunks:
                for copy in chunk[slot]:
                    copy.wait()


def attention_forward_kernel(
    count, info, x_ref, col_ref, bqv_ref, *refs
):
    step = pl.program_id(0)
    pieces, (a1_ref, p_ref, soft_ref, o_ref, h_ref, held, sems) = refs[:count], refs[count:]
    copies = piece_copies(info, pieces, held, sems)
    load_pieces(step, range(SHARDS), (copies,))

    @pl.when(step == 0)
    def first():
        col = col_ref[...].reshape(D, 8)
        values = x_ref[...].astype(F32)
        normed, _ = normalize(values)
        a1_ref[...] = (
            normed * col[:, GAIN1 : GAIN1 + 1] + col[:, SHIFT1 : SHIFT1 + 1]
        ).astype(BF16)
        h_ref[...] = values + col[:, BIAS_OUT : BIAS_OUT + 1]

    bias = bqv_ref[step]
    projected = matmul(held[step, :QKV], a1_ref[...])
    queries = (projected[:FEATS] + bias[:, 0:1]).astype(BF16)
    keys = projected[FEATS : 2 * FEATS].astype(BF16)
    values = (projected[2 * FEATS :] + bias[:, 1:2]).astype(BF16)
    p_ref[0, :FEATS] = queries
    p_ref[0, FEATS : 2 * FEATS] = keys
    p_ref[0, 2 * FEATS :] = values
    scaled = queries * SCALE
    for head in range(HEADS_SHARD):
        rows = slice(head * HD, (head + 1) * HD)
        scores = matmul(keys[rows], scaled[rows], 0, 0)
        exps = jnp.exp(scores - jnp.max(scores, axis=0, keepdims=True))
        soft = exps * (1.0 / jnp.sum(exps, axis=0, keepdims=True))
        soft = soft.astype(BF16)
        soft_ref[0, head] = soft
        o_ref[0, rows] = matmul(values[rows], soft).astype(BF16)
    h_ref[...] += matmul(held[step, QKV:], o_ref[0], 0, 0)


def mlp_forward_kernel(
    counts, info, h_ref, col_ref, b1_ref, *refs
):
    step = pl.program_id(0)
    pieces_one, pieces_two, refs = refs[:counts[0]], refs[counts[0]:sum(counts)], refs[sum(counts):]
    a2_ref, u_ref, slope_ref, y_ref, held_one, held_two, a2_rows, total, sems_one, sems_two = refs
    copies_one = piece_copies(info, pieces_one, held_one, sems_one)
    copies_two = piece_copies(info, pieces_two, held_two, sems_two)
    load_pieces(step, range(SHARDS), (copies_one, copies_two))

    @pl.when(step == 0)
    def first():
        col = col_ref[...].reshape(D, 8)
        normed, _ = normalize(h_ref[...])
        scaled = normed * col[:, GAIN2 : GAIN2 + 1] + col[:, SHIFT2 : SHIFT2 + 1]
        a2_ref[...] = scaled.astype(BF16)
        a2_rows[...] = scaled.T.astype(BF16)
        total[...] = jnp.zeros_like(total)

    inner = matmul(a2_rows[...], held_one[step]) + b1_ref[step]
    phi = 0.5 + 0.5 * lax.erf(inner * 0.7071067811865476)
    density = 0.3989422804014327 * jnp.exp(-0.5 * inner * inner)
    active = (inner * phi).astype(BF16)
    u_ref[0] = active
    slope_ref[0] = (phi + inner * density).astype(BF16)
    total[...] += matmul(active, held_two[step])

    @pl.when(step == SHARDS - 1)
    def last():
        col = col_ref[...].reshape(D, 8)
        y_ref[...] = h_ref[...] + total[...].T + col[:, BIAS_FC2 : BIAS_FC2 + 1]


def mlp_backward_kernel(
    last, counts, info, gy_ref, h_ref, a2_ref, col_ref, u_ref, slope_ref, *refs
):
    step = pl.program_id(0)
    if last:
        before_ref, *refs = refs
    pieces_one, pieces_two, refs = refs[:counts[0]], refs[counts[0]:sum(counts)], refs[sum(counts):]
    if last:
        gh_ref, dcol_ref, *refs = refs
    else:
        after_ref, *refs = refs
    grad_one, grad_two, db1_ref, held_one, held_two, gy_rows, total, sems_one, sems_two = refs
    copies_one = piece_copies(info, pieces_one, held_one, sems_one)
    copies_two = piece_copies(info, pieces_two, held_two, sems_two)
    load_pieces(step, BACK_ORDER[2:] if last else BACK_ORDER[:2], (copies_two, copies_one))

    @pl.when(step == 0)
    def first():
        gy_rows[...] = gy_ref[...].astype(F32).T.astype(BF16)
        total[...] = before_ref[...] if last else jnp.zeros_like(total)

    slot = info[(7 if last else 5) + step]
    d_active = matmul(gy_rows[...], held_two[slot], 1, 1)
    d_inner = d_active * slope_ref[0].astype(F32)
    rounded = d_inner.astype(BF16)
    db1_ref[step] = jnp.sum(rounded.astype(F32), axis=0, keepdims=True)
    grad_two[0] = matmul(u_ref[0], gy_rows[...], 0, 0).astype(BF16)
    grad_one[0] = matmul(a2_ref[...], rounded).astype(BF16)
    total[...] += matmul(rounded, held_one[slot], 1, 1)

    @pl.when(step == 1)
    def end():
        if not last:
            after_ref[...] = total[...]
            return
        col = col_ref[...].reshape(D, 8)
        normed, inv_std = normalize(h_ref[...])
        d_mid = total[...].T
        upstream = gy_ref[...].astype(F32)
        d_hidden = upstream + norm_backward(d_mid, normed, inv_std, col[:, GAIN2 : GAIN2 + 1])
        gh_ref[...] = d_hidden
        dcol_ref[...] = columns(
            [row_sums(d_mid * normed), row_sums(d_mid), row_sums(d_hidden), row_sums(upstream)], 8
        )


def attention_backward_kernel(
    last, count, info, gh_ref, x_ref, a1_ref, col_ref, p_ref, soft_ref, o_ref, *refs
):
    step = pl.program_id(0)
    if last:
        before_ref, *refs = refs
    pieces, refs = refs[:count], refs[count:]
    if last:
        gx_ref, dcol_ref, *refs = refs
    else:
        after_ref, *refs = refs
    grad_ref, dbqv_ref, held, gh_rounded, g_p, total, sems = refs
    copies = piece_copies(info, pieces, held, sems)
    load_pieces(step, BACK_ORDER[2:] if last else BACK_ORDER[:2], (copies,))

    @pl.when(step == 0)
    def first():
        gh_rounded[...] = gh_ref[...].astype(BF16)
        total[...] = before_ref[...] if last else jnp.zeros_like(total)

    slot = info[(7 if last else 5) + step]
    d_attended = matmul(held[slot, QKV:], gh_rounded[...]).astype(BF16)
    grad_ref[0, QKV:] = matmul(o_ref[0], gh_rounded[...], 1, 1).astype(BF16)
    for head in range(HEADS_SHARD):
        rows = slice(head * HD, (head + 1) * HD)
        queries = p_ref[0, rows]
        keys = p_ref[0, FEATS + head * HD : FEATS + (head + 1) * HD]
        values = p_ref[0, 2 * FEATS + head * HD : 2 * FEATS + (head + 1) * HD]
        soft = soft_ref[0, head]
        d_att = d_attended[rows]
        delta = jnp.sum(
            d_att.astype(F32) * o_ref[0, rows].astype(F32), axis=0, keepdims=True
        )
        d_soft = matmul(values, d_att, 0, 0)
        d_scores = (soft.astype(F32) * (d_soft - delta)).astype(BF16)
        g_p[rows] = (matmul(keys, d_scores) * SCALE).astype(BF16)
        g_p[FEATS + head * HD : FEATS + (head + 1) * HD] = (
            matmul(queries, d_scores, 1, 1) * SCALE
        ).astype(BF16)
        g_p[2 * FEATS + head * HD : 2 * FEATS + (head + 1) * HD] = matmul(
            d_att, soft, 1, 1
        ).astype(BF16)
    d_projected = g_p[...]
    grad_ref[0, :QKV] = matmul(d_projected, a1_ref[...], 1, 1).astype(BF16)
    total[...] += matmul(d_projected, held[slot, :QKV], 0, 0)
    dbqv_ref[step] = columns(
        [row_sums(d_projected[:FEATS].astype(F32)), row_sums(d_projected[2 * FEATS :].astype(F32))],
        8,
    )

    @pl.when(step == 1)
    def end():
        if not last:
            after_ref[...] = total[...]
            return
        col = col_ref[...].reshape(D, 8)
        normed, inv_std = normalize(x_ref[...].astype(F32))
        d_first = total[...].T
        gx_ref[...] = gh_ref[...] + norm_backward(
            d_first, normed, inv_std, col[:, GAIN1 : GAIN1 + 1]
        )
        dcol_ref[...] = columns([row_sums(d_first * normed), row_sums(d_first)], 8)


def whole(shape):
    return pl.BlockSpec(shape, lambda i, info: (0,) * len(shape))


def by_step(shape):
    return pl.BlockSpec((1,) + shape, lambda i, info: (i,) + (0,) * len(shape))


def by_slot(shape, last):
    first = 7 if last else 5
    return pl.BlockSpec((1,) + shape, lambda i, info: (info[first + i],) + (0,) * len(shape))


PIECE = [pl.BlockSpec(memory_space=pltpu.HBM)]
COPY_SEMS = pltpu.SemaphoreType.DMA((2 * SHARDS,))
HELD = pltpu.VMEM((SHARDS, D, D), BF16)


def of(shape, dtype=BF16):
    return jax.ShapeDtypeStruct(shape, dtype)


def run(kernel, name, steps, info, operands, in_specs, outs, out_specs, scratch, flops):
    return pl.pallas_call(
        kernel,
        name=name,
        out_shape=outs,
        grid_spec=pltpu.PrefetchScalarGridSpec(
            num_scalar_prefetch=1,
            grid=(steps,),
            in_specs=in_specs,
            out_specs=out_specs,
            scratch_shapes=scratch,
        ),
        compiler_params=pltpu.CompilerParams(
            vmem_limit_bytes=VMEM_LIMIT, dimension_semantics=("arbitrary",)
        ),
        cost_estimate=pl.CostEstimate(flops=flops * 16, bytes_accessed=2**28, transcendentals=0),
    )(info, *operands)


STREAM = (D, FRAMES)
ROWS = (FRAMES, D)
COLS = (SHARDS, FEATS, 8)
ATT_FLOPS = 2 * FRAMES * D * (4 * D + 2 * FRAMES)
MLP_FLOPS = 4 * FRAMES * D * SHARDS * FF_SHARD


def attention_forward(info, x, col, bqv, chunk):
    return run(
        functools.partial(attention_forward_kernel, len(chunk)), "attention_forward", SHARDS, info, (x, col, bqv, *chunk),
        [whole(STREAM), whole(COLS), whole((SHARDS, FEATS, 2))] + PIECE * len(chunk),
        [
            of(STREAM), of((SHARDS, QKV, FRAMES)), of((SHARDS, HEADS_SHARD, FRAMES, FRAMES)),
            of((SHARDS, FEATS, FRAMES)), of(STREAM, F32),
        ],
        [
            whole(STREAM), by_step((QKV, FRAMES)), by_step((HEADS_SHARD, FRAMES, FRAMES)),
            by_step((FEATS, FRAMES)), whole(STREAM),
        ],
        [HELD, COPY_SEMS],
        ATT_FLOPS,
    )


def mlp_forward(info, h, col, b1, chunk_one, chunk_two):
    return run(
        functools.partial(mlp_forward_kernel, (len(chunk_one), len(chunk_two))), "mlp_forward", SHARDS, info, (h, col, b1, *chunk_one, *chunk_two),
        [whole(STREAM), whole(COLS), whole((SHARDS, 1, FF_SHARD))] + PIECE * len(chunk_one + chunk_two),
        [of(STREAM), of((SHARDS, FRAMES, FF_SHARD)), of((SHARDS, FRAMES, FF_SHARD)), of(STREAM, F32)],
        [whole(STREAM), by_step((FRAMES, FF_SHARD)), by_step((FRAMES, FF_SHARD)), whole(STREAM)],
        [HELD, HELD, pltpu.VMEM(ROWS, BF16), pltpu.VMEM(ROWS, F32), COPY_SEMS, COPY_SEMS],
        MLP_FLOPS,
    )


def mlp_backward(info, gy, h, a2, col, u, slope, before, chunk_one, chunk_two):
    last = before is not None
    carried = (before,) if last else ()
    ends = [of(STREAM, F32), of((D, 8), F32)] if last else [of(ROWS, F32)]
    return run(
        functools.partial(mlp_backward_kernel, last, (len(chunk_one), len(chunk_two))), "mlp_backward", 2, info,
        (gy, h, a2, col, u, slope, *carried, *chunk_one, *chunk_two),
        [
            whole(STREAM), whole(STREAM), whole(STREAM), whole(COLS),
            by_slot((FRAMES, FF_SHARD), last), by_slot((FRAMES, FF_SHARD), last),
        ]
        + [whole(ROWS)] * len(carried)
        + PIECE * len(chunk_one + chunk_two),
        ends + [of((2, D, D)), of((2, D, D)), of((2, 1, FF_SHARD), F32)],
        [whole(end.shape) for end in ends]
        + [by_step((D, D)), by_step((D, D)), whole((2, 1, FF_SHARD))],
        [HELD, HELD, pltpu.VMEM(ROWS, BF16), pltpu.VMEM(ROWS, F32), COPY_SEMS, COPY_SEMS],
        MLP_FLOPS,
    )


def attention_backward(info, gh, x, a1, col, p, soft, o, before, chunk):
    last = before is not None
    carried = (before,) if last else ()
    ends = [of(STREAM, F32), of((D, 8), F32)] if last else [of(ROWS, F32)]
    return run(
        functools.partial(attention_backward_kernel, last, len(chunk)), "attention_backward", 2, info,
        (gh, x, a1, col, p, soft, o, *carried, *chunk),
        [
            whole(STREAM), whole(STREAM), whole(STREAM), whole(COLS),
            by_slot((QKV, FRAMES), last), by_slot((HEADS_SHARD, FRAMES, FRAMES), last),
            by_slot((FEATS, FRAMES), last),
        ]
        + [whole(ROWS)] * len(carried)
        + PIECE * len(chunk),
        ends + [of((2, D, D)), of((2, FEATS, 8), F32)],
        [whole(end.shape) for end in ends] + [by_step((D, D)), whole((2, FEATS, 8))],
        [HELD, pltpu.VMEM(STREAM, BF16), pltpu.VMEM((QKV, FRAMES), BF16), pltpu.VMEM(ROWS, F32), COPY_SEMS],
        ATT_FLOPS,
    )


def tie(groups):
    return lax.optimization_barrier(groups)


def flip(block, axis, bit):
    size = lax.axis_size(axis)
    return lax.ppermute(block, axis, [(i, i ^ bit) for i in range(size)])


def added(left, right):
    return (left.astype(F32) + right.astype(F32)).astype(BF16)


def with_rows(blocks, small):
    pad = ((0, 0), (0, 16 - small.shape[1]), (0, blocks.shape[2] - small.shape[2]))
    return jnp.concatenate([blocks, jnp.pad(small.astype(BF16), pad)], axis=1)


def by_bits(slots, shard):
    odd = shard % 2 == 1
    high = shard >= 2
    first, second, third, fourth = slots
    first, second = jnp.where(odd, second, first), jnp.where(odd, first, second)
    third, fourth = jnp.where(odd, fourth, third), jnp.where(odd, third, fourth)
    return jnp.stack(
        [
            jnp.where(high, third, first), jnp.where(high, fourth, second),
            jnp.where(high, first, third), jnp.where(high, second, fourth),
        ]
    )


def rows_of(value, place, parts):
    size = value.shape[-2] // parts
    return lax.dynamic_slice_in_dim(value, place * size, size, axis=value.ndim - 2)


class Chain:
    def start(self, send):
        self.arrived = flip(send, "tensor", 1)

    def cores(self, keep):
        self.value = added(keep, self.arrived)

    def scatter(self):
        parts = lax.axis_size("dp")
        rows = self.value.shape[-2] // parts
        split = self.value.reshape(-1, parts, rows, D)
        split = jnp.swapaxes(split, 0, 1)
        total = lax.psum_scatter(split, "dp", scatter_dimension=0, tiled=False)
        self.value = total if self.value.ndim == 3 else total[0]

    def send_y(self):
        self.kept, self.arrived = self.value[1], flip(self.value[0], "tensor", 2)

    def send_x(self, first, second):
        section = lax.axis_index("section")
        self.kept = jnp.where(section == 0, first.value, second.value)
        self.arrived = flip(jnp.where(section == 0, second.value, first.value), "section", 1)

    def fold(self):
        self.value = added(self.kept, self.arrived)

    def split(self):
        self.value = self.value.reshape(lax.axis_size("dp"), -1, D)

    def send_half(self, bit):
        mine = ((lax.axis_index("dp") & bit) != 0).astype(jnp.int32)
        blocks = self.value.reshape(-1, 2, *self.value.shape[1:])
        self.kept = lax.dynamic_index_in_dim(blocks, mine, 1, keepdims=False)
        self.arrived = flip(
            lax.dynamic_index_in_dim(blocks, 1 - mine, 1, keepdims=False), "dp", bit
        )

    def send_back(self, bit):
        self.arrived = flip(self.value, "dp", bit)

    def join(self, bit):
        upper = (lax.axis_index("dp") & bit) != 0
        value = jnp.where(
            upper,
            jnp.stack([self.arrived, self.value], axis=1),
            jnp.stack([self.value, self.arrived], axis=1),
        )
        self.value = value.reshape(-1, *value.shape[2:])


def tied(chains, *others):
    values = tie((tuple(chain.value for chain in chains), others))
    for chain, value in zip(chains, values[0]):
        chain.value = value
    return values[1]


def body(ends_in, ln_gain, ln_shift, w_qkv, b_qv, w_out, b_out, w_fc1, b_fc1, w_fc2, b_fc2):
    section = lax.axis_index("section")
    shard = lax.axis_index("tensor")
    zhalf = lax.axis_index("dp") % 2
    clips = ends_in.shape[1] // FRAMES
    info = jnp.stack(
        [shard, shard ^ 1, shard ^ 2, shard ^ 3, zhalf] + [jnp.int32(k) for k in BACK_ORDER]
    ).astype(jnp.int32)

    owned = [
        jnp.concatenate([w_qkv[0].transpose(1, 2, 0).reshape(QKV, D), w_out[0]], axis=0),
        w_fc1[0],
        w_fc2[0],
    ]
    nears = [rows_of(own, zhalf, 2) for own in owned]
    fars = [rows_of(own, 1 - zhalf, 2) for own in owned]
    beyond_a = flip(nears[0], "section", 1)

    small = jnp.concatenate(
        [ln_gain[0], ln_shift[0], b_qv[0], b_out, b_fc2, b_fc1.reshape(SHARDS, FEATS)], axis=0
    )
    ends = ends_in[0].T.reshape(FEATS, clips, FRAMES).transpose(1, 0, 2)
    ends = with_rows(ends, jnp.broadcast_to(small, (clips,) + small.shape))
    ends = lax.all_to_all(ends, ("section", "tensor"), split_axis=0, concat_axis=0, tiled=True)
    small = ends[:, FEATS : FEATS + 12, :FEATS].reshape(2, SHARDS, 12, FEATS).astype(F32)
    ends = ends[:, :FEATS].reshape(2, D, FRAMES)
    cols = jnp.transpose(small[:, :, :8], (0, 1, 3, 2))
    slots = by_bits([small[:, index] for index in range(SHARDS)], shard)
    bqvs = jnp.transpose(slots[:, :, 4:6], (1, 0, 3, 2))
    b1s = jnp.transpose(slots[:, :, 8:], (1, 0, 2, 3)).reshape(2, SHARDS, 1, FF_SHARD)

    def layers(own, other):
        return jnp.where(section == 0, own, other), jnp.where(section == 0, other, own)

    def over_y(block):
        return flip(block, "tensor", 2)

    def chunk_of(own, there):
        return tuple(
            part for pair in (own, there) for parts in (pair, [flip(x, "tensor", 1) for x in pair])
            for part in parts
        )

    n_dp = lax.axis_size("dp")
    beyond_a, near_one, own_two = tie((beyond_a, nears[1], owned[2]))
    beyond_one = flip(near_one, "section", 1)
    beyond_two = flip(own_two, "section", 1)
    near_a = layers(nears[0], beyond_a)
    far_a = layers(fars[0], flip(beyond_a, "dp", 1))
    there_a = over_y(near_a[0])
    there_a, beyond_one = tie((there_a, beyond_one))
    away_a = flip(there_a, "dp", 1)
    near_one = layers(nears[1], beyond_one)
    beyond_far_one = flip(beyond_one, "dp", 1)
    there_one = over_y(near_one[0])

    def attend(layer, stream, chunk):
        return attention_forward(info, stream, cols[layer], bqvs[layer], chunk)

    def feed(layer, h, chunk_one, chunk_two):
        return mlp_forward(info, h, cols[layer], b1s[layer], chunk_one, chunk_two)

    chunks = [[chunk_of((near_a[0], far_a[0]), (there_a, away_a))], []]
    stream = ends[0]
    a1, p, soft, o, h = attend(0, stream, chunks[0][0])
    h, beyond_two, there_one, beyond_far_one, late_a, late_far_a, late_one = tie(
        (h, beyond_two, there_one, beyond_far_one, near_a[1], far_a[1], near_one[1])
    )
    near_two = layers(nears[2], rows_of(beyond_two, zhalf, 2))
    far_two = layers(fars[2], rows_of(beyond_two, 1 - zhalf, 2))
    there_two = over_y(near_two[0])
    far_one = layers(fars[1], beyond_far_one)
    away_one = flip(there_one, "dp", 1)
    chunks[0].append(chunk_of((near_one[0], far_one[0]), (there_one, away_one)))
    there_two, late_a, late_one, late_two = tie((there_two, late_a, late_one, near_two[1]))
    chunks[0].append(chunk_of((near_two[0], far_two[0]), (there_two, flip(there_two, "dp", 1))))
    there_a, there_one, there_two = over_y(late_a), over_y(late_one), over_y(late_two)
    away_a = flip(there_a, "dp", 1)
    a2, u, slope, y = feed(0, h, *chunks[0][1:])
    stored = [(stream, a1, p, soft, o, h, a2, u, slope)]
    stream, there_a, away_a, there_one, there_two, late_a, late_far_a = tie(
        (y, there_a, away_a, there_one, there_two, late_a, late_far_a)
    )
    chunks[1].append(chunk_of((late_a, late_far_a), (there_a, away_a)))
    away_one, away_two = flip(there_one, "dp", 1), flip(there_two, "dp", 1)
    a1, p, soft, o, h = attend(1, stream, chunks[1][0])
    h, late = tie(
        (
            h,
            (late_one, far_one[1], there_one, away_one, late_two, far_two[1], there_two, away_two),
        )
    )
    chunks[1].append(chunk_of(late[0:2], late[2:4]))
    chunks[1].append(chunk_of(late[4:6], late[6:8]))
    a2, u, slope, y = feed(1, h, *chunks[1][1:])
    stored.append((stream, a1, p, soft, o, h, a2, u, slope))
    stream = y

    upstream = ends[1]
    chains = [[Chain() for _ in range(3)] for _ in range(2)]
    smalls = [None, None]
    ends_of = [None, None]
    late_a, late_one, late_two = chains[1]
    last_a, last_one, last_two = chains[0]
    for layer in (1, 0):
        chunk_a, chunk_one, chunk_two = chunks[layer]
        x, a1, p, soft, o, h, a2, u, slope = stored[layer]
        chain_a, chain_one, chain_two = chains[layer]
        after, send_one, send_two, db1_sent = mlp_backward(
            info, upstream, h, a2, cols[layer], u, slope, None, chunk_one, chunk_two
        )
        chain_two.start(send_two)
        chain_one.start(send_one)
        gh, dcol_two, keep_one, keep_two, db1_kept = mlp_backward(
            info, upstream, h, a2, cols[layer], u, slope, after, chunk_one, chunk_two
        )
        chain_two.cores(keep_two)
        chain_one.cores(keep_one)
        if layer == 0:
            late_a.fold()
            (gh,) = tied((late_a, last_two, last_one, late_one), gh)
            late_a.scatter()
            last_two.send_y()
            last_one.send_y()
        else:
            (gh,) = tied((late_two, late_one), gh)
            late_one.scatter()
            late_two.send_y()
        after, send_a, dbqv_sent = attention_backward(
            info, gh, x, a1, cols[layer], p, soft, o, None, chunk_a
        )
        chain_a.start(send_a)
        upstream, dcol_one, keep_a, dbqv_kept = attention_backward(
            info, gh, x, a1, cols[layer], p, soft, o, after, chunk_a
        )
        chain_a.cores(keep_a)
        if layer == 1:
            late_two.fold()
            (upstream,) = tied((late_two, late_a), upstream)
            late_two.scatter()
            late_a.send_y()
        else:
            last_two.fold()
            (upstream,) = tied((last_two, last_a, late_two), upstream)
            last_two.scatter()
            last_a.send_y()
        ends_of[layer] = (db1_kept, db1_sent, dbqv_kept, dbqv_sent, dcol_one, dcol_two)

    upstream, ends_of = tie((upstream, ends_of))
    for layer in range(2):
        db1_kept, db1_sent, dbqv_kept, dbqv_sent, dcol_one, dcol_two = ends_of[layer]
        db1 = by_bits([db1_kept[1], db1_sent[1], db1_kept[0], db1_sent[0]], shard)
        dbqv = by_bits([dbqv_kept[1], dbqv_sent[1], dbqv_kept[0], dbqv_sent[0]], shard)
        dcol = jnp.concatenate(
            [
                dcol_one[:, 0:1], dcol_two[:, 0:1], dcol_one[:, 1:2], dcol_two[:, 1:2],
                dbqv[:, :, 0:2].reshape(D, 2), dcol_two[:, 2:4],
            ],
            axis=1,
        )
        smalls[layer] = jnp.concatenate(
            [
                dcol.reshape(SHARDS, FEATS, 8).transpose(0, 2, 1),
                db1.reshape(SHARDS, SHARDS, FEATS),
            ],
            axis=1,
        )

    result = jnp.stack([upstream.astype(BF16), stream.astype(BF16)])
    result = with_rows(
        result.reshape(2 * SHARDS, FEATS, FRAMES), jnp.stack(smalls).reshape(-1, 12, FEATS)
    )

    late_one.send_y()
    bits = [1 << k for k in range(n_dp.bit_length() - 1)]

    last_one.fold()
    result, last_a.arrived = tied((last_one, late_a), result, last_a.arrived)
    last_one.scatter()
    result = lax.all_to_all(result, ("section", "tensor"), split_axis=0, concat_axis=0, tiled=True)

    last_a.fold()
    late_one.fold()
    tied((last_a, late_one, last_two))
    last_a.split()
    last_a.send_half(bits[0])
    pair_two, pair_one, pair_a = Chain(), Chain(), Chain()
    pair_two.send_x(last_two, late_two)

    last_a.fold()
    pair_two.fold()
    (result,) = tied((last_a, pair_two), result)
    pair_two.value = pair_two.value[None]
    for bit in bits[1:]:
        last_a.send_half(bit)
        if bit != bits[-1]:
            last_a.fold()
    pair_two.send_back(bits[-1])

    last_a.fold()
    last_a.value = last_a.value[0]
    pair_two.join(bits[-1])
    for bit in bits[-2:0:-1]:
        pair_two.send_back(bit)
        pair_two.join(bit)
    (result,) = tied((last_a, pair_two, last_one), result)
    pair_one.send_x(last_one, late_one)
    pair_a.send_x(last_a, late_a)
    pair_two.send_back(bits[0])
    small_sum = result[:, FEATS : FEATS + 12, :FEATS].astype(F32).sum(axis=0)

    for pair in (pair_one, pair_a):
        pair.fold()
        pair.value = pair.value[None]
    pair_two.join(bits[0])
    result, small_sum = tied((pair_one, pair_a, pair_two), result, small_sum)
    small_sum += flip(small_sum, "dp", bits[0])
    for bit in bits[:0:-1]:
        for pair in (pair_one, pair_a):
            pair.send_back(bit)
        for pair in (pair_one, pair_a):
            pair.join(bit)
    result, small_sum = tied((pair_one, pair_a), result, small_sum)
    for bit in bits[1:]:
        small_sum += flip(small_sum, "dp", bit)
    for pair in (pair_one, pair_a):
        pair.send_back(bits[0])
    result = result[:, :FEATS].transpose(1, 0, 2).reshape(FEATS, clips * FRAMES).T.astype(F32)
    for pair in (pair_one, pair_a):
        pair.join(bits[0])
    for pair in (pair_two, pair_one, pair_a):
        pair.value = pair.value.reshape(D, D)

    grad_a, grad_one, grad_two = [pair.value.astype(F32) for pair in (pair_a, pair_one, pair_two)]
    return (
        result[None],
        small_sum[None, 0:2],
        small_sum[None, 2:4],
        grad_a[:QKV].reshape(3, FEATS, D).transpose(2, 0, 1)[None],
        small_sum[None, 4:6],
        grad_a[QKV:][None],
        small_sum[6:7],
        grad_one[None],
        small_sum[8:12].reshape(1, FF_SHARD),
        grad_two[None],
        small_sum[7:8],
    )


def solution(mesh):
    placed = (
        P("section", "dp", "tensor"),
        P("section", None, "tensor"),
        P("section", None, "tensor"),
        P("section", None, None, "tensor"),
        P("section", None, "tensor"),
        P("section", "tensor", None),
        P("section", "tensor"),
        P("section", None, "tensor"),
        P("section", "tensor"),
        P("section", "tensor", None),
        P("section", "tensor"),
    )
    return jax.shard_map(
        body, mesh=mesh, in_specs=placed, out_specs=placed, check_vma=False
    )
```

```python
import functools

import jax
import jax.numpy as jnp
from jax import lax
from jax.experimental import pallas as pl
from jax.experimental.pallas import tpu as pltpu
from jax.sharding import PartitionSpec as P

D = 768
HD = 64
FRAMES = 448
SHARDS = 4
HEADS_SHARD = 3
FEATS = HEADS_SHARD * HD
QKV = 3 * FEATS
FF_SHARD = 768
HALF = D // 2
EPSILON = 1e-05
SCALE = float(HD) ** (-0.5)
VMEM_LIMIT = 48 * 1024 * 1024
GAIN1, GAIN2, SHIFT1, SHIFT2, BIAS_Q, BIAS_V, BIAS_OUT, BIAS_FC2 = range(8)
BACK_ORDER = (3, 1, 2, 0)
F32 = jnp.float32
BF16 = jnp.bfloat16


def matmul(left, right, left_dim=1, right_dim=0):
    return lax.dot_general(
        left, right, (((left_dim,), (right_dim,)), ((), ())), preferred_element_type=F32
    )


def normalize(values):
    center = jnp.mean(values, axis=0, keepdims=True)
    moved = values - center
    inv_std = lax.rsqrt(jnp.mean(moved * moved, axis=0, keepdims=True) + EPSILON)
    return moved * inv_std, inv_std


def norm_backward(upstream, normed, inv_std, gain):
    scaled = upstream * gain
    mean_one = jnp.mean(scaled, axis=0, keepdims=True)
    mean_two = jnp.mean(scaled * normed, axis=0, keepdims=True)
    return inv_std * (scaled - mean_one - normed * mean_two)


def row_sums(values):
    return jnp.sum(values, axis=1, keepdims=True)


def columns(parts):
    rows = next(iter(parts.values())).shape[0]
    lane = lax.broadcasted_iota(jnp.int32, (rows, 8), 1)
    total = jnp.zeros((rows, 8), F32)
    for index, part in parts.items():
        total = jnp.where(lane == index, part, total)
    return total


def piece_copies(info, pieces, held, sems):
    first = pl.multiple_of(info[4] * HALF, HALF)
    second = pl.multiple_of((1 - info[4]) * HALF, HALF)
    copies, taken = [], 0
    for slot in range(SHARDS):
        targets = [held.at[slot]]
        if pieces[taken].shape[0] == HALF:
            targets = [held.at[slot, pl.ds(first, HALF)], held.at[slot, pl.ds(second, HALF)]]
        copies.append(
            tuple(
                pltpu.make_async_copy(pieces[taken + k], target, sems.at[2 * slot + k])
                for k, target in enumerate(targets)
            )
        )
        taken += len(targets)
    return tuple(copies)


def load_pieces(step, order, chunks):
    @pl.when(step == 0)
    def start():
        for slot in order:
            for chunk in chunks:
                for copy in chunk[slot]:
                    copy.start()

    for index, slot in enumerate(order):

        @pl.when(step == index)
        def wait():
            for chunk in chunks:
                for copy in chunk[slot]:
                    copy.wait()


def attention_forward_kernel(
    count, info, x_ref, col_ref, *refs
):
    step = pl.program_id(0)
    pieces, (a1_ref, p_ref, soft_ref, o_ref, h_ref, held, sems) = refs[:count], refs[count:]
    copies = piece_copies(info, pieces, held, sems)
    load_pieces(step, range(SHARDS), (copies,))

    @pl.when(step == 0)
    def first():
        col = col_ref[...].reshape(D, 8)
        values = x_ref[...].astype(F32)
        normed, _ = normalize(values)
        a1_ref[...] = (
            normed * col[:, GAIN1 : GAIN1 + 1] + col[:, SHIFT1 : SHIFT1 + 1]
        ).astype(BF16)
        h_ref[...] = values + col[:, BIAS_OUT : BIAS_OUT + 1]

    bias = col_ref[info[step]]
    projected = matmul(held[step, :QKV], a1_ref[...])
    queries = (projected[:FEATS] + bias[:, BIAS_Q : BIAS_Q + 1]).astype(BF16)
    keys = projected[FEATS : 2 * FEATS].astype(BF16)
    values = (projected[2 * FEATS :] + bias[:, BIAS_V : BIAS_V + 1]).astype(BF16)
    p_ref[0, :FEATS] = queries
    p_ref[0, FEATS : 2 * FEATS] = keys
    p_ref[0, 2 * FEATS :] = values
    scaled = queries * SCALE
    for head in range(HEADS_SHARD):
        rows = slice(head * HD, (head + 1) * HD)
        scores = matmul(keys[rows], scaled[rows], 0, 0)
        exps = jnp.exp(scores - jnp.max(scores, axis=0, keepdims=True))
        soft = exps * (1.0 / jnp.sum(exps, axis=0, keepdims=True))
        soft = soft.astype(BF16)
        soft_ref[0, head] = soft
        o_ref[0, rows] = matmul(values[rows], soft).astype(BF16)
    h_ref[...] += matmul(held[step, QKV:], o_ref[0], 0, 0)


def mlp_forward_kernel(
    counts, info, h_ref, col_ref, b1_ref, *refs
):
    step = pl.program_id(0)
    pieces_one, pieces_two, refs = refs[:counts[0]], refs[counts[0]:sum(counts)], refs[sum(counts):]
    a2_ref, u_ref, slope_ref, y_ref, held_one, held_two, a2_rows, total, sems_one, sems_two = refs
    copies_one = piece_copies(info, pieces_one, held_one, sems_one)
    copies_two = piece_copies(info, pieces_two, held_two, sems_two)
    load_pieces(step, range(SHARDS), (copies_one, copies_two))

    @pl.when(step == 0)
    def first():
        col = col_ref[...].reshape(D, 8)
        normed, _ = normalize(h_ref[...])
        scaled = normed * col[:, GAIN2 : GAIN2 + 1] + col[:, SHIFT2 : SHIFT2 + 1]
        a2_ref[...] = scaled.astype(BF16)
        a2_rows[...] = scaled.T.astype(BF16)
        total[...] = jnp.zeros_like(total)

    inner = matmul(a2_rows[...], held_one[step]) + b1_ref[info[step]]
    phi = 0.5 + 0.5 * lax.erf(inner * 0.7071067811865476)
    density = 0.3989422804014327 * jnp.exp(-0.5 * inner * inner)
    active = (inner * phi).astype(BF16)
    u_ref[0] = active
    slope_ref[0] = (phi + inner * density).astype(BF16)
    total[...] += matmul(active, held_two[step])

    @pl.when(step == SHARDS - 1)
    def last():
        col = col_ref[...].reshape(D, 8)
        y_ref[...] = h_ref[...] + total[...].T + col[:, BIAS_FC2 : BIAS_FC2 + 1]


def mlp_backward_kernel(
    last, counts, info, gy_ref, h_ref, a2_ref, col_ref, u_ref, slope_ref, *refs
):
    step = pl.program_id(0)
    if last:
        before_ref, *refs = refs
    pieces_one, pieces_two, refs = refs[:counts[0]], refs[counts[0]:sum(counts)], refs[sum(counts):]
    if last:
        gh_ref, dcol_ref, *refs = refs
    else:
        after_ref, *refs = refs
    grad_one, grad_two, db1_ref, held_one, held_two, gy_rows, total, sems_one, sems_two = refs
    copies_one = piece_copies(info, pieces_one, held_one, sems_one)
    copies_two = piece_copies(info, pieces_two, held_two, sems_two)
    load_pieces(step, BACK_ORDER[2:] if last else BACK_ORDER[:2], (copies_two, copies_one))

    @pl.when(step == 0)
    def first():
        gy_rows[...] = gy_ref[...].astype(F32).T.astype(BF16)
        db1_ref[...] = jnp.zeros_like(db1_ref)
        total[...] = before_ref[...] if last else jnp.zeros_like(total)

    slot = info[(7 if last else 5) + step]
    d_active = matmul(gy_rows[...], held_two[slot], 1, 1)
    d_inner = d_active * slope_ref[0].astype(F32)
    rounded = d_inner.astype(BF16)
    db1_ref[info[slot]] = jnp.sum(rounded.astype(F32), axis=0, keepdims=True)
    grad_two[0] = matmul(u_ref[0], gy_rows[...], 0, 0).astype(BF16)
    grad_one[0] = matmul(a2_ref[...], rounded).astype(BF16)
    total[...] += matmul(rounded, held_one[slot], 1, 1)

    @pl.when(step == 1)
    def end():
        if not last:
            after_ref[...] = total[...]
            return
        col = col_ref[...].reshape(D, 8)
        normed, inv_std = normalize(h_ref[...])
        d_mid = total[...].T
        upstream = gy_ref[...].astype(F32)
        d_hidden = upstream + norm_backward(d_mid, normed, inv_std, col[:, GAIN2 : GAIN2 + 1])
        gh_ref[...] = d_hidden
        dcol_ref[...] = columns(
            {
                GAIN2: row_sums(d_mid * normed),
                SHIFT2: row_sums(d_mid),
                BIAS_OUT: row_sums(d_hidden),
                BIAS_FC2: row_sums(upstream),
            }
        ).reshape(COLS)


def attention_backward_kernel(
    last, count, info, gh_ref, x_ref, a1_ref, col_ref, p_ref, soft_ref, o_ref, *refs
):
    step = pl.program_id(0)
    if last:
        before_ref, *refs = refs
    pieces, refs = refs[:count], refs[count:]
    if last:
        gx_ref, dcol_ref, *refs = refs
    else:
        after_ref, *refs = refs
    grad_ref, dbqv_ref, held, gh_rounded, g_p, total, sems = refs
    copies = piece_copies(info, pieces, held, sems)
    load_pieces(step, BACK_ORDER[2:] if last else BACK_ORDER[:2], (copies,))

    @pl.when(step == 0)
    def first():
        gh_rounded[...] = gh_ref[...].astype(BF16)
        dbqv_ref[...] = jnp.zeros_like(dbqv_ref)
        total[...] = before_ref[...] if last else jnp.zeros_like(total)

    slot = info[(7 if last else 5) + step]
    d_attended = matmul(held[slot, QKV:], gh_rounded[...]).astype(BF16)
    grad_ref[0, QKV:] = matmul(o_ref[0], gh_rounded[...], 1, 1).astype(BF16)
    for head in range(HEADS_SHARD):
        rows = slice(head * HD, (head + 1) * HD)
        queries = p_ref[0, rows]
        keys = p_ref[0, FEATS + head * HD : FEATS + (head + 1) * HD]
        values = p_ref[0, 2 * FEATS + head * HD : 2 * FEATS + (head + 1) * HD]
        soft = soft_ref[0, head]
        d_att = d_attended[rows]
        delta = jnp.sum(
            d_att.astype(F32) * o_ref[0, rows].astype(F32), axis=0, keepdims=True
        )
        d_soft = matmul(values, d_att, 0, 0)
        d_scores = (soft.astype(F32) * (d_soft - delta)).astype(BF16)
        g_p[rows] = (matmul(keys, d_scores) * SCALE).astype(BF16)
        g_p[FEATS + head * HD : FEATS + (head + 1) * HD] = (
            matmul(queries, d_scores, 1, 1) * SCALE
        ).astype(BF16)
        g_p[2 * FEATS + head * HD : 2 * FEATS + (head + 1) * HD] = matmul(
            d_att, soft, 1, 1
        ).astype(BF16)
    d_projected = g_p[...]
    grad_ref[0, :QKV] = matmul(d_projected, a1_ref[...], 1, 1).astype(BF16)
    total[...] += matmul(d_projected, held[slot, :QKV], 0, 0)
    dbqv_ref[info[slot]] = columns(
        {
            BIAS_Q: row_sums(d_projected[:FEATS].astype(F32)),
            BIAS_V: row_sums(d_projected[2 * FEATS :].astype(F32)),
        }
    )

    @pl.when(step == 1)
    def end():
        if not last:
            after_ref[...] = total[...]
            return
        col = col_ref[...].reshape(D, 8)
        normed, inv_std = normalize(x_ref[...].astype(F32))
        d_first = total[...].T
        gx_ref[...] = gh_ref[...] + norm_backward(
            d_first, normed, inv_std, col[:, GAIN1 : GAIN1 + 1]
        )
        dcol_ref[...] = columns(
            {GAIN1: row_sums(d_first * normed), SHIFT1: row_sums(d_first)}
        ).reshape(COLS)


def whole(shape):
    return pl.BlockSpec(shape, lambda i, info: (0,) * len(shape))


def by_step(shape):
    return pl.BlockSpec((1,) + shape, lambda i, info: (i,) + (0,) * len(shape))


def by_slot(shape, last):
    first = 7 if last else 5
    return pl.BlockSpec((1,) + shape, lambda i, info: (info[first + i],) + (0,) * len(shape))


PIECE = [pl.BlockSpec(memory_space=pltpu.HBM)]
COPY_SEMS = pltpu.SemaphoreType.DMA((2 * SHARDS,))
HELD = pltpu.VMEM((SHARDS, D, D), BF16)


def of(shape, dtype=BF16):
    return jax.ShapeDtypeStruct(shape, dtype)


def run(kernel, name, steps, info, operands, in_specs, outs, out_specs, scratch, flops):
    return pl.pallas_call(
        kernel,
        name=name,
        out_shape=outs,
        grid_spec=pltpu.PrefetchScalarGridSpec(
            num_scalar_prefetch=1,
            grid=(steps,),
            in_specs=in_specs,
            out_specs=out_specs,
            scratch_shapes=scratch,
        ),
        compiler_params=pltpu.CompilerParams(
            vmem_limit_bytes=VMEM_LIMIT, dimension_semantics=("arbitrary",)
        ),
        cost_estimate=pl.CostEstimate(flops=flops * 16, bytes_accessed=2**28, transcendentals=0),
    )(info, *operands)


STREAM = (D, FRAMES)
ROWS = (FRAMES, D)
COLS = (SHARDS, FEATS, 8)
ATT_FLOPS = 2 * FRAMES * D * (4 * D + 2 * FRAMES)
MLP_FLOPS = 4 * FRAMES * D * SHARDS * FF_SHARD


def attention_forward(info, x, col, chunk):
    return run(
        functools.partial(attention_forward_kernel, len(chunk)), "attention_forward", SHARDS, info, (x, col, *chunk),
        [whole(STREAM), whole(COLS)] + PIECE * len(chunk),
        [
            of(STREAM), of((SHARDS, QKV, FRAMES)), of((SHARDS, HEADS_SHARD, FRAMES, FRAMES)),
            of((SHARDS, FEATS, FRAMES)), of(STREAM, F32),
        ],
        [
            whole(STREAM), by_step((QKV, FRAMES)), by_step((HEADS_SHARD, FRAMES, FRAMES)),
            by_step((FEATS, FRAMES)), whole(STREAM),
        ],
        [HELD, COPY_SEMS],
        ATT_FLOPS,
    )


def mlp_forward(info, h, col, b1, chunk_one, chunk_two):
    return run(
        functools.partial(mlp_forward_kernel, (len(chunk_one), len(chunk_two))), "mlp_forward", SHARDS, info, (h, col, b1, *chunk_one, *chunk_two),
        [whole(STREAM), whole(COLS), whole((SHARDS, 1, FF_SHARD))] + PIECE * len(chunk_one + chunk_two),
        [of(STREAM), of((SHARDS, FRAMES, FF_SHARD)), of((SHARDS, FRAMES, FF_SHARD)), of(STREAM, F32)],
        [whole(STREAM), by_step((FRAMES, FF_SHARD)), by_step((FRAMES, FF_SHARD)), whole(STREAM)],
        [HELD, HELD, pltpu.VMEM(ROWS, BF16), pltpu.VMEM(ROWS, F32), COPY_SEMS, COPY_SEMS],
        MLP_FLOPS,
    )


def mlp_backward(info, gy, h, a2, col, u, slope, before, chunk_one, chunk_two):
    last = before is not None
    carried = (before,) if last else ()
    ends = [of(STREAM, F32), of(COLS, F32)] if last else [of(ROWS, F32)]
    return run(
        functools.partial(mlp_backward_kernel, last, (len(chunk_one), len(chunk_two))), "mlp_backward", 2, info,
        (gy, h, a2, col, u, slope, *carried, *chunk_one, *chunk_two),
        [
            whole(STREAM), whole(STREAM), whole(STREAM), whole(COLS),
            by_slot((FRAMES, FF_SHARD), last), by_slot((FRAMES, FF_SHARD), last),
        ]
        + [whole(ROWS)] * len(carried)
        + PIECE * len(chunk_one + chunk_two),
        ends + [of((2, D, D)), of((2, D, D)), of((SHARDS, 1, FF_SHARD), F32)],
        [whole(end.shape) for end in ends]
        + [by_step((D, D)), by_step((D, D)), whole((SHARDS, 1, FF_SHARD))],
        [HELD, HELD, pltpu.VMEM(ROWS, BF16), pltpu.VMEM(ROWS, F32), COPY_SEMS, COPY_SEMS],
        MLP_FLOPS,
    )


def attention_backward(info, gh, x, a1, col, p, soft, o, before, chunk):
    last = before is not None
    carried = (before,) if last else ()
    ends = [of(STREAM, F32), of(COLS, F32)] if last else [of(ROWS, F32)]
    return run(
        functools.partial(attention_backward_kernel, last, len(chunk)), "attention_backward", 2, info,
        (gh, x, a1, col, p, soft, o, *carried, *chunk),
        [
            whole(STREAM), whole(STREAM), whole(STREAM), whole(COLS),
            by_slot((QKV, FRAMES), last), by_slot((HEADS_SHARD, FRAMES, FRAMES), last),
            by_slot((FEATS, FRAMES), last),
        ]
        + [whole(ROWS)] * len(carried)
        + PIECE * len(chunk),
        ends + [of((2, D, D)), of(COLS, F32)],
        [whole(end.shape) for end in ends] + [by_step((D, D)), whole(COLS)],
        [HELD, pltpu.VMEM(STREAM, BF16), pltpu.VMEM((QKV, FRAMES), BF16), pltpu.VMEM(ROWS, F32), COPY_SEMS],
        ATT_FLOPS,
    )


def tie(groups):
    return lax.optimization_barrier(groups)


def flip(block, axis, bit):
    size = lax.axis_size(axis)
    return lax.ppermute(block, axis, [(i, i ^ bit) for i in range(size)])


def added(left, right):
    return (left.astype(F32) + right.astype(F32)).astype(BF16)


def sum_kernel(left_ref, right_ref, *out_refs):
    for index, out_ref in enumerate(out_refs):
        place = index if len(out_refs) > 1 else Ellipsis
        out_ref[...] = added(left_ref[place], right_ref[place])


def summed(left, right, outs):
    rows = left.shape[-2]
    block = 384 if rows % 384 == 0 else rows
    spec = pl.BlockSpec((block, D), lambda i: (i, 0))
    pair = pl.BlockSpec((2, block, D), lambda i: (0, i, 0))
    return pl.pallas_call(
        sum_kernel,
        name="row_sums",
        grid=(rows // block,),
        in_specs=[pair if outs == 2 else spec] * 2,
        out_specs=[spec] * outs,
        out_shape=[jax.ShapeDtypeStruct((rows, D), BF16)] * outs,
        compiler_params=pltpu.CompilerParams(vmem_limit_bytes=VMEM_LIMIT),
        cost_estimate=pl.CostEstimate(flops=2**36, bytes_accessed=2**28, transcendentals=0),
    )(left, right)


def with_rows(blocks, small):
    pad = ((0, 0), (0, 16 - small.shape[1]), (0, blocks.shape[2] - small.shape[2]))
    return jnp.concatenate([blocks, jnp.pad(small.astype(BF16), pad)], axis=1)


def rows_of(value, place, parts):
    size = value.shape[-2] // parts
    return lax.dynamic_slice_in_dim(value, place * size, size, axis=value.ndim - 2)


class Chain:
    def start(self, send):
        self.arrived = flip(send, "tensor", 1)

    def cores(self, keep):
        self.value = summed(keep, self.arrived, 2)

    def scatter(self):
        parts = lax.axis_size("dp")
        both = self.value if isinstance(self.value, (list, tuple)) else [self.value]
        split = jnp.stack([value.reshape(parts, -1, D) for value in both], axis=1)
        total = lax.psum_scatter(split, "dp", scatter_dimension=0, tiled=False)
        self.value = total if len(both) == 2 else total[0]

    def send_y(self):
        self.kept, self.arrived = self.value[1], flip(self.value[0], "tensor", 2)

    def fold_rows(self):
        rows = self.kept.shape
        (total,) = summed(self.kept.reshape(-1, D), self.arrived.reshape(-1, D), 1)
        self.value = total.reshape(rows)

    def send_x(self, first, second):
        section = lax.axis_index("section")
        self.kept = jnp.where(section == 0, first.value, second.value)
        self.arrived = flip(jnp.where(section == 0, second.value, first.value), "section", 1)

    def fold(self):
        self.value = added(self.kept, self.arrived)

    def split(self):
        self.value = self.value.reshape(lax.axis_size("dp"), -1, D)

    def send_half(self, bit):
        mine = ((lax.axis_index("dp") & bit) != 0).astype(jnp.int32)
        blocks = self.value.reshape(-1, 2, *self.value.shape[1:])
        self.kept = lax.dynamic_index_in_dim(blocks, mine, 1, keepdims=False)
        self.arrived = flip(
            lax.dynamic_index_in_dim(blocks, 1 - mine, 1, keepdims=False), "dp", bit
        )

    def send_back(self, bit):
        self.arrived = flip(self.value, "dp", bit)

    def join(self, bit):
        upper = (lax.axis_index("dp") & bit) != 0
        value = jnp.where(
            upper,
            jnp.stack([self.arrived, self.value], axis=1),
            jnp.stack([self.value, self.arrived], axis=1),
        )
        self.value = value.reshape(-1, *value.shape[2:])


def tied(chains, *others):
    values = tie((tuple(chain.value for chain in chains), others))
    for chain, value in zip(chains, values[0]):
        chain.value = value
    return values[1]


def body(ends_in, ln_gain, ln_shift, w_qkv, b_qv, w_out, b_out, w_fc1, b_fc1, w_fc2, b_fc2):
    section = lax.axis_index("section")
    shard = lax.axis_index("tensor")
    zhalf = lax.axis_index("dp") % 2
    clips = ends_in.shape[1] // FRAMES
    info = jnp.stack(
        [shard, shard ^ 1, shard ^ 2, shard ^ 3, zhalf] + [jnp.int32(k) for k in BACK_ORDER]
    ).astype(jnp.int32)

    owned = [
        jnp.concatenate([w_qkv[0].transpose(1, 2, 0).reshape(QKV, D), w_out[0]], axis=0),
        w_fc1[0],
        w_fc2[0],
    ]
    nears = [rows_of(own, zhalf, 2) for own in owned]
    fars = [rows_of(own, 1 - zhalf, 2) for own in owned]
    beyond_a = flip(nears[0], "section", 1)

    small = jnp.concatenate(
        [ln_gain[0], ln_shift[0], b_qv[0], b_out, b_fc2, b_fc1.reshape(SHARDS, FEATS)], axis=0
    )
    ends = ends_in[0].T.reshape(FEATS, clips, FRAMES).transpose(1, 0, 2)
    ends = with_rows(ends, jnp.broadcast_to(small, (clips,) + small.shape))
    ends = lax.all_to_all(ends, ("section", "tensor"), split_axis=0, concat_axis=0, tiled=True)
    small = ends[:, FEATS : FEATS + 12, :FEATS].astype(F32)
    cols = jnp.swapaxes(small[:, :8], 1, 2).reshape(2, SHARDS, FEATS, 8)
    b1s = small[:, 8:].reshape(2, SHARDS, 1, FF_SHARD)
    ends = ends[:, :FEATS].reshape(2, D, FRAMES)

    def layers(own, other):
        return jnp.where(section == 0, own, other), jnp.where(section == 0, other, own)

    def over_y(block):
        return flip(block, "tensor", 2)

    def chunk_of(own, there):
        return tuple(
            part for pair in (own, there) for parts in (pair, [flip(x, "tensor", 1) for x in pair])
            for part in parts
        )

    n_dp = lax.axis_size("dp")
    beyond_a, near_one, own_two = tie((beyond_a, nears[1], owned[2]))
    beyond_one = flip(near_one, "section", 1)
    beyond_two = flip(own_two, "section", 1)
    near_a = layers(nears[0], beyond_a)
    far_a = layers(fars[0], flip(beyond_a, "dp", 1))
    there_a = over_y(near_a[0])
    there_a, beyond_one = tie((there_a, beyond_one))
    away_a = flip(there_a, "dp", 1)
    near_one = layers(nears[1], beyond_one)
    beyond_far_one = flip(beyond_one, "dp", 1)
    there_one = over_y(near_one[0])

    def attend(layer, stream, chunk):
        return attention_forward(info, stream, cols[layer], chunk)

    def feed(layer, h, chunk_one, chunk_two):
        return mlp_forward(info, h, cols[layer], b1s[layer], chunk_one, chunk_two)

    there_one, beyond_two = tie((there_one, beyond_two))
    away_one = flip(there_one, "dp", 1)
    near_two = layers(nears[2], rows_of(beyond_two, zhalf, 2))
    far_two = layers(fars[2], rows_of(beyond_two, 1 - zhalf, 2))
    there_two = over_y(near_two[0])
    chunks = [[chunk_of((near_a[0], far_a[0]), (there_a, away_a))], []]
    stream = ends[0]
    a1, p, soft, o, h = attend(0, stream, chunks[0][0])
    h, away_one, there_two, beyond_far_one, late_a, late_far_a, late_one, late_two = tie(
        (h, away_one, there_two, beyond_far_one, near_a[1], far_a[1], near_one[1], near_two[1])
    )
    far_one = layers(fars[1], beyond_far_one)
    chunks[0].append(chunk_of((near_one[0], far_one[0]), (there_one, away_one)))
    chunks[0].append(chunk_of((near_two[0], far_two[0]), (there_two, flip(there_two, "dp", 1))))
    there_a, there_one, there_two = over_y(late_a), over_y(late_one), over_y(late_two)
    away_a = flip(there_a, "dp", 1)
    a2, u, slope, y = feed(0, h, *chunks[0][1:])
    stored = [(stream, a1, p, soft, o, h, a2, u, slope)]
    stream, there_a, away_a, there_one, there_two, late_a, late_far_a = tie(
        (y, there_a, away_a, there_one, there_two, late_a, late_far_a)
    )
    chunks[1].append(chunk_of((late_a, late_far_a), (there_a, away_a)))
    away_one, away_two = flip(there_one, "dp", 1), flip(there_two, "dp", 1)
    a1, p, soft, o, h = attend(1, stream, chunks[1][0])
    h, late = tie(
        (
            h,
            (late_one, far_one[1], there_one, away_one, late_two, far_two[1], there_two, away_two),
        )
    )
    chunks[1].append(chunk_of(late[0:2], late[2:4]))
    chunks[1].append(chunk_of(late[4:6], late[6:8]))
    a2, u, slope, y = feed(1, h, *chunks[1][1:])
    stored.append((stream, a1, p, soft, o, h, a2, u, slope))
    stream = y

    upstream = ends[1]
    chains = [[Chain() for _ in range(3)] for _ in range(2)]
    smalls = [None, None]
    ends_of = [None, None]
    late_a, late_one, late_two = chains[1]
    last_a, last_one, last_two = chains[0]
    for layer in (1, 0):
        chunk_a, chunk_one, chunk_two = chunks[layer]
        x, a1, p, soft, o, h, a2, u, slope = stored[layer]
        chain_a, chain_one, chain_two = chains[layer]
        after, send_one, send_two, db1_sent = mlp_backward(
            info, upstream, h, a2, cols[layer], u, slope, None, chunk_one, chunk_two
        )
        chain_two.start(send_two)
        chain_one.start(send_one)
        gh, dcol_two, keep_one, keep_two, db1_kept = mlp_backward(
            info, upstream, h, a2, cols[layer], u, slope, after, chunk_one, chunk_two
        )
        chain_two.cores(keep_two)
        chain_one.cores(keep_one)
        if layer == 0:
            late_a.fold_rows()
            (gh,) = tied((late_a, last_two, last_one, late_one), gh)
            late_a.scatter()
            last_two.send_y()
            last_one.send_y()
        else:
            (gh,) = tied((late_two, late_one), gh)
            late_one.scatter()
            late_two.send_y()
        after, send_a, dbqv_sent = attention_backward(
            info, gh, x, a1, cols[layer], p, soft, o, None, chunk_a
        )
        chain_a.start(send_a)
        upstream, dcol_one, keep_a, dbqv_kept = attention_backward(
            info, gh, x, a1, cols[layer], p, soft, o, after, chunk_a
        )
        chain_a.cores(keep_a)
        if layer == 1:
            late_two.fold_rows()
            (upstream,) = tied((late_two, late_a), upstream)
            late_two.scatter()
            late_a.send_y()
        else:
            last_two.fold_rows()
            (upstream,) = tied((last_two, last_a, late_two), upstream)
            last_two.scatter()
            last_a.send_y()
            late_one.send_y()
        ends_of[layer] = (db1_kept, db1_sent, (dbqv_kept, dbqv_sent, dcol_one, dcol_two))

    bits = [1 << k for k in range(n_dp.bit_length() - 1)]
    pair_two, pair_one, pair_a = Chain(), Chain(), Chain()

    def start_far(pair):
        pair.value = pair.value[None]
        pair.send_back(bits[-1])

    def finish_far(pair):
        pair.join(bits[-1])
        for bit in bits[-2:0:-1]:
            pair.send_back(bit)
            pair.join(bit)

    last_one.fold_rows()
    tied((last_one, late_a))
    last_one.scatter()

    tied((last_two, late_two))
    pair_two.send_x(last_two, late_two)

    pair_two.fold()
    upstream, ends_of = tied((pair_two,), upstream, ends_of)
    start_far(pair_two)
    for layer in range(2):
        db1_kept, db1_sent, dcols = ends_of[layer]
        smalls[layer] = jnp.concatenate(
            [
                jnp.swapaxes(sum(dcols), 1, 2),
                (db1_kept + db1_sent).reshape(SHARDS, SHARDS, FEATS),
            ],
            axis=1,
        )
    result = jnp.stack([upstream.astype(BF16), stream.astype(BF16)])
    result = with_rows(
        result.reshape(2 * SHARDS, FEATS, FRAMES), jnp.stack(smalls).reshape(-1, 12, FEATS)
    )
    result = lax.all_to_all(result, ("section", "tensor"), split_axis=0, concat_axis=0, tiled=True)

    last_a.fold_rows()
    finish_far(pair_two)
    tied((last_a, pair_two))
    last_a.split()
    last_a.send_half(bits[0])
    pair_two.send_back(bits[0])

    last_a.fold()
    late_one.fold()
    tied((last_a, late_one, last_one))
    for bit in bits[1:]:
        last_a.send_half(bit)
        if bit != bits[-1]:
            last_a.fold()
    pair_one.send_x(last_one, late_one)

    pair_one.fold()
    pair_two.join(bits[0])
    (result,) = tied((pair_one, pair_two), result)
    start_far(pair_one)
    small_sum = result[:, FEATS : FEATS + 12, :FEATS].astype(F32).sum(axis=0)
    result = result[:, :FEATS].transpose(1, 0, 2).reshape(FEATS, clips * FRAMES).T.astype(F32)

    last_a.fold()
    last_a.value = last_a.value[0]
    (small_sum,) = tied((last_a,), small_sum)
    pair_a.send_x(last_a, late_a)
    finish_far(pair_one)
    small_sum += flip(small_sum, "dp", bits[0])

    pair_a.fold()
    (small_sum,) = tied((pair_a, pair_one), small_sum)
    start_far(pair_a)
    pair_one.send_back(bits[0])
    for bit in bits[1:]:
        small_sum += flip(small_sum, "dp", bit)

    finish_far(pair_a)
    pair_one.join(bits[0])
    (small_sum,) = tied((pair_a, pair_one), small_sum)
    pair_a.send_back(bits[0])
    pair_a.join(bits[0])
    for pair in (pair_two, pair_one, pair_a):
        pair.value = pair.value.reshape(D, D)

    grad_a, grad_one, grad_two = [pair.value.astype(F32) for pair in (pair_a, pair_one, pair_two)]
    return (
        result[None],
        small_sum[None, 0:2],
        small_sum[None, 2:4],
        grad_a[:QKV].reshape(3, FEATS, D).transpose(2, 0, 1)[None],
        small_sum[None, 4:6],
        grad_a[QKV:][None],
        small_sum[6:7],
        grad_one[None],
        small_sum[8:12].reshape(1, FF_SHARD),
        grad_two[None],
        small_sum[7:8],
    )


def solution(mesh):
    placed = (
        P("section", "dp", "tensor"),
        P("section", None, "tensor"),
        P("section", None, "tensor"),
        P("section", None, None, "tensor"),
        P("section", None, "tensor"),
        P("section", "tensor", None),
        P("section", "tensor"),
        P("section", None, "tensor"),
        P("section", "tensor"),
        P("section", "tensor", None),
        P("section", "tensor"),
    )
    return jax.shard_map(
        body, mesh=mesh, in_specs=placed, out_specs=placed, check_vma=False
    )
```

```python
import functools

import jax
import jax.numpy as jnp
from jax import lax
from jax.experimental import pallas as pl
from jax.experimental.pallas import tpu as pltpu
from jax.sharding import PartitionSpec as P

D = 768
HD = 64
FRAMES = 448
SHARDS = 4
HEADS_SHARD = 3
FEATS = HEADS_SHARD * HD
QKV = 3 * FEATS
FF_SHARD = 768
HALF = D // 2
EPSILON = 1e-05
SCALE = float(HD) ** (-0.5)
VMEM_LIMIT = 60 * 1024 * 1024
GAIN1, GAIN2, SHIFT1, SHIFT2, BIAS_Q, BIAS_V, BIAS_OUT, BIAS_FC2 = range(8)
BACK_ORDER = (3, 1, 2, 0)
F32 = jnp.float32
BF16 = jnp.bfloat16


def matmul(left, right, left_dim=1, right_dim=0):
    return lax.dot_general(
        left, right, (((left_dim,), (right_dim,)), ((), ())), preferred_element_type=F32
    )


def normalize(values):
    center = jnp.mean(values, axis=0, keepdims=True)
    moved = values - center
    inv_std = lax.rsqrt(jnp.mean(moved * moved, axis=0, keepdims=True) + EPSILON)
    return moved * inv_std, inv_std


def norm_backward(upstream, normed, inv_std, gain):
    scaled = upstream * gain
    mean_one = jnp.mean(scaled, axis=0, keepdims=True)
    mean_two = jnp.mean(scaled * normed, axis=0, keepdims=True)
    return inv_std * (scaled - mean_one - normed * mean_two)


def row_sums(values):
    return jnp.sum(values, axis=1, keepdims=True)


def columns(parts):
    rows = next(iter(parts.values())).shape[0]
    lane = lax.broadcasted_iota(jnp.int32, (rows, 8), 1)
    total = jnp.zeros((rows, 8), F32)
    for index, part in parts.items():
        total = jnp.where(lane == index, part, total)
    return total


def piece_copies(info, pieces, held, sems):
    first = pl.multiple_of(info[4] * HALF, HALF)
    second = pl.multiple_of((1 - info[4]) * HALF, HALF)
    copies, taken = [], 0
    for slot in range(SHARDS):
        targets = [held.at[slot]]
        if pieces[taken].shape[0] == HALF:
            targets = [held.at[slot, pl.ds(first, HALF)], held.at[slot, pl.ds(second, HALF)]]
        copies.append(
            tuple(
                pltpu.make_async_copy(pieces[taken + k], target, sems.at[2 * slot + k])
                for k, target in enumerate(targets)
            )
        )
        taken += len(targets)
    return tuple(copies)


def load_pieces(step, order, chunks):
    @pl.when(step == 0)
    def start():
        for slot in order:
            for chunk in chunks:
                for copy in chunk[slot]:
                    copy.start()

    for index, slot in enumerate(order):

        @pl.when(step == index)
        def wait():
            for chunk in chunks:
                for copy in chunk[slot]:
                    copy.wait()


def attention_forward_kernel(
    count, info, x_ref, col_ref, *refs
):
    step = pl.program_id(0)
    pieces, (a1_ref, p_ref, soft_ref, o_ref, h_ref, held, sems) = refs[:count], refs[count:]
    copies = piece_copies(info, pieces, held, sems)
    load_pieces(step, range(SHARDS), (copies,))

    @pl.when(step == 0)
    def first():
        col = col_ref[...].reshape(D, 8)
        values = x_ref[...].astype(F32)
        normed, _ = normalize(values)
        a1_ref[...] = (
            normed * col[:, GAIN1 : GAIN1 + 1] + col[:, SHIFT1 : SHIFT1 + 1]
        ).astype(BF16)
        h_ref[...] = values + col[:, BIAS_OUT : BIAS_OUT + 1]

    bias = col_ref[info[step]]
    projected = matmul(held[step, :QKV], a1_ref[...])
    queries = (projected[:FEATS] + bias[:, BIAS_Q : BIAS_Q + 1]).astype(BF16)
    keys = projected[FEATS : 2 * FEATS].astype(BF16)
    values = (projected[2 * FEATS :] + bias[:, BIAS_V : BIAS_V + 1]).astype(BF16)
    p_ref[0, :FEATS] = queries
    p_ref[0, FEATS : 2 * FEATS] = keys
    p_ref[0, 2 * FEATS :] = values
    scaled = queries * SCALE
    for head in range(HEADS_SHARD):
        rows = slice(head * HD, (head + 1) * HD)
        scores = matmul(keys[rows], scaled[rows], 0, 0)
        exps = jnp.exp(scores - jnp.max(scores, axis=0, keepdims=True))
        soft = exps * (1.0 / jnp.sum(exps, axis=0, keepdims=True))
        soft = soft.astype(BF16)
        soft_ref[0, head] = soft
        o_ref[0, rows] = matmul(values[rows], soft).astype(BF16)
    h_ref[...] += matmul(held[step, QKV:], o_ref[0], 0, 0)


def mlp_forward_kernel(
    counts, info, h_ref, col_ref, b1_ref, *refs
):
    step = pl.program_id(0)
    pieces_one, pieces_two, refs = refs[:counts[0]], refs[counts[0]:sum(counts)], refs[sum(counts):]
    a2_ref, u_ref, slope_ref, y_ref, held_one, held_two, a2_rows, total, sems_one, sems_two = refs
    copies_one = piece_copies(info, pieces_one, held_one, sems_one)
    copies_two = piece_copies(info, pieces_two, held_two, sems_two)
    load_pieces(step, range(SHARDS), (copies_one, copies_two))

    @pl.when(step == 0)
    def first():
        col = col_ref[...].reshape(D, 8)
        normed, _ = normalize(h_ref[...])
        scaled = normed * col[:, GAIN2 : GAIN2 + 1] + col[:, SHIFT2 : SHIFT2 + 1]
        a2_ref[...] = scaled.astype(BF16)
        a2_rows[...] = scaled.T.astype(BF16)
        total[...] = jnp.zeros_like(total)

    inner = matmul(a2_rows[...], held_one[step]) + b1_ref[info[step]]
    phi = 0.5 + 0.5 * lax.erf(inner * 0.7071067811865476)
    density = 0.3989422804014327 * jnp.exp(-0.5 * inner * inner)
    active = (inner * phi).astype(BF16)
    u_ref[0] = active
    slope_ref[0] = (phi + inner * density).astype(BF16)
    total[...] += matmul(active, held_two[step])

    @pl.when(step == SHARDS - 1)
    def last():
        col = col_ref[...].reshape(D, 8)
        y_ref[...] = h_ref[...] + total[...].T + col[:, BIAS_FC2 : BIAS_FC2 + 1]


def mlp_backward_kernel(
    last, counts, info, gy_ref, h_ref, a2_ref, col_ref, u_ref, slope_ref, *refs
):
    step = pl.program_id(0)
    if last:
        before_ref, *refs = refs
    pieces_one, pieces_two, refs = refs[:counts[0]], refs[counts[0]:sum(counts)], refs[sum(counts):]
    if last:
        gh_ref, dcol_ref, *refs = refs
    else:
        after_ref, *refs = refs
    grad_one, grad_two, db1_ref, held_one, held_two, gy_rows, total, sems_one, sems_two = refs
    copies_one = piece_copies(info, pieces_one, held_one, sems_one)
    copies_two = piece_copies(info, pieces_two, held_two, sems_two)
    load_pieces(step, BACK_ORDER[2:] if last else BACK_ORDER[:2], (copies_two, copies_one))

    @pl.when(step == 0)
    def first():
        gy_rows[...] = gy_ref[...].astype(F32).T.astype(BF16)
        db1_ref[...] = jnp.zeros_like(db1_ref)
        total[...] = before_ref[...] if last else jnp.zeros_like(total)

    slot = info[(7 if last else 5) + step]
    d_active = matmul(gy_rows[...], held_two[slot], 1, 1)
    d_inner = d_active * slope_ref[0].astype(F32)
    rounded = d_inner.astype(BF16)
    db1_ref[info[slot]] = jnp.sum(rounded.astype(F32), axis=0, keepdims=True)
    grad_two[0] = matmul(u_ref[0], gy_rows[...], 0, 0).astype(BF16)
    grad_one[0] = matmul(a2_ref[...], rounded).astype(BF16)
    total[...] += matmul(rounded, held_one[slot], 1, 1)

    @pl.when(step == 1)
    def end():
        if not last:
            after_ref[...] = total[...]
            return
        col = col_ref[...].reshape(D, 8)
        normed, inv_std = normalize(h_ref[...])
        d_mid = total[...].T
        upstream = gy_ref[...].astype(F32)
        d_hidden = upstream + norm_backward(d_mid, normed, inv_std, col[:, GAIN2 : GAIN2 + 1])
        gh_ref[...] = d_hidden
        dcol_ref[...] = columns(
            {
                GAIN2: row_sums(d_mid * normed),
                SHIFT2: row_sums(d_mid),
                BIAS_OUT: row_sums(d_hidden),
                BIAS_FC2: row_sums(upstream),
            }
        ).reshape(COLS)


def attention_backward_kernel(
    last, count, info, gh_ref, x_ref, a1_ref, col_ref, p_ref, soft_ref, o_ref, *refs
):
    step = pl.program_id(0)
    if last:
        before_ref, *refs = refs
    pieces, refs = refs[:count], refs[count:]
    if last:
        gx_ref, dcol_ref, *refs = refs
    else:
        after_ref, *refs = refs
    grad_ref, dbqv_ref, held, gh_rounded, g_p, total, sems = refs
    copies = piece_copies(info, pieces, held, sems)
    load_pieces(step, BACK_ORDER[2:] if last else BACK_ORDER[:2], (copies,))

    @pl.when(step == 0)
    def first():
        gh_rounded[...] = gh_ref[...].astype(BF16)
        dbqv_ref[...] = jnp.zeros_like(dbqv_ref)
        total[...] = before_ref[...] if last else jnp.zeros_like(total)

    slot = info[(7 if last else 5) + step]
    d_attended = matmul(held[slot, QKV:], gh_rounded[...]).astype(BF16)
    grad_ref[0, QKV:] = matmul(o_ref[0], gh_rounded[...], 1, 1).astype(BF16)
    for head in range(HEADS_SHARD):
        rows = slice(head * HD, (head + 1) * HD)
        queries = p_ref[0, rows]
        keys = p_ref[0, FEATS + head * HD : FEATS + (head + 1) * HD]
        values = p_ref[0, 2 * FEATS + head * HD : 2 * FEATS + (head + 1) * HD]
        soft = soft_ref[0, head]
        d_att = d_attended[rows]
        delta = jnp.sum(
            d_att.astype(F32) * o_ref[0, rows].astype(F32), axis=0, keepdims=True
        )
        d_soft = matmul(values, d_att, 0, 0)
        d_scores = (soft.astype(F32) * (d_soft - delta)).astype(BF16)
        g_p[rows] = (matmul(keys, d_scores) * SCALE).astype(BF16)
        g_p[FEATS + head * HD : FEATS + (head + 1) * HD] = (
            matmul(queries, d_scores, 1, 1) * SCALE
        ).astype(BF16)
        g_p[2 * FEATS + head * HD : 2 * FEATS + (head + 1) * HD] = matmul(
            d_att, soft, 1, 1
        ).astype(BF16)
    d_projected = g_p[...]
    grad_ref[0, :QKV] = matmul(d_projected, a1_ref[...], 1, 1).astype(BF16)
    total[...] += matmul(d_projected, held[slot, :QKV], 0, 0)
    dbqv_ref[info[slot]] = columns(
        {
            BIAS_Q: row_sums(d_projected[:FEATS].astype(F32)),
            BIAS_V: row_sums(d_projected[2 * FEATS :].astype(F32)),
        }
    )

    @pl.when(step == 1)
    def end():
        if not last:
            after_ref[...] = total[...]
            return
        col = col_ref[...].reshape(D, 8)
        normed, inv_std = normalize(x_ref[...].astype(F32))
        d_first = total[...].T
        gx_ref[...] = gh_ref[...] + norm_backward(
            d_first, normed, inv_std, col[:, GAIN1 : GAIN1 + 1]
        )
        dcol_ref[...] = columns(
            {GAIN1: row_sums(d_first * normed), SHIFT1: row_sums(d_first)}
        ).reshape(COLS)


def whole(shape):
    return pl.BlockSpec(shape, lambda i, info: (0,) * len(shape))


def by_step(shape):
    return pl.BlockSpec((1,) + shape, lambda i, info: (i,) + (0,) * len(shape))


def by_slot(shape, last):
    first = 7 if last else 5
    return pl.BlockSpec((1,) + shape, lambda i, info: (info[first + i],) + (0,) * len(shape))


PIECE = [pl.BlockSpec(memory_space=pltpu.HBM)]
COPY_SEMS = pltpu.SemaphoreType.DMA((2 * SHARDS,))
HELD = pltpu.VMEM((SHARDS, D, D), BF16)


def of(shape, dtype=BF16):
    return jax.ShapeDtypeStruct(shape, dtype)


def run(kernel, name, steps, info, operands, in_specs, outs, out_specs, scratch, flops):
    return pl.pallas_call(
        kernel,
        name=name,
        out_shape=outs,
        grid_spec=pltpu.PrefetchScalarGridSpec(
            num_scalar_prefetch=1,
            grid=(steps,),
            in_specs=in_specs,
            out_specs=out_specs,
            scratch_shapes=scratch,
        ),
        compiler_params=pltpu.CompilerParams(
            vmem_limit_bytes=VMEM_LIMIT, dimension_semantics=("arbitrary",)
        ),
        cost_estimate=pl.CostEstimate(flops=flops * 16, bytes_accessed=2**28, transcendentals=0),
    )(info, *operands)


STREAM = (D, FRAMES)
ROWS = (FRAMES, D)
COLS = (SHARDS, FEATS, 8)
ATT_FLOPS = 2 * FRAMES * D * (4 * D + 2 * FRAMES)
MLP_FLOPS = 4 * FRAMES * D * SHARDS * FF_SHARD


def attention_forward(info, x, col, chunk):
    return run(
        functools.partial(attention_forward_kernel, len(chunk)), "attention_forward", SHARDS, info, (x, col, *chunk),
        [whole(STREAM), whole(COLS)] + PIECE * len(chunk),
        [
            of(STREAM), of((SHARDS, QKV, FRAMES)), of((SHARDS, HEADS_SHARD, FRAMES, FRAMES)),
            of((SHARDS, FEATS, FRAMES)), of(STREAM, F32),
        ],
        [
            whole(STREAM), by_step((QKV, FRAMES)), by_step((HEADS_SHARD, FRAMES, FRAMES)),
            by_step((FEATS, FRAMES)), whole(STREAM),
        ],
        [HELD, COPY_SEMS],
        ATT_FLOPS,
    )


def mlp_forward(info, h, col, b1, chunk_one, chunk_two):
    return run(
        functools.partial(mlp_forward_kernel, (len(chunk_one), len(chunk_two))), "mlp_forward", SHARDS, info, (h, col, b1, *chunk_one, *chunk_two),
        [whole(STREAM), whole(COLS), whole((SHARDS, 1, FF_SHARD))] + PIECE * len(chunk_one + chunk_two),
        [of(STREAM), of((SHARDS, FRAMES, FF_SHARD)), of((SHARDS, FRAMES, FF_SHARD)), of(STREAM, F32)],
        [whole(STREAM), by_step((FRAMES, FF_SHARD)), by_step((FRAMES, FF_SHARD)), whole(STREAM)],
        [HELD, HELD, pltpu.VMEM(ROWS, BF16), pltpu.VMEM(ROWS, F32), COPY_SEMS, COPY_SEMS],
        MLP_FLOPS,
    )


def mlp_backward(info, gy, h, a2, col, u, slope, before, chunk_one, chunk_two):
    last = before is not None
    carried = (before,) if last else ()
    ends = [of(STREAM, F32), of(COLS, F32)] if last else [of(ROWS, F32)]
    return run(
        functools.partial(mlp_backward_kernel, last, (len(chunk_one), len(chunk_two))), "mlp_backward", 2, info,
        (gy, h, a2, col, u, slope, *carried, *chunk_one, *chunk_two),
        [
            whole(STREAM), whole(STREAM), whole(STREAM), whole(COLS),
            by_slot((FRAMES, FF_SHARD), last), by_slot((FRAMES, FF_SHARD), last),
        ]
        + [whole(ROWS)] * len(carried)
        + PIECE * len(chunk_one + chunk_two),
        ends + [of((2, D, D)), of((2, D, D)), of((SHARDS, 1, FF_SHARD), F32)],
        [whole(end.shape) for end in ends]
        + [by_step((D, D)), by_step((D, D)), whole((SHARDS, 1, FF_SHARD))],
        [HELD, HELD, pltpu.VMEM(ROWS, BF16), pltpu.VMEM(ROWS, F32), COPY_SEMS, COPY_SEMS],
        MLP_FLOPS,
    )


def attention_backward(info, gh, x, a1, col, p, soft, o, before, chunk):
    last = before is not None
    carried = (before,) if last else ()
    ends = [of(STREAM, F32), of(COLS, F32)] if last else [of(ROWS, F32)]
    return run(
        functools.partial(attention_backward_kernel, last, len(chunk)), "attention_backward", 2, info,
        (gh, x, a1, col, p, soft, o, *carried, *chunk),
        [
            whole(STREAM), whole(STREAM), whole(STREAM), whole(COLS),
            by_slot((QKV, FRAMES), last), by_slot((HEADS_SHARD, FRAMES, FRAMES), last),
            by_slot((FEATS, FRAMES), last),
        ]
        + [whole(ROWS)] * len(carried)
        + PIECE * len(chunk),
        ends + [of((2, D, D)), of(COLS, F32)],
        [whole(end.shape) for end in ends] + [by_step((D, D)), whole(COLS)],
        [HELD, pltpu.VMEM(STREAM, BF16), pltpu.VMEM((QKV, FRAMES), BF16), pltpu.VMEM(ROWS, F32), COPY_SEMS],
        ATT_FLOPS,
    )


def tie(groups):
    return lax.optimization_barrier(groups)


def flip(block, axis, bit):
    size = lax.axis_size(axis)
    return lax.ppermute(block, axis, [(i, i ^ bit) for i in range(size)])


def added(left, right):
    return (left.astype(F32) + right.astype(F32)).astype(BF16)


def sum_kernel(left_ref, right_ref, *out_refs):
    for index, out_ref in enumerate(out_refs):
        place = index if len(out_refs) > 1 else Ellipsis
        out_ref[...] = added(left_ref[place], right_ref[place])


def summed(left, right, outs):
    rows = left.shape[-2]
    block = 384 if rows % 384 == 0 else rows
    spec = pl.BlockSpec((block, D), lambda i: (i, 0))
    pair = pl.BlockSpec((2, block, D), lambda i: (0, i, 0))
    return pl.pallas_call(
        sum_kernel,
        name="row_sums",
        grid=(rows // block,),
        in_specs=[pair if outs == 2 else spec] * 2,
        out_specs=[spec] * outs,
        out_shape=[jax.ShapeDtypeStruct((rows, D), BF16)] * outs,
        compiler_params=pltpu.CompilerParams(vmem_limit_bytes=VMEM_LIMIT // 4),
        cost_estimate=pl.CostEstimate(flops=2**36, bytes_accessed=2**28, transcendentals=0),
    )(left, right)


def with_rows(blocks, small):
    pad = ((0, 0), (0, 16 - small.shape[1]), (0, blocks.shape[2] - small.shape[2]))
    return jnp.concatenate([blocks, jnp.pad(small.astype(BF16), pad)], axis=1)


def rows_of(value, place, parts):
    size = value.shape[-2] // parts
    return lax.dynamic_slice_in_dim(value, place * size, size, axis=value.ndim - 2)


class Chain:
    def start(self, send):
        self.arrived = flip(send, "tensor", 1)

    def cores(self, keep):
        self.value = summed(keep, self.arrived, 2)

    def scatter(self):
        parts = lax.axis_size("dp")
        both = self.value if isinstance(self.value, (list, tuple)) else [self.value]
        split = jnp.stack([value.reshape(parts, -1, D) for value in both], axis=1)
        total = lax.psum_scatter(split, "dp", scatter_dimension=0, tiled=False)
        self.value = total if len(both) == 2 else total[0]

    def send_y(self):
        self.kept, self.arrived = self.value[1], flip(self.value[0], "tensor", 2)

    def fold_rows(self):
        rows = self.kept.shape
        (total,) = summed(self.kept.reshape(-1, D), self.arrived.reshape(-1, D), 1)
        self.value = total.reshape(rows)

    def send_x(self, first, second):
        section = lax.axis_index("section")
        self.kept = jnp.where(section == 0, first.value, second.value)
        self.arrived = flip(jnp.where(section == 0, second.value, first.value), "section", 1)

    def fold(self):
        self.value = added(self.kept, self.arrived)

    def split(self):
        self.value = self.value.reshape(lax.axis_size("dp"), -1, D)

    def send_half(self, bit):
        mine = ((lax.axis_index("dp") & bit) != 0).astype(jnp.int32)
        blocks = self.value.reshape(-1, 2, *self.value.shape[1:])
        self.kept = lax.dynamic_index_in_dim(blocks, mine, 1, keepdims=False)
        self.arrived = flip(
            lax.dynamic_index_in_dim(blocks, 1 - mine, 1, keepdims=False), "dp", bit
        )

    def send_back(self, bit):
        self.arrived = flip(self.value, "dp", bit)

    def join(self, bit):
        upper = (lax.axis_index("dp") & bit) != 0
        value = jnp.where(
            upper,
            jnp.stack([self.arrived, self.value], axis=1),
            jnp.stack([self.value, self.arrived], axis=1),
        )
        self.value = value.reshape(-1, *value.shape[2:])


def tied(chains, *others):
    values = tie((tuple(chain.value for chain in chains), others))
    for chain, value in zip(chains, values[0]):
        chain.value = value
    return values[1]


def body(ends_in, ln_gain, ln_shift, w_qkv, b_qv, w_out, b_out, w_fc1, b_fc1, w_fc2, b_fc2):
    section = lax.axis_index("section")
    shard = lax.axis_index("tensor")
    zhalf = lax.axis_index("dp") % 2
    clips = ends_in.shape[1] // FRAMES
    info = jnp.stack(
        [shard, shard ^ 1, shard ^ 2, shard ^ 3, zhalf] + [jnp.int32(k) for k in BACK_ORDER]
    ).astype(jnp.int32)

    owned = [
        jnp.concatenate([w_qkv[0].transpose(1, 2, 0).reshape(QKV, D), w_out[0]], axis=0),
        w_fc1[0],
        w_fc2[0],
    ]
    nears = [rows_of(own, zhalf, 2) for own in owned]
    fars = [rows_of(own, 1 - zhalf, 2) for own in owned]
    beyond_a = flip(nears[0], "section", 1)

    small = jnp.concatenate(
        [ln_gain[0], ln_shift[0], b_qv[0], b_out, b_fc2, b_fc1.reshape(SHARDS, FEATS)], axis=0
    )
    ends = ends_in[0].T.reshape(FEATS, clips, FRAMES).transpose(1, 0, 2)
    ends = with_rows(ends, jnp.broadcast_to(small, (clips,) + small.shape))
    beyond_a, near_one, own_two, ends = tie((beyond_a, nears[1], owned[2], ends))
    ends = lax.all_to_all(ends, ("section", "tensor"), split_axis=0, concat_axis=0, tiled=True)
    small = ends[:, FEATS : FEATS + 12, :FEATS].astype(F32)
    cols = jnp.swapaxes(small[:, :8], 1, 2).reshape(2, SHARDS, FEATS, 8)
    b1s = small[:, 8:].reshape(2, SHARDS, 1, FF_SHARD)
    ends = ends[:, :FEATS].reshape(2, D, FRAMES)

    def layers(own, other):
        return jnp.where(section == 0, own, other), jnp.where(section == 0, other, own)

    def over_y(block):
        return flip(block, "tensor", 2)

    def chunk_of(own, there):
        return tuple(
            part for pair in (own, there) for parts in (pair, [flip(x, "tensor", 1) for x in pair])
            for part in parts
        )

    n_dp = lax.axis_size("dp")
    beyond_one = flip(near_one, "section", 1)
    beyond_two = flip(own_two, "section", 1)
    near_a = layers(nears[0], beyond_a)
    far_a = layers(fars[0], flip(beyond_a, "dp", 1))
    there_a = over_y(near_a[0])
    there_a, beyond_one = tie((there_a, beyond_one))
    away_a = flip(there_a, "dp", 1)
    near_one = layers(nears[1], beyond_one)
    beyond_far_one = flip(beyond_one, "dp", 1)
    there_one = over_y(near_one[0])

    def attend(layer, stream, chunk):
        return attention_forward(info, stream, cols[layer], chunk)

    def feed(layer, h, chunk_one, chunk_two):
        return mlp_forward(info, h, cols[layer], b1s[layer], chunk_one, chunk_two)

    there_one, beyond_two = tie((there_one, beyond_two))
    away_one = flip(there_one, "dp", 1)
    near_two = layers(nears[2], rows_of(beyond_two, zhalf, 2))
    far_two = layers(fars[2], rows_of(beyond_two, 1 - zhalf, 2))
    there_two = over_y(near_two[0])
    chunks = [[chunk_of((near_a[0], far_a[0]), (there_a, away_a))], []]
    stream = ends[0]
    a1, p, soft, o, h = attend(0, stream, chunks[0][0])
    h, away_one, there_two, beyond_far_one, late_a, late_far_a, late_one, late_two = tie(
        (h, away_one, there_two, beyond_far_one, near_a[1], far_a[1], near_one[1], (near_two[1], far_two[1]))
    )
    far_one = layers(fars[1], beyond_far_one)
    chunks[0].append(chunk_of((near_one[0], far_one[0]), (there_one, away_one)))
    chunks[0].append(chunk_of((near_two[0], far_two[0]), (there_two, flip(there_two, "dp", 1))))
    there_a, there_one = over_y(late_a), over_y(late_one)
    there_two, away_two = over_y(late_two[0]), over_y(late_two[1])
    away_a = flip(there_a, "dp", 1)
    a2, u, slope, y = feed(0, h, *chunks[0][1:])
    stored = [(stream, a1, p, soft, o, h, a2, u, slope)]
    stream, there_a, away_a, there_one, late_a, late_far_a = tie(
        (y, there_a, away_a, there_one, late_a, late_far_a)
    )
    chunks[1].append(chunk_of((late_a, late_far_a), (there_a, away_a)))
    away_one = flip(there_one, "dp", 1)
    a1, p, soft, o, h = attend(1, stream, chunks[1][0])
    h, late = tie(
        (
            h,
            (late_one, far_one[1], there_one, away_one, *late_two, there_two, away_two),
        )
    )
    chunks[1].append(chunk_of(late[0:2], late[2:4]))
    chunks[1].append(chunk_of(late[4:6], late[6:8]))
    a2, u, slope, y = feed(1, h, *chunks[1][1:])
    stored.append((stream, a1, p, soft, o, h, a2, u, slope))
    stream = y

    upstream = ends[1]
    bits = [1 << k for k in range(n_dp.bit_length() - 1)]
    chains = [[Chain() for _ in range(3)] for _ in range(2)]
    smalls = [None, None]
    ends_of = [None, None]
    late_a, late_one, late_two = chains[1]
    last_a, last_one, last_two = chains[0]
    for layer in (1, 0):
        chunk_a, chunk_one, chunk_two = chunks[layer]
        x, a1, p, soft, o, h, a2, u, slope = stored[layer]
        chain_a, chain_one, chain_two = chains[layer]
        after, send_one, send_two, db1_sent = mlp_backward(
            info, upstream, h, a2, cols[layer], u, slope, None, chunk_one, chunk_two
        )
        chain_two.start(send_two)
        chain_one.start(send_one)
        gh, dcol_two, keep_one, keep_two, db1_kept = mlp_backward(
            info, upstream, h, a2, cols[layer], u, slope, after, chunk_one, chunk_two
        )
        chain_two.cores(keep_two)
        chain_one.cores(keep_one)
        if layer == 0:
            late_a.fold_rows()
            (gh,) = tied((late_a, last_two, last_one, late_one), gh)
            late_a.split()
            late_a.send_half(bits[0])
            last_two.send_y()
            last_one.send_y()
        else:
            (gh,) = tied((late_two, late_one), gh)
            late_one.scatter()
            late_two.send_y()
        after, send_a, dbqv_sent = attention_backward(
            info, gh, x, a1, cols[layer], p, soft, o, None, chunk_a
        )
        chain_a.start(send_a)
        upstream, dcol_one, keep_a, dbqv_kept = attention_backward(
            info, gh, x, a1, cols[layer], p, soft, o, after, chunk_a
        )
        chain_a.cores(keep_a)
        if layer == 1:
            late_two.fold_rows()
            (upstream,) = tied((late_two, late_a), upstream)
            late_two.scatter()
            late_a.send_y()
        else:
            last_two.fold_rows()
            late_a.fold()
            (upstream,) = tied((last_two, last_a, late_two, late_a), upstream)
            for bit in bits[1:]:
                late_a.send_half(bit)
                if bit != bits[-1]:
                    late_a.fold()
            last_two.scatter()
            last_a.send_y()
            late_one.send_y()
        ends_of[layer] = (db1_kept, db1_sent, (dbqv_kept, dbqv_sent, dcol_one, dcol_two))

    pair_two, pair_one, pair_a = Chain(), Chain(), Chain()

    def start_far(pair):
        pair.value = pair.value[None]
        pair.send_back(bits[-1])

    def finish_far(pair):
        pair.join(bits[-1])
        for bit in bits[-2:0:-1]:
            pair.send_back(bit)
            pair.join(bit)

    last_one.fold_rows()
    late_a.fold()
    late_a.value = late_a.value[0]
    tied((last_one, late_a))
    last_one.scatter()
    tied((last_two, late_two))
    pair_two.send_x(last_two, late_two)

    pair_two.fold()
    upstream, ends_of = tied((pair_two,), upstream, ends_of)
    for layer in range(2):
        db1_kept, db1_sent, dcols = ends_of[layer]
        smalls[layer] = jnp.concatenate(
            [
                jnp.swapaxes(sum(dcols), 1, 2),
                (db1_kept + db1_sent).reshape(SHARDS, SHARDS, FEATS),
            ],
            axis=1,
        )
    result = jnp.stack([upstream.astype(BF16), stream.astype(BF16)])
    result = with_rows(
        result.reshape(2 * SHARDS, FEATS, FRAMES), jnp.stack(smalls).reshape(-1, 12, FEATS)
    )
    result = lax.all_to_all(result, ("section", "tensor"), split_axis=0, concat_axis=0, tiled=True)

    last_a.fold_rows()
    tied((last_a, pair_two))
    last_a.split()
    last_a.send_half(bits[0])
    start_far(pair_two)

    last_a.fold()
    tied((last_a,))
    for bit in bits[1:]:
        last_a.send_half(bit)
        if bit != bits[-1]:
            last_a.fold()

    late_one.fold()
    finish_far(pair_two)
    (result,) = tied((pair_two, last_one, late_one), result)
    pair_one.send_x(last_one, late_one)
    pair_two.send_back(bits[0])
    small_sum = result[:, FEATS : FEATS + 12, :FEATS].astype(F32).sum(axis=0)

    last_a.fold()
    last_a.value = last_a.value[0]
    pair_one.fold()
    result, small_sum = tied((last_a, pair_one), result, small_sum)
    pair_a.send_x(last_a, late_a)
    start_far(pair_one)
    small_sum += flip(small_sum, "dp", bits[0])

    pair_a.fold()
    pair_two.join(bits[0])
    result, small_sum = tied((pair_a, pair_two), result, small_sum)
    start_far(pair_a)
    for bit in bits[1:]:
        small_sum += flip(small_sum, "dp", bit)

    finish_far(pair_one)
    (result,) = tied((pair_one,), result)
    pair_one.send_back(bits[0])
    result = result[:, :FEATS].transpose(1, 0, 2).reshape(FEATS, clips * FRAMES).T.astype(F32)

    finish_far(pair_a)
    (small_sum,) = tied((pair_a,), small_sum)
    pair_a.send_back(bits[0])
    pair_one.join(bits[0])
    pair_a.join(bits[0])
    for pair in (pair_two, pair_one, pair_a):
        pair.value = pair.value.reshape(D, D)

    grad_a, grad_one, grad_two = [pair.value.astype(F32) for pair in (pair_a, pair_one, pair_two)]
    return (
        result[None],
        small_sum[None, 0:2],
        small_sum[None, 2:4],
        grad_a[:QKV].reshape(3, FEATS, D).transpose(2, 0, 1)[None],
        small_sum[None, 4:6],
        grad_a[QKV:][None],
        small_sum[6:7],
        grad_one[None],
        small_sum[8:12].reshape(1, FF_SHARD),
        grad_two[None],
        small_sum[7:8],
    )


def solution(mesh):
    placed = (
        P("section", "dp", "tensor"),
        P("section", None, "tensor"),
        P("section", None, "tensor"),
        P("section", None, None, "tensor"),
        P("section", None, "tensor"),
        P("section", "tensor", None),
        P("section", "tensor"),
        P("section", None, "tensor"),
        P("section", "tensor"),
        P("section", "tensor", None),
        P("section", "tensor"),
    )
    return jax.shard_map(
        body, mesh=mesh, in_specs=placed, out_specs=placed, check_vma=False
    )
```

```python
import functools

import jax
import jax.numpy as jnp
from jax import lax
from jax.experimental import pallas as pl
from jax.experimental.pallas import tpu as pltpu
from jax.sharding import PartitionSpec as P

D = 768
HD = 64
FRAMES = 448
SHARDS = 4
HEADS_SHARD = 3
FEATS = HEADS_SHARD * HD
QKV = 3 * FEATS
FF_SHARD = 768
HALF = D // 2
EPSILON = 1e-05
SCALE = float(HD) ** (-0.5)
VMEM_LIMIT = 60 * 1024 * 1024
GAIN1, GAIN2, SHIFT1, SHIFT2, BIAS_Q, BIAS_V, BIAS_OUT, BIAS_FC2 = range(8)
BACK_ORDER = (3, 1, 2, 0)
F32 = jnp.float32
BF16 = jnp.bfloat16


def matmul(left, right, left_dim=1, right_dim=0):
    return lax.dot_general(
        left, right, (((left_dim,), (right_dim,)), ((), ())), preferred_element_type=F32
    )


def normalize(values):
    center = jnp.mean(values, axis=0, keepdims=True)
    moved = values - center
    inv_std = lax.rsqrt(jnp.mean(moved * moved, axis=0, keepdims=True) + EPSILON)
    return moved * inv_std, inv_std


def norm_backward(upstream, normed, inv_std, gain):
    scaled = upstream * gain
    mean_one = jnp.mean(scaled, axis=0, keepdims=True)
    mean_two = jnp.mean(scaled * normed, axis=0, keepdims=True)
    return inv_std * (scaled - mean_one - normed * mean_two)


def row_sums(values):
    return jnp.sum(values, axis=1, keepdims=True)


def columns(parts):
    rows = next(iter(parts.values())).shape[0]
    lane = lax.broadcasted_iota(jnp.int32, (rows, 8), 1)
    total = jnp.zeros((rows, 8), F32)
    for index, part in parts.items():
        total = jnp.where(lane == index, part, total)
    return total


def piece_copies(info, pieces, held, sems):
    first = pl.multiple_of(info[4] * HALF, HALF)
    second = pl.multiple_of((1 - info[4]) * HALF, HALF)
    copies, taken = [], 0
    for slot in range(SHARDS):
        targets = [held.at[slot]]
        if pieces[taken].shape[0] == HALF:
            targets = [held.at[slot, pl.ds(first, HALF)], held.at[slot, pl.ds(second, HALF)]]
        copies.append(
            tuple(
                pltpu.make_async_copy(pieces[taken + k], target, sems.at[2 * slot + k])
                for k, target in enumerate(targets)
            )
        )
        taken += len(targets)
    return tuple(copies)


def load_pieces(step, order, chunks):
    @pl.when(step == 0)
    def start():
        for slot in order:
            for chunk in chunks:
                for copy in chunk[slot]:
                    copy.start()

    for index, slot in enumerate(order):

        @pl.when(step == index)
        def wait():
            for chunk in chunks:
                for copy in chunk[slot]:
                    copy.wait()


def attention_forward_kernel(
    count, info, x_ref, col_ref, *refs
):
    step = pl.program_id(0)
    pieces, (a1_ref, p_ref, soft_ref, o_ref, h_ref, held, sems) = refs[:count], refs[count:]
    copies = piece_copies(info, pieces, held, sems)
    load_pieces(step, range(SHARDS), (copies,))

    @pl.when(step == 0)
    def first():
        col = col_ref[...].reshape(D, 8)
        values = x_ref[...].astype(F32)
        normed, _ = normalize(values)
        a1_ref[...] = (
            normed * col[:, GAIN1 : GAIN1 + 1] + col[:, SHIFT1 : SHIFT1 + 1]
        ).astype(BF16)
        h_ref[...] = values + col[:, BIAS_OUT : BIAS_OUT + 1]

    bias = col_ref[info[step]]
    projected = matmul(held[step, :QKV], a1_ref[...])
    queries = (projected[:FEATS] + bias[:, BIAS_Q : BIAS_Q + 1]).astype(BF16)
    keys = projected[FEATS : 2 * FEATS].astype(BF16)
    values = (projected[2 * FEATS :] + bias[:, BIAS_V : BIAS_V + 1]).astype(BF16)
    p_ref[0, :FEATS] = queries
    p_ref[0, FEATS : 2 * FEATS] = keys
    p_ref[0, 2 * FEATS :] = values
    scaled = queries * SCALE
    for head in range(HEADS_SHARD):
        rows = slice(head * HD, (head + 1) * HD)
        scores = matmul(keys[rows], scaled[rows], 0, 0)
        exps = jnp.exp(scores - jnp.max(scores, axis=0, keepdims=True))
        soft = exps * (1.0 / jnp.sum(exps, axis=0, keepdims=True))
        soft = soft.astype(BF16)
        soft_ref[0, head] = soft
        o_ref[0, rows] = matmul(values[rows], soft).astype(BF16)
    h_ref[...] += matmul(held[step, QKV:], o_ref[0], 0, 0)


def mlp_forward_kernel(
    counts, info, h_ref, col_ref, b1_ref, *refs
):
    step = pl.program_id(0)
    pieces_one, pieces_two, refs = refs[:counts[0]], refs[counts[0]:sum(counts)], refs[sum(counts):]
    a2_ref, u_ref, slope_ref, y_ref, held_one, held_two, a2_rows, total, sems_one, sems_two = refs
    copies_one = piece_copies(info, pieces_one, held_one, sems_one)
    copies_two = piece_copies(info, pieces_two, held_two, sems_two)
    load_pieces(step, range(SHARDS), (copies_one, copies_two))

    @pl.when(step == 0)
    def first():
        col = col_ref[...].reshape(D, 8)
        normed, _ = normalize(h_ref[...])
        scaled = normed * col[:, GAIN2 : GAIN2 + 1] + col[:, SHIFT2 : SHIFT2 + 1]
        a2_ref[...] = scaled.astype(BF16)
        a2_rows[...] = scaled.T.astype(BF16)
        total[...] = jnp.zeros_like(total)

    inner = matmul(a2_rows[...], held_one[step]) + b1_ref[info[step]]
    phi = 0.5 + 0.5 * lax.erf(inner * 0.7071067811865476)
    density = 0.3989422804014327 * jnp.exp(-0.5 * inner * inner)
    active = (inner * phi).astype(BF16)
    u_ref[0] = active
    slope_ref[0] = (phi + inner * density).astype(BF16)
    total[...] += matmul(active, held_two[step])

    @pl.when(step == SHARDS - 1)
    def last():
        col = col_ref[...].reshape(D, 8)
        y_ref[...] = h_ref[...] + total[...].T + col[:, BIAS_FC2 : BIAS_FC2 + 1]


def mlp_backward_kernel(
    last, counts, info, gy_ref, h_ref, a2_ref, col_ref, u_ref, slope_ref, *refs
):
    step = pl.program_id(0)
    if last:
        before_ref, *refs = refs
    pieces_one, pieces_two, refs = refs[:counts[0]], refs[counts[0]:sum(counts)], refs[sum(counts):]
    if last:
        gh_ref, dcol_ref, *refs = refs
    else:
        after_ref, *refs = refs
    grad_one, grad_two, db1_ref, held_one, held_two, gy_rows, total, sems_one, sems_two = refs
    copies_one = piece_copies(info, pieces_one, held_one, sems_one)
    copies_two = piece_copies(info, pieces_two, held_two, sems_two)
    load_pieces(step, BACK_ORDER[2:] if last else BACK_ORDER[:2], (copies_two, copies_one))

    @pl.when(step == 0)
    def first():
        gy_rows[...] = gy_ref[...].astype(F32).T.astype(BF16)
        db1_ref[...] = jnp.zeros_like(db1_ref)
        total[...] = before_ref[...] if last else jnp.zeros_like(total)

    slot = info[(7 if last else 5) + step]
    d_active = matmul(gy_rows[...], held_two[slot], 1, 1)
    d_inner = d_active * slope_ref[0].astype(F32)
    rounded = d_inner.astype(BF16)
    db1_ref[info[slot]] = jnp.sum(rounded.astype(F32), axis=0, keepdims=True)
    grad_two[0] = matmul(u_ref[0], gy_rows[...], 0, 0).astype(BF16)
    grad_one[0] = matmul(a2_ref[...], rounded).astype(BF16)
    total[...] += matmul(rounded, held_one[slot], 1, 1)

    @pl.when(step == 1)
    def end():
        if not last:
            after_ref[...] = total[...]
            return
        col = col_ref[...].reshape(D, 8)
        normed, inv_std = normalize(h_ref[...])
        d_mid = total[...].T
        upstream = gy_ref[...].astype(F32)
        d_hidden = upstream + norm_backward(d_mid, normed, inv_std, col[:, GAIN2 : GAIN2 + 1])
        gh_ref[...] = d_hidden
        dcol_ref[...] = columns(
            {
                GAIN2: row_sums(d_mid * normed),
                SHIFT2: row_sums(d_mid),
                BIAS_OUT: row_sums(d_hidden),
                BIAS_FC2: row_sums(upstream),
            }
        ).reshape(COLS)


def attention_backward_kernel(
    last, count, info, gh_ref, x_ref, a1_ref, col_ref, p_ref, soft_ref, o_ref, *refs
):
    step = pl.program_id(0)
    if last:
        before_ref, *refs = refs
    pieces, refs = refs[:count], refs[count:]
    if last:
        gx_ref, dcol_ref, *refs = refs
    else:
        after_ref, *refs = refs
    grad_ref, dbqv_ref, held, gh_rounded, g_p, total, sems = refs
    copies = piece_copies(info, pieces, held, sems)
    load_pieces(step, BACK_ORDER[2:] if last else BACK_ORDER[:2], (copies,))

    @pl.when(step == 0)
    def first():
        gh_rounded[...] = gh_ref[...].astype(BF16)
        dbqv_ref[...] = jnp.zeros_like(dbqv_ref)
        total[...] = before_ref[...] if last else jnp.zeros_like(total)

    slot = info[(7 if last else 5) + step]
    d_attended = matmul(held[slot, QKV:], gh_rounded[...]).astype(BF16)
    grad_ref[0, QKV:] = matmul(o_ref[0], gh_rounded[...], 1, 1).astype(BF16)
    for head in range(HEADS_SHARD):
        rows = slice(head * HD, (head + 1) * HD)
        queries = p_ref[0, rows]
        keys = p_ref[0, FEATS + head * HD : FEATS + (head + 1) * HD]
        values = p_ref[0, 2 * FEATS + head * HD : 2 * FEATS + (head + 1) * HD]
        soft = soft_ref[0, head]
        d_att = d_attended[rows]
        delta = jnp.sum(
            d_att.astype(F32) * o_ref[0, rows].astype(F32), axis=0, keepdims=True
        )
        d_soft = matmul(values, d_att, 0, 0)
        d_scores = (soft.astype(F32) * (d_soft - delta)).astype(BF16)
        g_p[rows] = (matmul(keys, d_scores) * SCALE).astype(BF16)
        g_p[FEATS + head * HD : FEATS + (head + 1) * HD] = (
            matmul(queries, d_scores, 1, 1) * SCALE
        ).astype(BF16)
        g_p[2 * FEATS + head * HD : 2 * FEATS + (head + 1) * HD] = matmul(
            d_att, soft, 1, 1
        ).astype(BF16)
    d_projected = g_p[...]
    grad_ref[0, :QKV] = matmul(d_projected, a1_ref[...], 1, 1).astype(BF16)
    total[...] += matmul(d_projected, held[slot, :QKV], 0, 0)
    dbqv_ref[info[slot]] = columns(
        {
            BIAS_Q: row_sums(d_projected[:FEATS].astype(F32)),
            BIAS_V: row_sums(d_projected[2 * FEATS :].astype(F32)),
        }
    )

    @pl.when(step == 1)
    def end():
        if not last:
            after_ref[...] = total[...]
            return
        col = col_ref[...].reshape(D, 8)
        normed, inv_std = normalize(x_ref[...].astype(F32))
        d_first = total[...].T
        gx_ref[...] = gh_ref[...] + norm_backward(
            d_first, normed, inv_std, col[:, GAIN1 : GAIN1 + 1]
        )
        dcol_ref[...] = columns(
            {GAIN1: row_sums(d_first * normed), SHIFT1: row_sums(d_first)}
        ).reshape(COLS)


def whole(shape):
    return pl.BlockSpec(shape, lambda i, info: (0,) * len(shape))


def by_step(shape):
    return pl.BlockSpec((1,) + shape, lambda i, info: (i,) + (0,) * len(shape))


def by_slot(shape, last):
    first = 7 if last else 5
    return pl.BlockSpec((1,) + shape, lambda i, info: (info[first + i],) + (0,) * len(shape))


PIECE = [pl.BlockSpec(memory_space=pltpu.HBM)]
COPY_SEMS = pltpu.SemaphoreType.DMA((2 * SHARDS,))
HELD = pltpu.VMEM((SHARDS, D, D), BF16)


def of(shape, dtype=BF16):
    return jax.ShapeDtypeStruct(shape, dtype)


def run(kernel, name, steps, info, operands, in_specs, outs, out_specs, scratch, flops):
    return pl.pallas_call(
        kernel,
        name=name,
        out_shape=outs,
        grid_spec=pltpu.PrefetchScalarGridSpec(
            num_scalar_prefetch=1,
            grid=(steps,),
            in_specs=in_specs,
            out_specs=out_specs,
            scratch_shapes=scratch,
        ),
        compiler_params=pltpu.CompilerParams(
            vmem_limit_bytes=VMEM_LIMIT, dimension_semantics=("arbitrary",)
        ),
        cost_estimate=pl.CostEstimate(flops=flops * 16, bytes_accessed=2**28, transcendentals=0),
    )(info, *operands)


STREAM = (D, FRAMES)
ROWS = (FRAMES, D)
COLS = (SHARDS, FEATS, 8)
ATT_FLOPS = 2 * FRAMES * D * (4 * D + 2 * FRAMES)
MLP_FLOPS = 4 * FRAMES * D * SHARDS * FF_SHARD


def attention_forward(info, x, col, chunk):
    return run(
        functools.partial(attention_forward_kernel, len(chunk)), "attention_forward", SHARDS, info, (x, col, *chunk),
        [whole(STREAM), whole(COLS)] + PIECE * len(chunk),
        [
            of(STREAM), of((SHARDS, QKV, FRAMES)), of((SHARDS, HEADS_SHARD, FRAMES, FRAMES)),
            of((SHARDS, FEATS, FRAMES)), of(STREAM, F32),
        ],
        [
            whole(STREAM), by_step((QKV, FRAMES)), by_step((HEADS_SHARD, FRAMES, FRAMES)),
            by_step((FEATS, FRAMES)), whole(STREAM),
        ],
        [HELD, COPY_SEMS],
        ATT_FLOPS,
    )


def mlp_forward(info, h, col, b1, chunk_one, chunk_two):
    return run(
        functools.partial(mlp_forward_kernel, (len(chunk_one), len(chunk_two))), "mlp_forward", SHARDS, info, (h, col, b1, *chunk_one, *chunk_two),
        [whole(STREAM), whole(COLS), whole((SHARDS, 1, FF_SHARD))] + PIECE * len(chunk_one + chunk_two),
        [of(STREAM), of((SHARDS, FRAMES, FF_SHARD)), of((SHARDS, FRAMES, FF_SHARD)), of(STREAM, F32)],
        [whole(STREAM), by_step((FRAMES, FF_SHARD)), by_step((FRAMES, FF_SHARD)), whole(STREAM)],
        [HELD, HELD, pltpu.VMEM(ROWS, BF16), pltpu.VMEM(ROWS, F32), COPY_SEMS, COPY_SEMS],
        MLP_FLOPS,
    )


def mlp_backward(info, gy, h, a2, col, u, slope, before, chunk_one, chunk_two):
    last = before is not None
    carried = (before,) if last else ()
    ends = [of(STREAM, F32), of(COLS, F32)] if last else [of(ROWS, F32)]
    return run(
        functools.partial(mlp_backward_kernel, last, (len(chunk_one), len(chunk_two))), "mlp_backward", 2, info,
        (gy, h, a2, col, u, slope, *carried, *chunk_one, *chunk_two),
        [
            whole(STREAM), whole(STREAM), whole(STREAM), whole(COLS),
            by_slot((FRAMES, FF_SHARD), last), by_slot((FRAMES, FF_SHARD), last),
        ]
        + [whole(ROWS)] * len(carried)
        + PIECE * len(chunk_one + chunk_two),
        ends + [of((2, D, D)), of((2, D, D)), of((SHARDS, 1, FF_SHARD), F32)],
        [whole(end.shape) for end in ends]
        + [by_step((D, D)), by_step((D, D)), whole((SHARDS, 1, FF_SHARD))],
        [HELD, HELD, pltpu.VMEM(ROWS, BF16), pltpu.VMEM(ROWS, F32), COPY_SEMS, COPY_SEMS],
        MLP_FLOPS,
    )


def attention_backward(info, gh, x, a1, col, p, soft, o, before, chunk):
    last = before is not None
    carried = (before,) if last else ()
    ends = [of(STREAM, F32), of(COLS, F32)] if last else [of(ROWS, F32)]
    return run(
        functools.partial(attention_backward_kernel, last, len(chunk)), "attention_backward", 2, info,
        (gh, x, a1, col, p, soft, o, *carried, *chunk),
        [
            whole(STREAM), whole(STREAM), whole(STREAM), whole(COLS),
            by_slot((QKV, FRAMES), last), by_slot((HEADS_SHARD, FRAMES, FRAMES), last),
            by_slot((FEATS, FRAMES), last),
        ]
        + [whole(ROWS)] * len(carried)
        + PIECE * len(chunk),
        ends + [of((2, D, D)), of(COLS, F32)],
        [whole(end.shape) for end in ends] + [by_step((D, D)), whole(COLS)],
        [HELD, pltpu.VMEM(STREAM, BF16), pltpu.VMEM((QKV, FRAMES), BF16), pltpu.VMEM(ROWS, F32), COPY_SEMS],
        ATT_FLOPS,
    )


def tie(groups):
    return lax.optimization_barrier(groups)


def flip(block, axis, bit):
    size = lax.axis_size(axis)
    return lax.ppermute(block, axis, [(i, i ^ bit) for i in range(size)])


def added(left, right):
    return (left.astype(F32) + right.astype(F32)).astype(BF16)


def sum_kernel(left_ref, right_ref, *out_refs):
    for index, out_ref in enumerate(out_refs):
        place = index if len(out_refs) > 1 else Ellipsis
        out_ref[...] = added(left_ref[place], right_ref[place])


def summed(left, right, outs):
    rows = left.shape[-2]
    block = 384 if rows % 384 == 0 else rows
    spec = pl.BlockSpec((block, D), lambda i: (i, 0))
    pair = pl.BlockSpec((2, block, D), lambda i: (0, i, 0))
    return pl.pallas_call(
        sum_kernel,
        name="row_sums",
        grid=(rows // block,),
        in_specs=[pair if outs == 2 else spec] * 2,
        out_specs=[spec] * outs,
        out_shape=[jax.ShapeDtypeStruct((rows, D), BF16)] * outs,
        compiler_params=pltpu.CompilerParams(vmem_limit_bytes=VMEM_LIMIT // 4),
        cost_estimate=pl.CostEstimate(flops=2**36, bytes_accessed=2**28, transcendentals=0),
    )(left, right)


def with_rows(blocks, small):
    pad = ((0, 0), (0, 16 - small.shape[1]), (0, blocks.shape[2] - small.shape[2]))
    return jnp.concatenate([blocks, jnp.pad(small.astype(BF16), pad)], axis=1)


def rows_of(value, place, parts):
    size = value.shape[-2] // parts
    return lax.dynamic_slice_in_dim(value, place * size, size, axis=value.ndim - 2)


class Chain:
    def start(self, send):
        self.arrived = flip(send, "tensor", 1)

    def cores(self, keep):
        self.value = summed(keep, self.arrived, 2)

    def scatter(self):
        parts = lax.axis_size("dp")
        both = self.value if isinstance(self.value, (list, tuple)) else [self.value]
        split = jnp.stack([value.reshape(parts, -1, D) for value in both], axis=1)
        total = lax.psum_scatter(split, "dp", scatter_dimension=0, tiled=False)
        self.value = total if len(both) == 2 else total[0]

    def send_y(self):
        self.kept, self.arrived = self.value[1], flip(self.value[0], "tensor", 2)

    def fold_rows(self):
        rows = self.kept.shape
        (total,) = summed(self.kept.reshape(-1, D), self.arrived.reshape(-1, D), 1)
        self.value = total.reshape(rows)

    def send_x(self, first, second):
        section = lax.axis_index("section")
        self.kept = jnp.where(section == 0, first.value, second.value)
        self.arrived = flip(jnp.where(section == 0, second.value, first.value), "section", 1)

    def fold(self):
        self.value = added(self.kept, self.arrived)

    def split(self):
        self.value = self.value.reshape(lax.axis_size("dp"), -1, D)

    def send_half(self, bit):
        mine = ((lax.axis_index("dp") & bit) != 0).astype(jnp.int32)
        blocks = self.value.reshape(-1, 2, *self.value.shape[1:])
        self.kept = lax.dynamic_index_in_dim(blocks, mine, 1, keepdims=False)
        self.arrived = flip(
            lax.dynamic_index_in_dim(blocks, 1 - mine, 1, keepdims=False), "dp", bit
        )

    def send_back(self, bit):
        self.arrived = flip(self.value, "dp", bit)

    def join(self, bit):
        upper = (lax.axis_index("dp") & bit) != 0
        rows = []
        for arrived, value in zip(self.arrived, self.value):
            rows += [jnp.where(upper, arrived, value), jnp.where(upper, value, arrived)]
        self.value = jnp.concatenate(rows, axis=0).reshape(len(rows), -1, D)


def tied(chains, *others):
    values = tie((tuple(chain.value for chain in chains), others))
    for chain, value in zip(chains, values[0]):
        chain.value = value
    return values[1]


def body(ends_in, ln_gain, ln_shift, w_qkv, b_qv, w_out, b_out, w_fc1, b_fc1, w_fc2, b_fc2):
    section = lax.axis_index("section")
    shard = lax.axis_index("tensor")
    zhalf = lax.axis_index("dp") % 2
    clips = ends_in.shape[1] // FRAMES
    info = jnp.stack(
        [shard, shard ^ 1, shard ^ 2, shard ^ 3, zhalf] + [jnp.int32(k) for k in BACK_ORDER]
    ).astype(jnp.int32)

    owned = [
        jnp.concatenate([w_qkv[0].transpose(1, 2, 0).reshape(QKV, D), w_out[0]], axis=0),
        w_fc1[0],
        w_fc2[0],
    ]
    nears = [rows_of(own, zhalf, 2) for own in owned]
    fars = [rows_of(own, 1 - zhalf, 2) for own in owned]
    beyond_a = flip(nears[0], "section", 1)

    small = jnp.concatenate(
        [ln_gain[0], ln_shift[0], b_qv[0], b_out, b_fc2, b_fc1.reshape(SHARDS, FEATS)], axis=0
    )
    ends = ends_in[0].T.reshape(FEATS, clips, FRAMES).transpose(1, 0, 2)
    ends = with_rows(ends, jnp.broadcast_to(small, (clips,) + small.shape))
    beyond_a, near_one, ends = tie((beyond_a, nears[1], ends))
    ends = lax.all_to_all(ends, ("section", "tensor"), split_axis=0, concat_axis=0, tiled=True)
    small = ends[:, FEATS : FEATS + 12, :FEATS].astype(F32)
    cols = jnp.swapaxes(small[:, :8], 1, 2).reshape(2, SHARDS, FEATS, 8)
    b1s = small[:, 8:].reshape(2, SHARDS, 1, FF_SHARD)
    ends = ends[:, :FEATS].reshape(2, D, FRAMES)

    def layers(own, other):
        return jnp.where(section == 0, own, other), jnp.where(section == 0, other, own)

    def over_y(block):
        return flip(block, "tensor", 2)

    def chunk_of(own, there):
        return tuple(
            part for pair in (own, there) for parts in (pair, [flip(x, "tensor", 1) for x in pair])
            for part in parts
        )

    n_dp = lax.axis_size("dp")
    beyond_one = flip(near_one, "section", 1)
    near_a = layers(nears[0], beyond_a)
    far_a = layers(fars[0], flip(beyond_a, "dp", 1))
    there_a = over_y(near_a[0])
    there_a, beyond_one, own_two = tie((there_a, beyond_one, owned[2]))
    beyond_two = flip(own_two, "section", 1)
    away_a = flip(there_a, "dp", 1)
    near_one = layers(nears[1], beyond_one)
    beyond_far_one = flip(beyond_one, "dp", 1)
    there_one = over_y(near_one[0])

    def attend(layer, stream, chunk):
        return attention_forward(info, stream, cols[layer], chunk)

    def feed(layer, h, chunk_one, chunk_two):
        return mlp_forward(info, h, cols[layer], b1s[layer], chunk_one, chunk_two)

    there_one, beyond_two = tie((there_one, beyond_two))
    away_one = flip(there_one, "dp", 1)
    near_two = layers(nears[2], rows_of(beyond_two, zhalf, 2))
    far_two = layers(fars[2], rows_of(beyond_two, 1 - zhalf, 2))
    there_two = over_y(near_two[0])
    chunks = [[chunk_of((near_a[0], far_a[0]), (there_a, away_a))], []]
    stream = ends[0]
    a1, p, soft, o, h = attend(0, stream, chunks[0][0])
    h, away_one, there_two, beyond_far_one, late_a, late_far_a, late_one, late_two = tie(
        (h, away_one, there_two, beyond_far_one, near_a[1], far_a[1], near_one[1], (near_two[1], far_two[1]))
    )
    far_one = layers(fars[1], beyond_far_one)
    chunks[0].append(chunk_of((near_one[0], far_one[0]), (there_one, away_one)))
    chunks[0].append(chunk_of((near_two[0], far_two[0]), (there_two, flip(there_two, "dp", 1))))
    there_a, there_one = over_y(late_a), over_y(late_one)
    there_two, away_two = over_y(late_two[0]), over_y(late_two[1])
    away_a = flip(there_a, "dp", 1)
    a2, u, slope, y = feed(0, h, *chunks[0][1:])
    stored = [(stream, a1, p, soft, o, h, a2, u, slope)]
    stream, there_a, away_a, there_one, late_a, late_far_a = tie(
        (y, there_a, away_a, there_one, late_a, late_far_a)
    )
    chunks[1].append(chunk_of((late_a, late_far_a), (there_a, away_a)))
    away_one = flip(there_one, "dp", 1)
    a1, p, soft, o, h = attend(1, stream, chunks[1][0])
    h, late = tie(
        (
            h,
            (late_one, far_one[1], there_one, away_one, *late_two, there_two, away_two),
        )
    )
    chunks[1].append(chunk_of(late[0:2], late[2:4]))
    chunks[1].append(chunk_of(late[4:6], late[6:8]))
    a2, u, slope, y = feed(1, h, *chunks[1][1:])
    stored.append((stream, a1, p, soft, o, h, a2, u, slope))
    stream = y

    upstream = ends[1]
    bits = [1 << k for k in range(n_dp.bit_length() - 1)]
    chains = [[Chain() for _ in range(3)] for _ in range(2)]
    smalls = [None, None]
    ends_of = [None, None]
    late_a, late_one, late_two = chains[1]
    last_a, last_one, last_two = chains[0]
    for layer in (1, 0):
        chunk_a, chunk_one, chunk_two = chunks[layer]
        x, a1, p, soft, o, h, a2, u, slope = stored[layer]
        chain_a, chain_one, chain_two = chains[layer]
        after, send_one, send_two, db1_sent = mlp_backward(
            info, upstream, h, a2, cols[layer], u, slope, None, chunk_one, chunk_two
        )
        chain_two.start(send_two)
        chain_one.start(send_one)
        gh, dcol_two, keep_one, keep_two, db1_kept = mlp_backward(
            info, upstream, h, a2, cols[layer], u, slope, after, chunk_one, chunk_two
        )
        chain_two.cores(keep_two)
        chain_one.cores(keep_one)
        if layer == 0:
            late_a.fold_rows()
            (gh,) = tied((late_a, last_two, last_one, late_one), gh)
            late_a.split()
            late_a.send_half(bits[0])
            last_two.send_y()
            last_one.send_y()
        else:
            (gh,) = tied((late_two, late_one), gh)
            late_one.scatter()
            late_two.send_y()
        after, send_a, dbqv_sent = attention_backward(
            info, gh, x, a1, cols[layer], p, soft, o, None, chunk_a
        )
        chain_a.start(send_a)
        upstream, dcol_one, keep_a, dbqv_kept = attention_backward(
            info, gh, x, a1, cols[layer], p, soft, o, after, chunk_a
        )
        chain_a.cores(keep_a)
        ends_of[layer] = (db1_kept, db1_sent, (dbqv_kept, dbqv_sent, dcol_one, dcol_two))
        if layer == 1:
            late_two.fold_rows()
            (upstream,) = tied((late_two, late_a), upstream)
            late_two.scatter()
            late_a.send_y()
        else:
            last_two.fold_rows()
            late_a.fold()
            upstream, ends_of = tied((last_two, last_a, late_two, late_a), upstream, ends_of)
            for bit in bits[1:]:
                late_a.send_half(bit)
                if bit != bits[-1]:
                    late_a.fold()
            last_two.scatter()
            last_a.send_y()
            late_one.send_y()

    pair_two, pair_one, pair_a = Chain(), Chain(), Chain()

    def start_far(pair):
        pair.value = pair.value[None]
        pair.send_back(bits[-1])

    def finish_far(pair):
        pair.join(bits[-1])
        for bit in bits[-2:0:-1]:
            pair.send_back(bit)
            pair.join(bit)

    for layer in range(2):
        db1_kept, db1_sent, dcols = ends_of[layer]
        smalls[layer] = jnp.concatenate(
            [
                jnp.swapaxes(sum(dcols), 1, 2),
                (db1_kept + db1_sent).reshape(SHARDS, SHARDS, FEATS),
            ],
            axis=1,
        )
    result = jnp.stack([upstream.astype(BF16), stream.astype(BF16)])
    result = with_rows(
        result.reshape(2 * SHARDS, FEATS, FRAMES), jnp.stack(smalls).reshape(-1, 12, FEATS)
    )
    late_a.fold()
    late_a.value = late_a.value[0]
    result, last_one.arrived = tied((last_two, late_two, late_a), result, last_one.arrived)
    last_one.fold_rows()
    late_one.fold()
    tied((last_one, late_one, last_two, late_two))
    last_one.scatter()
    pair_two.send_x(last_two, late_two)
    result = lax.all_to_all(result, ("section", "tensor"), split_axis=0, concat_axis=0, tiled=True)

    last_a.fold_rows()
    tied((last_a,))
    last_a.split()
    last_a.send_half(bits[0])
    pair_two.fold()
    start_far(pair_two)

    last_a.fold()
    (pair_two.arrived,) = tied((last_a,), pair_two.arrived)
    for bit in bits[1:]:
        last_a.send_half(bit)
        if bit != bits[-1]:
            last_a.fold()
    finish_far(pair_two)
    (result,) = tied((pair_two,), result)
    pair_two.send_back(bits[0])

    last_a.fold()
    last_a.value = last_a.value[0]
    pair_a.send_x(last_a, late_a)
    pair_one.send_x(last_one, late_one)
    pair_a.fold()
    pair_one.fold()
    result, pair_two.arrived = tied((pair_a, pair_one), result, pair_two.arrived)
    start_far(pair_a)
    start_far(pair_one)
    small_sum = result[:, FEATS : FEATS + 12, :FEATS].astype(F32).sum(axis=0)
    small_parts = [flip(small_sum, "dp", k) for k in range(1, n_dp)] if n_dp <= 4 else None
    pair_two.join(bits[0])

    finish_far(pair_a)
    (pair_one.arrived,) = tied((pair_a,), pair_one.arrived)
    pair_a.send_back(bits[0])
    finish_far(pair_one)
    (result,) = tied((pair_one,), result)
    pair_one.send_back(bits[0])
    result = result[:, :FEATS].transpose(1, 0, 2).reshape(FEATS, clips * FRAMES).T.astype(F32)
    pair_a.join(bits[0])
    if small_parts is None:
        small_sum = lax.psum(small_sum, "dp")
    else:
        small_parts, pair_a.value = tie((small_parts, pair_a.value))
        small_sum = sum(small_parts, small_sum)
    pair_one.join(bits[0])
    for pair in (pair_two, pair_one, pair_a):
        pair.value = pair.value.reshape(D, D)

    grad_a, grad_one, grad_two = [pair.value.astype(F32) for pair in (pair_a, pair_one, pair_two)]
    return (
        result[None],
        small_sum[None, 0:2],
        small_sum[None, 2:4],
        grad_a[:QKV].reshape(3, FEATS, D).transpose(2, 0, 1)[None],
        small_sum[None, 4:6],
        grad_a[QKV:][None],
        small_sum[6:7],
        grad_one[None],
        small_sum[8:12].reshape(1, FF_SHARD),
        grad_two[None],
        small_sum[7:8],
    )


def solution(mesh):
    placed = (
        P("section", "dp", "tensor"),
        P("section", None, "tensor"),
        P("section", None, "tensor"),
        P("section", None, None, "tensor"),
        P("section", None, "tensor"),
        P("section", "tensor", None),
        P("section", "tensor"),
        P("section", None, "tensor"),
        P("section", "tensor"),
        P("section", "tensor", None),
        P("section", "tensor"),
    )
    return jax.shard_map(
        body, mesh=mesh, in_specs=placed, out_specs=placed, check_vma=False
    )
```

```python
import functools

import jax
import jax.numpy as jnp
from jax import lax
from jax.experimental import pallas as pl
from jax.experimental.pallas import tpu as pltpu
from jax.sharding import PartitionSpec as P

D = 768
HD = 64
FRAMES = 448
SHARDS = 4
HEADS_SHARD = 3
FEATS = HEADS_SHARD * HD
QKV = 3 * FEATS
FF_SHARD = 768
HALF = D // 2
EPSILON = 1e-05
SCALE = float(HD) ** (-0.5)
VMEM_LIMIT = 60 * 1024 * 1024
GAIN1, GAIN2, SHIFT1, SHIFT2, BIAS_Q, BIAS_V, BIAS_OUT, BIAS_FC2 = range(8)
BACK_ORDER = (3, 1, 2, 0)
F32 = jnp.float32
BF16 = jnp.bfloat16


def matmul(left, right, left_dim=1, right_dim=0):
    return lax.dot_general(
        left, right, (((left_dim,), (right_dim,)), ((), ())), preferred_element_type=F32
    )


def normalize(values):
    center = jnp.mean(values, axis=0, keepdims=True)
    moved = values - center
    inv_std = lax.rsqrt(jnp.mean(moved * moved, axis=0, keepdims=True) + EPSILON)
    return moved * inv_std, inv_std


def norm_backward(upstream, normed, inv_std, gain):
    scaled = upstream * gain
    mean_one = jnp.mean(scaled, axis=0, keepdims=True)
    mean_two = jnp.mean(scaled * normed, axis=0, keepdims=True)
    return inv_std * (scaled - mean_one - normed * mean_two)


def row_sums(values):
    return jnp.sum(values, axis=1, keepdims=True)


def columns(parts):
    rows = next(iter(parts.values())).shape[0]
    lane = lax.broadcasted_iota(jnp.int32, (rows, 8), 1)
    total = jnp.zeros((rows, 8), F32)
    for index, part in parts.items():
        total = jnp.where(lane == index, part, total)
    return total


def piece_copies(info, pieces, held, sems):
    first = pl.multiple_of(info[4] * HALF, HALF)
    second = pl.multiple_of((1 - info[4]) * HALF, HALF)
    copies, taken = [], 0
    for slot in range(SHARDS):
        targets = [held.at[slot]]
        if pieces[taken].shape[0] == HALF:
            targets = [held.at[slot, pl.ds(first, HALF)], held.at[slot, pl.ds(second, HALF)]]
        copies.append(
            tuple(
                pltpu.make_async_copy(pieces[taken + k], target, sems.at[2 * slot + k])
                for k, target in enumerate(targets)
            )
        )
        taken += len(targets)
    return tuple(copies)


def load_pieces(step, order, chunks):
    @pl.when(step == 0)
    def start():
        for slot in order:
            for chunk in chunks:
                for copy in chunk[slot]:
                    copy.start()

    for index, slot in enumerate(order):

        @pl.when(step == index)
        def wait():
            for chunk in chunks:
                for copy in chunk[slot]:
                    copy.wait()


def attention_forward_kernel(
    count, info, x_ref, col_ref, *refs
):
    step = pl.program_id(0)
    pieces, (a1_ref, p_ref, soft_ref, o_ref, h_ref, held, sems) = refs[:count], refs[count:]
    copies = piece_copies(info, pieces, held, sems)
    load_pieces(step, range(SHARDS), (copies,))

    @pl.when(step == 0)
    def first():
        col = col_ref[...].reshape(D, 8)
        values = x_ref[...].astype(F32)
        normed, _ = normalize(values)
        a1_ref[...] = (
            normed * col[:, GAIN1 : GAIN1 + 1] + col[:, SHIFT1 : SHIFT1 + 1]
        ).astype(BF16)
        h_ref[...] = values + col[:, BIAS_OUT : BIAS_OUT + 1]

    bias = col_ref[info[step]]
    projected = matmul(held[step, :QKV], a1_ref[...])
    queries = (projected[:FEATS] + bias[:, BIAS_Q : BIAS_Q + 1]).astype(BF16)
    keys = projected[FEATS : 2 * FEATS].astype(BF16)
    values = (projected[2 * FEATS :] + bias[:, BIAS_V : BIAS_V + 1]).astype(BF16)
    p_ref[0, :FEATS] = queries
    p_ref[0, FEATS : 2 * FEATS] = keys
    p_ref[0, 2 * FEATS :] = values
    scaled = queries * SCALE
    for head in range(HEADS_SHARD):
        rows = slice(head * HD, (head + 1) * HD)
        scores = matmul(keys[rows], scaled[rows], 0, 0)
        exps = jnp.exp(scores - jnp.max(scores, axis=0, keepdims=True))
        soft = exps * (1.0 / jnp.sum(exps, axis=0, keepdims=True))
        soft = soft.astype(BF16)
        soft_ref[0, head] = soft
        o_ref[0, rows] = matmul(values[rows], soft).astype(BF16)
    h_ref[...] += matmul(held[step, QKV:], o_ref[0], 0, 0)


def mlp_forward_kernel(
    counts, info, h_ref, col_ref, b1_ref, *refs
):
    step = pl.program_id(0)
    pieces_one, pieces_two, refs = refs[:counts[0]], refs[counts[0]:sum(counts)], refs[sum(counts):]
    a2_ref, u_ref, slope_ref, y_ref, held_one, held_two, a2_rows, total, sems_one, sems_two = refs
    copies_one = piece_copies(info, pieces_one, held_one, sems_one)
    copies_two = piece_copies(info, pieces_two, held_two, sems_two)
    load_pieces(step, range(SHARDS), (copies_one, copies_two))

    @pl.when(step == 0)
    def first():
        col = col_ref[...].reshape(D, 8)
        normed, _ = normalize(h_ref[...])
        scaled = normed * col[:, GAIN2 : GAIN2 + 1] + col[:, SHIFT2 : SHIFT2 + 1]
        a2_ref[...] = scaled.astype(BF16)
        a2_rows[...] = scaled.T.astype(BF16)
        total[...] = jnp.zeros_like(total)

    inner = matmul(a2_rows[...], held_one[step]) + b1_ref[info[step]]
    phi = 0.5 + 0.5 * lax.erf(inner * 0.7071067811865476)
    density = 0.3989422804014327 * jnp.exp(-0.5 * inner * inner)
    active = (inner * phi).astype(BF16)
    u_ref[0] = active
    slope_ref[0] = (phi + inner * density).astype(BF16)
    total[...] += matmul(active, held_two[step])

    @pl.when(step == SHARDS - 1)
    def last():
        col = col_ref[...].reshape(D, 8)
        y_ref[...] = h_ref[...] + total[...].T + col[:, BIAS_FC2 : BIAS_FC2 + 1]


def mlp_backward_kernel(
    last, counts, info, gy_ref, h_ref, a2_ref, col_ref, u_ref, slope_ref, *refs
):
    step = pl.program_id(0)
    if last:
        before_ref, *refs = refs
    pieces_one, pieces_two, refs = refs[:counts[0]], refs[counts[0]:sum(counts)], refs[sum(counts):]
    if last:
        gh_ref, dcol_ref, *refs = refs
    else:
        after_ref, *refs = refs
    grad_one, grad_two, db1_ref, held_one, held_two, gy_rows, total, sems_one, sems_two = refs
    copies_one = piece_copies(info, pieces_one, held_one, sems_one)
    copies_two = piece_copies(info, pieces_two, held_two, sems_two)
    load_pieces(step, BACK_ORDER[2:] if last else BACK_ORDER[:2], (copies_two, copies_one))

    @pl.when(step == 0)
    def first():
        gy_rows[...] = gy_ref[...].astype(F32).T.astype(BF16)
        db1_ref[...] = jnp.zeros_like(db1_ref)
        total[...] = before_ref[...] if last else jnp.zeros_like(total)

    slot = info[(7 if last else 5) + step]
    d_active = matmul(gy_rows[...], held_two[slot], 1, 1)
    d_inner = d_active * slope_ref[0].astype(F32)
    rounded = d_inner.astype(BF16)
    db1_ref[info[slot]] = jnp.sum(rounded.astype(F32), axis=0, keepdims=True)
    grad_two[0] = matmul(u_ref[0], gy_rows[...], 0, 0).astype(BF16)
    grad_one[0] = matmul(a2_ref[...], rounded).astype(BF16)
    total[...] += matmul(rounded, held_one[slot], 1, 1)

    @pl.when(step == 1)
    def end():
        if not last:
            after_ref[...] = total[...]
            return
        col = col_ref[...].reshape(D, 8)
        normed, inv_std = normalize(h_ref[...])
        d_mid = total[...].T
        upstream = gy_ref[...].astype(F32)
        d_hidden = upstream + norm_backward(d_mid, normed, inv_std, col[:, GAIN2 : GAIN2 + 1])
        gh_ref[...] = d_hidden
        dcol_ref[...] = columns(
            {
                GAIN2: row_sums(d_mid * normed),
                SHIFT2: row_sums(d_mid),
                BIAS_OUT: row_sums(d_hidden),
                BIAS_FC2: row_sums(upstream),
            }
        ).reshape(COLS)


def attention_backward_kernel(
    last, count, info, gh_ref, x_ref, a1_ref, col_ref, p_ref, soft_ref, o_ref, *refs
):
    step = pl.program_id(0)
    if last:
        before_ref, *refs = refs
    pieces, refs = refs[:count], refs[count:]
    if last:
        gx_ref, dcol_ref, *refs = refs
    else:
        after_ref, *refs = refs
    grad_ref, dbqv_ref, held, gh_rounded, g_p, total, sems = refs
    copies = piece_copies(info, pieces, held, sems)
    load_pieces(step, BACK_ORDER[2:] if last else BACK_ORDER[:2], (copies,))

    @pl.when(step == 0)
    def first():
        gh_rounded[...] = gh_ref[...].astype(BF16)
        dbqv_ref[...] = jnp.zeros_like(dbqv_ref)
        total[...] = before_ref[...] if last else jnp.zeros_like(total)

    slot = info[(7 if last else 5) + step]
    d_attended = matmul(held[slot, QKV:], gh_rounded[...]).astype(BF16)
    grad_ref[0, QKV:] = matmul(o_ref[0], gh_rounded[...], 1, 1).astype(BF16)
    for head in range(HEADS_SHARD):
        rows = slice(head * HD, (head + 1) * HD)
        queries = p_ref[0, rows]
        keys = p_ref[0, FEATS + head * HD : FEATS + (head + 1) * HD]
        values = p_ref[0, 2 * FEATS + head * HD : 2 * FEATS + (head + 1) * HD]
        soft = soft_ref[0, head]
        d_att = d_attended[rows]
        delta = jnp.sum(
            d_att.astype(F32) * o_ref[0, rows].astype(F32), axis=0, keepdims=True
        )
        d_soft = matmul(values, d_att, 0, 0)
        d_scores = (soft.astype(F32) * (d_soft - delta)).astype(BF16)
        g_p[rows] = (matmul(keys, d_scores) * SCALE).astype(BF16)
        g_p[FEATS + head * HD : FEATS + (head + 1) * HD] = (
            matmul(queries, d_scores, 1, 1) * SCALE
        ).astype(BF16)
        g_p[2 * FEATS + head * HD : 2 * FEATS + (head + 1) * HD] = matmul(
            d_att, soft, 1, 1
        ).astype(BF16)
    d_projected = g_p[...]
    grad_ref[0, :QKV] = matmul(d_projected, a1_ref[...], 1, 1).astype(BF16)
    total[...] += matmul(d_projected, held[slot, :QKV], 0, 0)
    dbqv_ref[info[slot]] = columns(
        {
            BIAS_Q: row_sums(d_projected[:FEATS].astype(F32)),
            BIAS_V: row_sums(d_projected[2 * FEATS :].astype(F32)),
        }
    )

    @pl.when(step == 1)
    def end():
        if not last:
            after_ref[...] = total[...]
            return
        col = col_ref[...].reshape(D, 8)
        normed, inv_std = normalize(x_ref[...].astype(F32))
        d_first = total[...].T
        gx_ref[...] = gh_ref[...] + norm_backward(
            d_first, normed, inv_std, col[:, GAIN1 : GAIN1 + 1]
        )
        dcol_ref[...] = columns(
            {GAIN1: row_sums(d_first * normed), SHIFT1: row_sums(d_first)}
        ).reshape(COLS)


def whole(shape):
    return pl.BlockSpec(shape, lambda i, info: (0,) * len(shape))


def by_step(shape):
    return pl.BlockSpec((1,) + shape, lambda i, info: (i,) + (0,) * len(shape))


def by_slot(shape, last):
    first = 7 if last else 5
    return pl.BlockSpec((1,) + shape, lambda i, info: (info[first + i],) + (0,) * len(shape))


PIECE = [pl.BlockSpec(memory_space=pltpu.HBM)]
COPY_SEMS = pltpu.SemaphoreType.DMA((2 * SHARDS,))
HELD = pltpu.VMEM((SHARDS, D, D), BF16)


def of(shape, dtype=BF16):
    return jax.ShapeDtypeStruct(shape, dtype)


def run(kernel, name, steps, info, operands, in_specs, outs, out_specs, scratch, flops):
    return pl.pallas_call(
        kernel,
        name=name,
        out_shape=outs,
        grid_spec=pltpu.PrefetchScalarGridSpec(
            num_scalar_prefetch=1,
            grid=(steps,),
            in_specs=in_specs,
            out_specs=out_specs,
            scratch_shapes=scratch,
        ),
        compiler_params=pltpu.CompilerParams(
            vmem_limit_bytes=VMEM_LIMIT, dimension_semantics=("arbitrary",)
        ),
        cost_estimate=pl.CostEstimate(flops=flops * 16, bytes_accessed=2**28, transcendentals=0),
    )(info, *operands)


STREAM = (D, FRAMES)
ROWS = (FRAMES, D)
COLS = (SHARDS, FEATS, 8)
ATT_FLOPS = 2 * FRAMES * D * (4 * D + 2 * FRAMES)
MLP_FLOPS = 4 * FRAMES * D * SHARDS * FF_SHARD


def attention_forward(info, x, col, chunk):
    return run(
        functools.partial(attention_forward_kernel, len(chunk)), "attention_forward", SHARDS, info, (x, col, *chunk),
        [whole(STREAM), whole(COLS)] + PIECE * len(chunk),
        [
            of(STREAM), of((SHARDS, QKV, FRAMES)), of((SHARDS, HEADS_SHARD, FRAMES, FRAMES)),
            of((SHARDS, FEATS, FRAMES)), of(STREAM, F32),
        ],
        [
            whole(STREAM), by_step((QKV, FRAMES)), by_step((HEADS_SHARD, FRAMES, FRAMES)),
            by_step((FEATS, FRAMES)), whole(STREAM),
        ],
        [HELD, COPY_SEMS],
        ATT_FLOPS,
    )


def mlp_forward(info, h, col, b1, chunk_one, chunk_two):
    return run(
        functools.partial(mlp_forward_kernel, (len(chunk_one), len(chunk_two))), "mlp_forward", SHARDS, info, (h, col, b1, *chunk_one, *chunk_two),
        [whole(STREAM), whole(COLS), whole((SHARDS, 1, FF_SHARD))] + PIECE * len(chunk_one + chunk_two),
        [of(STREAM), of((SHARDS, FRAMES, FF_SHARD)), of((SHARDS, FRAMES, FF_SHARD)), of(STREAM, F32)],
        [whole(STREAM), by_step((FRAMES, FF_SHARD)), by_step((FRAMES, FF_SHARD)), whole(STREAM)],
        [HELD, HELD, pltpu.VMEM(ROWS, BF16), pltpu.VMEM(ROWS, F32), COPY_SEMS, COPY_SEMS],
        MLP_FLOPS,
    )


def mlp_backward(info, gy, h, a2, col, u, slope, before, chunk_one, chunk_two):
    last = before is not None
    carried = (before,) if last else ()
    ends = [of(STREAM, F32), of(COLS, F32)] if last else [of(ROWS, F32)]
    return run(
        functools.partial(mlp_backward_kernel, last, (len(chunk_one), len(chunk_two))), "mlp_backward", 2, info,
        (gy, h, a2, col, u, slope, *carried, *chunk_one, *chunk_two),
        [
            whole(STREAM), whole(STREAM), whole(STREAM), whole(COLS),
            by_slot((FRAMES, FF_SHARD), last), by_slot((FRAMES, FF_SHARD), last),
        ]
        + [whole(ROWS)] * len(carried)
        + PIECE * len(chunk_one + chunk_two),
        ends + [of((2, D, D)), of((2, D, D)), of((SHARDS, 1, FF_SHARD), F32)],
        [whole(end.shape) for end in ends]
        + [by_step((D, D)), by_step((D, D)), whole((SHARDS, 1, FF_SHARD))],
        [HELD, HELD, pltpu.VMEM(ROWS, BF16), pltpu.VMEM(ROWS, F32), COPY_SEMS, COPY_SEMS],
        MLP_FLOPS,
    )


def attention_backward(info, gh, x, a1, col, p, soft, o, before, chunk):
    last = before is not None
    carried = (before,) if last else ()
    ends = [of(STREAM, F32), of(COLS, F32)] if last else [of(ROWS, F32)]
    return run(
        functools.partial(attention_backward_kernel, last, len(chunk)), "attention_backward", 2, info,
        (gh, x, a1, col, p, soft, o, *carried, *chunk),
        [
            whole(STREAM), whole(STREAM), whole(STREAM), whole(COLS),
            by_slot((QKV, FRAMES), last), by_slot((HEADS_SHARD, FRAMES, FRAMES), last),
            by_slot((FEATS, FRAMES), last),
        ]
        + [whole(ROWS)] * len(carried)
        + PIECE * len(chunk),
        ends + [of((2, D, D)), of(COLS, F32)],
        [whole(end.shape) for end in ends] + [by_step((D, D)), whole(COLS)],
        [HELD, pltpu.VMEM(STREAM, BF16), pltpu.VMEM((QKV, FRAMES), BF16), pltpu.VMEM(ROWS, F32), COPY_SEMS],
        ATT_FLOPS,
    )


def tie(groups):
    return lax.optimization_barrier(groups)


def flip(block, axis, bit):
    size = lax.axis_size(axis)
    return lax.ppermute(block, axis, [(i, i ^ bit) for i in range(size)])


def added(left, right):
    return (left.astype(F32) + right.astype(F32)).astype(BF16)


def sum_kernel(left_ref, right_ref, *out_refs):
    for index, out_ref in enumerate(out_refs):
        place = index if len(out_refs) > 1 else Ellipsis
        out_ref[...] = added(left_ref[place], right_ref[place])


def summed(left, right, outs):
    rows = left.shape[-2]
    block = 384 if rows % 384 == 0 else rows
    spec = pl.BlockSpec((block, D), lambda i: (i, 0))
    pair = pl.BlockSpec((2, block, D), lambda i: (0, i, 0))
    return pl.pallas_call(
        sum_kernel,
        name="row_sums",
        grid=(rows // block,),
        in_specs=[pair if outs == 2 else spec] * 2,
        out_specs=[spec] * outs,
        out_shape=[jax.ShapeDtypeStruct((rows, D), BF16)] * outs,
        compiler_params=pltpu.CompilerParams(vmem_limit_bytes=VMEM_LIMIT // 4),
        cost_estimate=pl.CostEstimate(flops=2**36, bytes_accessed=2**28, transcendentals=0),
    )(left, right)


def with_rows(blocks, small):
    pad = ((0, 0), (0, 16 - small.shape[1]), (0, blocks.shape[2] - small.shape[2]))
    return jnp.concatenate([blocks, jnp.pad(small.astype(BF16), pad)], axis=1)


def rows_of(value, place, parts):
    size = value.shape[-2] // parts
    return lax.dynamic_slice_in_dim(value, place * size, size, axis=value.ndim - 2)


class Chain:
    def start(self, send):
        self.arrived = flip(send, "tensor", 1)

    def cores(self, keep):
        self.value = summed(keep, self.arrived, 2)

    def scatter(self):
        parts = lax.axis_size("dp")
        both = self.value if isinstance(self.value, (list, tuple)) else [self.value]
        split = jnp.stack([value.reshape(parts, -1, D) for value in both], axis=1)
        total = lax.psum_scatter(split, "dp", scatter_dimension=0, tiled=False)
        self.value = total if len(both) == 2 else total[0]

    def send_y(self):
        self.kept, self.arrived = self.value[1], flip(self.value[0], "tensor", 2)

    def fold_rows(self):
        rows = self.kept.shape
        (total,) = summed(self.kept.reshape(-1, D), self.arrived.reshape(-1, D), 1)
        self.value = total.reshape(rows)

    def send_x(self, first, second):
        section = lax.axis_index("section")
        self.kept = jnp.where(section == 0, first.value, second.value)
        self.arrived = flip(jnp.where(section == 0, second.value, first.value), "section", 1)

    def fold(self):
        self.value = added(self.kept, self.arrived)

    def split(self):
        self.value = self.value.reshape(lax.axis_size("dp"), -1, D)

    def send_half(self, bit):
        mine = ((lax.axis_index("dp") & bit) != 0).astype(jnp.int32)
        blocks = self.value.reshape(-1, 2, *self.value.shape[1:])
        self.kept = lax.dynamic_index_in_dim(blocks, mine, 1, keepdims=False)
        self.arrived = flip(
            lax.dynamic_index_in_dim(blocks, 1 - mine, 1, keepdims=False), "dp", bit
        )

    def send_back(self, bit):
        self.arrived = flip(self.value, "dp", bit)

    def join(self, bit):
        upper = (lax.axis_index("dp") & bit) != 0
        value = jnp.where(
            upper,
            jnp.stack([self.arrived, self.value], axis=1),
            jnp.stack([self.value, self.arrived], axis=1),
        )
        self.value = value.reshape(-1, *value.shape[2:])


def tied(chains, *others):
    values = tie((tuple(chain.value for chain in chains), others))
    for chain, value in zip(chains, values[0]):
        chain.value = value
    return values[1]


def body(ends_in, ln_gain, ln_shift, w_qkv, b_qv, w_out, b_out, w_fc1, b_fc1, w_fc2, b_fc2):
    section = lax.axis_index("section")
    shard = lax.axis_index("tensor")
    zhalf = lax.axis_index("dp") % 2
    clips = ends_in.shape[1] // FRAMES
    info = jnp.stack(
        [shard, shard ^ 1, shard ^ 2, shard ^ 3, zhalf] + [jnp.int32(k) for k in BACK_ORDER]
    ).astype(jnp.int32)

    owned = [
        jnp.concatenate([w_qkv[0].transpose(1, 2, 0).reshape(QKV, D), w_out[0]], axis=0),
        w_fc1[0],
        w_fc2[0],
    ]
    nears = [rows_of(own, zhalf, 2) for own in owned]
    fars = [rows_of(own, 1 - zhalf, 2) for own in owned]
    beyond_a = flip(nears[0], "section", 1)

    small = jnp.concatenate(
        [ln_gain[0], ln_shift[0], b_qv[0], b_out, b_fc2, b_fc1.reshape(SHARDS, FEATS)], axis=0
    )
    ends = ends_in[0].T.reshape(FEATS, clips, FRAMES).transpose(1, 0, 2)
    ends = with_rows(ends, jnp.broadcast_to(small, (clips,) + small.shape))
    beyond_a, near_one, own_two, ends = tie((beyond_a, nears[1], owned[2], ends))
    ends = lax.all_to_all(ends, ("section", "tensor"), split_axis=0, concat_axis=0, tiled=True)
    small = ends[:, FEATS : FEATS + 12, :FEATS].astype(F32)
    cols = jnp.swapaxes(small[:, :8], 1, 2).reshape(2, SHARDS, FEATS, 8)
    b1s = small[:, 8:].reshape(2, SHARDS, 1, FF_SHARD)
    ends = ends[:, :FEATS].reshape(2, D, FRAMES)

    def layers(own, other):
        return jnp.where(section == 0, own, other), jnp.where(section == 0, other, own)

    def over_y(block):
        return flip(block, "tensor", 2)

    def chunk_of(own, there):
        return tuple(
            part for pair in (own, there) for parts in (pair, [flip(x, "tensor", 1) for x in pair])
            for part in parts
        )

    n_dp = lax.axis_size("dp")
    beyond_one = flip(near_one, "section", 1)
    beyond_two = flip(own_two, "section", 1)
    near_a = layers(nears[0], beyond_a)
    far_a = layers(fars[0], flip(beyond_a, "dp", 1))
    there_a = over_y(near_a[0])
    there_a, beyond_one = tie((there_a, beyond_one))
    away_a = flip(there_a, "dp", 1)
    near_one = layers(nears[1], beyond_one)
    beyond_far_one = flip(beyond_one, "dp", 1)
    there_one = over_y(near_one[0])

    def attend(layer, stream, chunk):
        return attention_forward(info, stream, cols[layer], chunk)

    def feed(layer, h, chunk_one, chunk_two):
        return mlp_forward(info, h, cols[layer], b1s[layer], chunk_one, chunk_two)

    there_one, beyond_two = tie((there_one, beyond_two))
    away_one = flip(there_one, "dp", 1)
    near_two = layers(nears[2], rows_of(beyond_two, zhalf, 2))
    far_two = layers(fars[2], rows_of(beyond_two, 1 - zhalf, 2))
    there_two = over_y(near_two[0])
    chunks = [[chunk_of((near_a[0], far_a[0]), (there_a, away_a))], []]
    stream = ends[0]
    a1, p, soft, o, h = attend(0, stream, chunks[0][0])
    h, away_one, there_two, beyond_far_one, late_a, late_far_a, late_one, late_two = tie(
        (h, away_one, there_two, beyond_far_one, near_a[1], far_a[1], near_one[1], (near_two[1], far_two[1]))
    )
    far_one = layers(fars[1], beyond_far_one)
    chunks[0].append(chunk_of((near_one[0], far_one[0]), (there_one, away_one)))
    chunks[0].append(chunk_of((near_two[0], far_two[0]), (there_two, flip(there_two, "dp", 1))))
    there_a, there_one = over_y(late_a), over_y(late_one)
    there_two, away_two = over_y(late_two[0]), over_y(late_two[1])
    away_a = flip(there_a, "dp", 1)
    a2, u, slope, y = feed(0, h, *chunks[0][1:])
    stored = [(stream, a1, p, soft, o, h, a2, u, slope)]
    stream, there_a, away_a, there_one, late_a, late_far_a = tie(
        (y, there_a, away_a, there_one, late_a, late_far_a)
    )
    chunks[1].append(chunk_of((late_a, late_far_a), (there_a, away_a)))
    away_one = flip(there_one, "dp", 1)
    a1, p, soft, o, h = attend(1, stream, chunks[1][0])
    h, late = tie(
        (
            h,
            (late_one, far_one[1], there_one, away_one, *late_two, there_two, away_two),
        )
    )
    chunks[1].append(chunk_of(late[0:2], late[2:4]))
    chunks[1].append(chunk_of(late[4:6], late[6:8]))
    a2, u, slope, y = feed(1, h, *chunks[1][1:])
    stored.append((stream, a1, p, soft, o, h, a2, u, slope))
    stream = y

    upstream = ends[1]
    bits = [1 << k for k in range(n_dp.bit_length() - 1)]
    chains = [[Chain() for _ in range(3)] for _ in range(2)]
    smalls = [None, None]
    ends_of = [None, None]
    late_a, late_one, late_two = chains[1]
    last_a, last_one, last_two = chains[0]
    for layer in (1, 0):
        chunk_a, chunk_one, chunk_two = chunks[layer]
        x, a1, p, soft, o, h, a2, u, slope = stored[layer]
        chain_a, chain_one, chain_two = chains[layer]
        after, send_one, send_two, db1_sent = mlp_backward(
            info, upstream, h, a2, cols[layer], u, slope, None, chunk_one, chunk_two
        )
        chain_two.start(send_two)
        chain_one.start(send_one)
        gh, dcol_two, keep_one, keep_two, db1_kept = mlp_backward(
            info, upstream, h, a2, cols[layer], u, slope, after, chunk_one, chunk_two
        )
        chain_two.cores(keep_two)
        chain_one.cores(keep_one)
        if layer == 0:
            late_a.fold_rows()
            (gh,) = tied((late_a, last_two, last_one, late_one), gh)
            late_a.split()
            late_a.send_half(bits[0])
            last_two.send_y()
            late_one.send_y()
            last_one.send_y()
        else:
            (gh,) = tied((late_two, late_one), gh)
            late_one.scatter()
            late_two.send_y()
        after, send_a, dbqv_sent = attention_backward(
            info, gh, x, a1, cols[layer], p, soft, o, None, chunk_a
        )
        chain_a.start(send_a)
        upstream, dcol_one, keep_a, dbqv_kept = attention_backward(
            info, gh, x, a1, cols[layer], p, soft, o, after, chunk_a
        )
        chain_a.cores(keep_a)
        if layer == 1:
            late_two.fold_rows()
            (upstream,) = tied((late_two, late_a), upstream)
            late_two.scatter()
            late_a.send_y()
        else:
            last_two.fold_rows()
            late_a.fold()
            late_one.fold()
            (upstream,) = tied((last_two, last_a, late_two, late_a, late_one), upstream)
            for bit in bits[1:]:
                late_a.send_half(bit)
                if bit != bits[-1]:
                    late_a.fold()
            last_two.scatter()
            last_a.send_y()
        ends_of[layer] = (db1_kept, db1_sent, (dbqv_kept, dbqv_sent, dcol_one, dcol_two))

    pair_two, pair_one, pair_a = Chain(), Chain(), Chain()

    def start_far(pair):
        pair.value = pair.value[None]
        pair.send_back(bits[-1])

    def finish_far(pair):
        pair.join(bits[-1])
        for bit in bits[-2:0:-1]:
            pair.send_back(bit)
            pair.join(bit)

    last_one.fold_rows()
    late_a.fold()
    late_a.value = late_a.value[0]
    tied((last_one, late_a))
    last_one.scatter()
    tied((last_two, late_two))
    pair_two.send_x(last_two, late_two)

    pair_two.fold()
    upstream, ends_of = tied((pair_two,), upstream, ends_of)
    for layer in range(2):
        db1_kept, db1_sent, dcols = ends_of[layer]
        smalls[layer] = jnp.concatenate(
            [
                jnp.swapaxes(sum(dcols), 1, 2),
                (db1_kept + db1_sent).reshape(SHARDS, SHARDS, FEATS),
            ],
            axis=1,
        )
    result = jnp.stack([upstream.astype(BF16), stream.astype(BF16)])
    result = with_rows(
        result.reshape(2 * SHARDS, FEATS, FRAMES), jnp.stack(smalls).reshape(-1, 12, FEATS)
    )
    result = lax.all_to_all(result, ("section", "tensor"), split_axis=0, concat_axis=0, tiled=True)

    last_a.fold_rows()
    tied((last_a, pair_two))
    last_a.split()
    last_a.send_half(bits[0])
    start_far(pair_two)

    last_a.fold()
    (pair_two.arrived,) = tied((last_a,), pair_two.arrived)
    for bit in bits[1:]:
        last_a.send_half(bit)
        if bit != bits[-1]:
            last_a.fold()

    finish_far(pair_two)
    (result,) = tied((pair_two, last_one), result)
    pair_one.send_x(last_one, late_one)
    pair_two.send_back(bits[0])
    small_sum = result[:, FEATS : FEATS + 12, :FEATS].astype(F32).sum(axis=0)

    last_a.fold()
    last_a.value = last_a.value[0]
    pair_one.fold()
    result, small_sum = tied((last_a, pair_one), result, small_sum)
    pair_a.send_x(last_a, late_a)
    start_far(pair_one)
    small_parts = [flip(small_sum, "dp", k) for k in range(1, n_dp)] if n_dp <= 4 else None

    pair_a.fold()
    pair_two.join(bits[0])
    (result,) = tied((pair_a, pair_two), result)
    start_far(pair_a)

    finish_far(pair_one)
    (result,) = tied((pair_one,), result)
    pair_one.send_back(bits[0])
    result = result[:, :FEATS].transpose(1, 0, 2).reshape(FEATS, clips * FRAMES).T.astype(F32)

    finish_far(pair_a)
    tied((pair_a,))
    pair_a.send_back(bits[0])
    pair_one.join(bits[0])
    if small_parts is None:
        small_sum = lax.psum(small_sum, "dp")
    else:
        small_parts, pair_one.value = tie((small_parts, pair_one.value))
        small_sum = sum(small_parts, small_sum)
    pair_a.join(bits[0])
    for pair in (pair_two, pair_one, pair_a):
        pair.value = pair.value.reshape(D, D)

    grad_a, grad_one, grad_two = [pair.value.astype(F32) for pair in (pair_a, pair_one, pair_two)]
    return (
        result[None],
        small_sum[None, 0:2],
        small_sum[None, 2:4],
        grad_a[:QKV].reshape(3, FEATS, D).transpose(2, 0, 1)[None],
        small_sum[None, 4:6],
        grad_a[QKV:][None],
        small_sum[6:7],
        grad_one[None],
        small_sum[8:12].reshape(1, FF_SHARD),
        grad_two[None],
        small_sum[7:8],
    )


def solution(mesh):
    placed = (
        P("section", "dp", "tensor"),
        P("section", None, "tensor"),
        P("section", None, "tensor"),
        P("section", None, None, "tensor"),
        P("section", None, "tensor"),
        P("section", "tensor", None),
        P("section", "tensor"),
        P("section", None, "tensor"),
        P("section", "tensor"),
        P("section", "tensor", None),
        P("section", "tensor"),
    )
    return jax.shard_map(
        body, mesh=mesh, in_specs=placed, out_specs=placed, check_vma=False
    )
```
